32 devices in a mesh: wide: 8 (over z, x), blk: 4 (over y, core).
Axes of the slice: x: 2, y: 2, z: 4, core: 2. Of those that a mesh axis runs over, the one named last changes fastest.
Arguments:
- inputs: bfloat16 [16, 512, 768], P('wide', 'blk'), may hold values from -6 to 6
- ln1_gain: float32 [768], replicated, may hold values from 0.5 to 1.5
- ln1_shift: float32 [768], replicated, may hold values from -3 to 3
- w_qkv: bfloat16 [768, 2304], replicated, may hold values from -0.21875 to 0.21875
- q_bias: float32 [768], replicated, may hold values from -3 to 3
- v_bias: float32 [768], replicated, may hold values from -3 to 3
- w_out: bfloat16 [768, 768], replicated, may hold values from -1.25 to 1.25
- out_bias: float32 [768], replicated, may hold values from -3 to 3
- table_x: float32 [64, 12], replicated, may hold values from -3 to 3
- table_y: float32 [64, 12], replicated, may hold values from -3 to 3
- ln2_gain: float32 [768], replicated, may hold values from 0.5 to 1.5
- ln2_shift: float32 [768], replicated, may hold values from -3 to 3
- w_up: bfloat16 [768, 3072], replicated, may hold values from -0.21875 to 0.21875
- up_bias: float32 [3072], replicated, may hold values from -3 to 3
- w_down: bfloat16 [3072, 768], replicated, may hold values from -0.109375 to 0.109375
- down_bias: float32 [768], replicated, may hold values from -3 to 3
- cotangent: bfloat16 [16, 512, 768], P('wide', 'blk'), may hold values from -6 to 6
- page_ids: int32 [16, 512], P('wide'), may hold values from 0 to 4, as said below
- corners: int32 [2, 16, 512], P(None, 'wide'), may hold values from 0 to 768
Outputs:
- output: float32 [16, 512, 768], P('wide', 'blk')
- grad_inputs: float32 [16, 512, 768], P('wide', 'blk')
- grad_ln1_gain: float32 [768], replicated
- grad_ln1_shift: float32 [768], replicated
- grad_w_qkv: float32 [768, 2304], replicated
- grad_q_bias: float32 [768], replicated
- grad_v_bias: float32 [768], replicated
- grad_w_out: float32 [768, 768], replicated
- grad_out_bias: float32 [768], replicated
- grad_table_x: float32 [64, 12], replicated
- grad_table_y: float32 [64, 12], replicated
- grad_ln2_gain: float32 [768], replicated
- grad_ln2_shift: float32 [768], replicated
- grad_w_up: float32 [768, 3072], replicated
- grad_up_bias: float32 [3072], replicated
- grad_w_down: float32 [3072, 768], replicated
- grad_down_bias: float32 [768], replicated
The draws below stay inside these ranges and needn't reach their ends.
Inputs may be any that keep to these rules, and one draw needn't show every extreme that they name: `page_ids`: along each row page ids start at 0 and never fall, and the row's last position carries page 4; in each row one page covers every position from below 64 to at least 448.
All inputs are finite; a program needn't handle non-finite values.
Results may differ from the reference program's by a relative error of at most 0.012.
Values may be sent and summed in bfloat16 or wider, within the bound.
A program may use at most 192 MiB of HBM per device.

```python
from functools import partial
import jax
import jax.numpy as jnp
from jax import lax

D = 768
HEADS = 12
HEAD_DIM = 64
FF = 3072
SEQ = 512
BUCKETS = 64
BIN_PX = 16
ROWS = 16


def draw_page_ids(key, part):
    key = jax.random.fold_in(key, 11)
    first_key, second_key, third_key = jax.random.split(key, 3)
    span_len = SEQ // 8
    opening = jax.random.randint(first_key, (ROWS, 1), 2, span_len)
    closing = SEQ - 2 - jax.random.randint(second_key, (ROWS, 1), 0, span_len - 2)
    breaks = jax.random.randint(third_key, (ROWS, SEQ), 0, 24) == 0
    places = jnp.arange(SEQ, dtype=jnp.int32)[None, :]
    inside = (places > opening) & (places < closing)
    forced = (places == 1) | (places == opening) | (places == closing) | (places == SEQ - 1)
    breaks = breaks & jnp.logical_not(inside) | forced
    breaks = breaks & (places > 0)
    counted = jnp.cumsum(breaks.astype(jnp.int32), axis=1).astype(jnp.int32)
    return jnp.minimum(counted, 4).astype(jnp.int32)


def place_ends(values, rng, least, largest):
    shape = values.shape
    spot = [jax.random.randint(jax.random.fold_in(rng, axis), (), 0, shape[axis]) for axis in range(len(shape))]
    values = values.at[tuple(spot)].set(least)
    longest = shape.index(max(shape))
    spot[longest] = (spot[longest] + 1) % shape[longest]
    return values.at[tuple(spot)].set(largest)


def level_of(rng, shape, shards, smallest, largest):
    def one(position, blocks):
        draws = jax.random.uniform(jax.random.fold_in(jax.random.fold_in(rng, 6), position), (blocks,), jnp.float32, smallest / len(shards), largest / len(shards))
        return jnp.repeat(jnp.exp(draws), shape[position] // blocks).reshape((-1,) + (1,) * (len(shape) - position - 1))

    level = one(*shards[0])
    for cut in shards[1:]:
        level = level * one(*cut)
    return level


def scatter_about(stream_key, extent, scale, bound, shards=(), held_as=jnp.bfloat16):
    level = level_of(stream_key, extent, shards, -0.22, 0.18) if shards else 1.0
    entries = jax.random.normal(stream_key, extent, jnp.float32) * scale * level
    return jnp.minimum(jnp.maximum(entries, -bound), bound).astype(held_as)


def setup_inputs(seed: int = 0) -> dict:
    key_of = jax.random.split(jax.random.key(seed), 20)
    return {
        "inputs": scatter_about(key_of[0], (ROWS, SEQ, D), 1.0, 6.0, ((0, 8), (1, 4))),
        "ln1_gain": jnp.clip(1.0 + 0.1 * jax.random.normal(key_of[1], (D,), jnp.float32), 0.5, 1.5),
        "ln1_shift": scatter_about(key_of[2], (D,), 0.3, 3.0, (), jnp.float32),
        "w_qkv": scatter_about(key_of[3], (D, 3 * D), D ** -0.5, 0.21875),
        "q_bias": scatter_about(key_of[4], (D,), 0.5, 3.0, (), jnp.float32),
        "v_bias": scatter_about(key_of[5], (D,), 0.5, 3.0, (), jnp.float32),
        "w_out": scatter_about(key_of[6], (D, D), (D // 32) ** -0.5, 1.25),
        "out_bias": scatter_about(key_of[7], (D,), 0.3, 3.0, (), jnp.float32),
        "table_x": scatter_about(key_of[8], (BUCKETS, HEADS), 0.5, 3.0, (), jnp.float32),
        "table_y": scatter_about(key_of[9], (BUCKETS, HEADS), 0.5, 3.0, (), jnp.float32),
        "ln2_gain": jnp.clip(1.0 + 0.1 * jax.random.normal(key_of[10], (D,), jnp.float32), 0.5, 1.5),
        "ln2_shift": scatter_about(key_of[11], (D,), 0.3, 3.0, (), jnp.float32),
        "w_up": scatter_about(key_of[12], (D, FF), D ** -0.5, 0.21875),
        "up_bias": scatter_about(key_of[13], (FF,), 0.5, 3.0, (), jnp.float32),
        "w_down": scatter_about(key_of[14], (FF, D), FF ** -0.5, 0.109375),
        "down_bias": scatter_about(key_of[15], (D,), 0.3, 3.0, (), jnp.float32),
        "cotangent": scatter_about(key_of[16], (ROWS, SEQ, D), 1.0, 6.0, ((0, 8), (1, 4))),
        "page_ids": draw_page_ids(jax.random.fold_in(key_of[19], 71), 0),
        "corners": place_ends(jax.random.randint(key_of[18], (2, ROWS, SEQ), 0, 769), jax.random.fold_in(key_of[18], 1), 0, 768).astype(jnp.int32),
    }


@jax.custom_vjp
def low(v):
    return lax.optimization_barrier(v.astype(jnp.bfloat16)).astype(jnp.float32)

@jax.custom_vjp
def low_back(v):
    return v

def low_keep(v):
    return (low(v), None)

def low_pass(kept, grad):
    return (grad,)

def back_keep(v):
    return (v, None)

def back_low(kept, grad):
    return (low(grad),)
low.defvjp(low_keep, low_pass)
low_back.defvjp(back_keep, back_low)

def layer_norm(values, gain, shift):
    mean_val = lax.optimization_barrier(jnp.mean(values, axis=-1, keepdims=True))
    centered = values - mean_val
    spread_sq = lax.optimization_barrier(jnp.mean(centered * centered, axis=-1, keepdims=True))
    return centered * lax.rsqrt(spread_sq + 1e-05) * gain + shift

def bin_index(query_pos, key_pos):
    offset = jnp.floor_divide(key_pos[None, :] - query_pos[:, None], BIN_PX)
    return jnp.clip(offset, -(BUCKETS // 2), BUCKETS // 2 - 1) + BUCKETS // 2

def attend_row(pieces, table_x, table_y):
    query, key, value, coord_x, coord_y, pages = pieces
    query = query.reshape(SEQ, HEADS, HEAD_DIM)
    key = key.reshape(SEQ, HEADS, HEAD_DIM)
    value = value.reshape(SEQ, HEADS, HEAD_DIM)
    raw = jnp.einsum('qhd,khd->hqk', query, key, precision=lax.Precision.HIGHEST) * HEAD_DIM ** (-0.5)
    bias_x = jnp.transpose(table_x[bin_index(coord_x, coord_x)], (2, 0, 1))
    bias_y = jnp.transpose(table_y[bin_index(coord_y, coord_y)], (2, 0, 1))
    scores = low_back(raw + bias_x + bias_y)
    same = (pages[:, None] == pages[None, :])[None]
    masked = jnp.where(same, scores, -1e+30)
    row_max = lax.optimization_barrier(jnp.max(masked, axis=-1, keepdims=True))
    exp_terms = jnp.exp(masked - row_max)
    weights = exp_terms / lax.optimization_barrier(jnp.sum(exp_terms, axis=-1, keepdims=True))
    mixed = jnp.einsum('hqk,khd->qhd', low(weights), value, precision=lax.Precision.HIGHEST)
    return mixed.reshape(SEQ, D)

def forward(inputs, ln1_gain, ln1_shift, w_qkv, q_bias, v_bias, w_out, out_bias, table_x, table_y, ln2_gain, ln2_shift, w_up, up_bias, w_down, down_bias, page_ids, corners):
    tokens = inputs.reshape(ROWS * SEQ, D)
    normed = low(layer_norm(tokens, ln1_gain, ln1_shift))
    joined = jnp.dot(normed, w_qkv, precision=lax.Precision.HIGHEST)
    query = low(low_back(joined[:, :D] + q_bias))
    key = low(low_back(joined[:, D:2 * D]))
    value = low(low_back(joined[:, 2 * D:] + v_bias))
    row_fn = jax.checkpoint(partial(attend_row, table_x=table_x, table_y=table_y))
    attended = lax.map(row_fn, (query.reshape(ROWS, SEQ, D), key.reshape(ROWS, SEQ, D), value.reshape(ROWS, SEQ, D), corners[0], corners[1], page_ids))
    attended = low(low_back(attended.reshape(ROWS * SEQ, D)))
    branch = low_back(jnp.dot(attended, w_out, precision=lax.Precision.HIGHEST) + out_bias)
    middle = tokens + branch
    normed_two = low(layer_norm(middle, ln2_gain, ln2_shift))
    hidden = jnp.dot(normed_two, w_up, precision=lax.Precision.HIGHEST) + up_bias
    active = low(jax.nn.gelu(low_back(hidden), approximate=False))
    result = middle + (jnp.dot(active, w_down, precision=lax.Precision.HIGHEST) + down_bias)
    return result.reshape(ROWS, SEQ, D)

def reference(inputs, ln1_gain, ln1_shift, w_qkv, q_bias, v_bias, w_out, out_bias, table_x, table_y, ln2_gain, ln2_shift, w_up, up_bias, w_down, down_bias, cotangent, page_ids, corners):
    floats = tuple((argument.astype(jnp.float32) for argument in (inputs, ln1_gain, ln1_shift, w_qkv, q_bias, v_bias, w_out, out_bias, table_x, table_y, ln2_gain, ln2_shift, w_up, up_bias, w_down, down_bias)))

    def wrapped(*params):
        return forward(*params, page_ids, corners)
    output, pullback = jax.vjp(wrapped, *floats)
    gradients = pullback(cotangent.astype(jnp.float32))
    return (output, gradients[0], gradients[1], gradients[2], gradients[3], gradients[4], gradients[5], gradients[6], gradients[7], gradients[8], gradients[9], gradients[10], gradients[11], gradients[12], gradients[13], gradients[14], gradients[15])
```

```python
import functools
import math

import jax
import jax.numpy as jnp
from jax import lax
from jax.experimental import pallas as pl
from jax.experimental.pallas import tpu as pltpu
from jax.sharding import PartitionSpec as P

HEADS = 12
HEAD_DIM = 64
BUCKETS = 64
BIN_PX = 16
MESH = pl.DeviceIdType.MESH
MIB = 1024 * 1024

CHUNKS = 6
SIDE = 768
PIECE = SIDE // 16
SIBLING = ("blk", 1)
ALONG_Y, ALONG_X, NEAR_Z, FAR_Z = ("blk", 2), ("wide", 1), ("wide", 2), ("wide", 4)
ROUTES = ((ALONG_Y, ALONG_X, NEAR_Z, FAR_Z), (ALONG_X, ALONG_Y, NEAR_Z, FAR_Z)) * 3
ORDER = (
    0, 1, 2, 3, 0, 1, 2, 3, 0, 1, 4, 5, 0, 2, 3, 1, 0, 2, 1, 3, 0, 4, 5, 2, 0, 1, 3, 4, 5, 1, 2, 4, 3, 0, 5, 1, 4, 2,
    5, 3, 4, 5, 0, 4, 1, 5, 0, 3, 1, 2, 5, 4, 2, 3, 2, 3, 4, 5, 4, 5,
)


def outer_steps(wide):
    return tuple(("wide", 1 << level) for level in range(3, wide.bit_length() - 1))


def step_bit(step):
    axis, mask = step
    return lax.rem(lax.div(lax.axis_index(axis), mask), 2)


def step_target(step):
    axis, mask = step
    place = lax.axis_index(axis)
    return {axis: place + mask * (1 - 2 * step_bit(step))}


def remote(source, target, sems, step):
    return pltpu.make_async_remote_copy(
        source, target, sems.at[0], sems.at[1], device_id=step_target(step), device_id_type=MESH
    )


def greet(steps):
    barrier = pltpu.get_barrier_semaphore()
    for step in steps:
        pl.semaphore_signal(barrier, inc=1, device_id=step_target(step), device_id_type=MESH)
    pl.semaphore_wait(barrier, len(steps))


def add_rows(target, target_row, left, left_row, right, right_row, count):
    def body(i, carry):
        def rows(first):
            return pl.ds(pl.multiple_of(first + i * PIECE, 16), PIECE)

        total = left[rows(left_row), :].astype(jnp.float32) + right[rows(right_row), :].astype(jnp.float32)
        target[rows(target_row), :] = total.astype(target.dtype)
        return carry

    lax.fori_loop(0, count // PIECE, body, 0)


def chunk_task(route, outer, mine, inbox, whole, sems, land):
    first, size, box, slot = 0, SIDE, 0, 0
    firsts = []
    for step in route:
        half = size // 2
        bit = step_bit(step)
        keep, give = first + bit * half, first + (1 - bit) * half
        copy = remote(
            mine.at[pl.ds(pl.multiple_of(give, 16), half), :], inbox.at[pl.ds(box, half), :], sems.at[slot], step
        )
        copy.start()
        yield
        copy.wait()
        add_rows(whole if half == PIECE else mine, keep, mine, keep, inbox, box, half)
        firsts.append(first)
        first, size, box, slot = keep, half, box + half, slot + 1
    for step in outer:
        piece = whole.at[pl.ds(pl.multiple_of(first, 16), size), :]
        copy = remote(piece, inbox.at[pl.ds(box, size), :], sems.at[slot], step)
        copy.start()
        copy.wait()
        add_rows(whole, first, whole, first, inbox, box, size)
        box, slot = box + size, slot + 1
    for step, before in zip(reversed(route), reversed(firsts)):
        piece = whole.at[pl.ds(pl.multiple_of(first, 16), size), :]
        copy = remote(piece, piece, sems.at[slot], step)
        copy.start()
        yield
        copy.wait()
        first, size, slot = before, size * 2, slot + 1
    copies = []
    for view, place in land:
        copies.append(remote(view, place, sems.at[slot], SIBLING))
        copies.append(pltpu.make_async_copy(view, place, sems.at[slot + 1, 0]))
        slot += 2
    for copy in copies:
        copy.start()
    yield
    for copy in copies:
        copy.wait()


def small_task(steps, total, inbox, sems):
    for slot, step in enumerate(steps):
        copy = remote(total, inbox.at[slot], sems.at[slot], step)
        copy.start()
        yield
        copy.wait()
        total[...] += inbox[slot]


def landing(index, whole, side, o_up, o_down, o_qkv, o_out):
    def at(array, first, width):
        return array.at[:, pl.ds(pl.multiple_of(first, 128), width)]

    if index < 2:
        return ((whole, at(o_up, side * 1536 + index * SIDE, SIDE)),)
    if index < 4:
        first = pl.multiple_of(side * 1536 + (index - 2) * SIDE, 16)
        return ((whole, o_down.at[pl.ds(first, SIDE), :]),)
    if index == 4:
        return ((whole, at(o_qkv, side * 1152, SIDE)),)
    return (
        (at(whole, 0, 384), at(o_qkv, side * 1152 + SIDE, 384)),
        (at(whole, 384, 384), at(o_out, side * 384, 384)),
    )


def reduce_kernel(outer, up, down, qkv, out, small, o_up, o_down, o_qkv, o_out, o_small, mine, inbox, whole,
                  small_in, load_sem, sems, small_sems):
    inner = (SIBLING, ALONG_Y, ALONG_X, NEAR_Z, FAR_Z)
    greet(inner + outer)
    side = step_bit(SIBLING)
    loads = []

    def load(view, place):
        copy = pltpu.make_async_copy(view, place, load_sem.at[len(loads)])
        copy.start()
        loads.append(copy)

    for k in range(2):
        load(up.at[:, pl.ds(k * SIDE, SIDE)], mine.at[k])
        load(down.at[pl.ds(k * SIDE, SIDE), :], mine.at[2 + k])
    load(qkv.at[:, pl.ds(0, SIDE)], mine.at[4])
    load(qkv.at[:, pl.ds(SIDE, 384)], mine.at[5, :, pl.ds(0, 384)])
    load(out, mine.at[5, :, pl.ds(384, 384)])
    o_small[...] = small[...]
    for copy in loads:
        copy.wait()
    tasks = [
        chunk_task(
            ROUTES[k],
            outer,
            mine.at[k],
            inbox.at[k],
            whole.at[k],
            sems.at[k],
            landing(k, whole.at[k], side, o_up, o_down, o_qkv, o_out),
        )
        for k in range(CHUNKS)
    ]
    small_steps = small_task(inner + outer, o_small, small_in, small_sems)
    for count, index in enumerate(ORDER):
        next(tasks[index], None)
        if count % 4 == 3:
            next(small_steps, None)


def reduce_gradients(up, down, qkv, out, small):
    outer = outer_steps(lax.axis_size("wide"))
    slots = 12 + len(outer)
    hbm = pl.BlockSpec(memory_space=pl.ANY)
    vmem = pl.BlockSpec(memory_space=pltpu.VMEM)
    bf16 = jnp.bfloat16
    return pl.pallas_call(
        functools.partial(reduce_kernel, outer),
        out_shape=(
            jax.ShapeDtypeStruct((SIDE, 3072), bf16),
            jax.ShapeDtypeStruct((3072, SIDE), bf16),
            jax.ShapeDtypeStruct((SIDE, 2304), bf16),
            jax.ShapeDtypeStruct((SIDE, SIDE), bf16),
            jax.ShapeDtypeStruct(small.shape, jnp.float32),
        ),
        in_specs=[hbm, hbm, hbm, hbm, vmem],
        out_specs=(hbm, hbm, hbm, hbm, vmem),
        scratch_shapes=[
            pltpu.VMEM((CHUNKS, SIDE, SIDE), bf16),
            pltpu.VMEM((CHUNKS, SIDE - PIECE + PIECE * len(outer), SIDE), bf16),
            pltpu.VMEM((CHUNKS, SIDE, SIDE), bf16),
            pltpu.VMEM((5 + len(outer),) + small.shape, jnp.float32),
            pltpu.SemaphoreType.DMA((7,)),
            pltpu.SemaphoreType.DMA((CHUNKS, slots, 2)),
            pltpu.SemaphoreType.DMA((5 + len(outer), 2)),
        ],
        compiler_params=pltpu.CompilerParams(
            collective_id=0, has_side_effects=True, vmem_limit_bytes=56 * MIB
        ),
        cost_estimate=pl.CostEstimate(flops=10**7, bytes_accessed=3 * 10**7, transcendentals=0),
    )(up, down, qkv, out, small)


def with_sibling(array):
    pairs = [(place, place ^ 1) for place in range(lax.axis_size("blk"))]
    return jnp.concatenate((array, lax.ppermute(array, "blk", pairs)), axis=0)


def half_with_sibling(array, width, axis_index):
    pairs = [(place, place ^ 1) for place in range(lax.axis_size("blk"))]
    side = lax.rem(axis_index, 2)
    kept = lax.dynamic_slice_in_dim(array, side * width, width, 1)
    given = lax.dynamic_slice_in_dim(array, (1 - side) * width, width, 1)
    return jnp.concatenate((kept, lax.ppermute(given, "blk", pairs)), axis=0)


def layer_stats(values):
    mean_val = jnp.mean(values, axis=-1, keepdims=True)
    centered = values - mean_val
    inv_std = lax.rsqrt(jnp.mean(centered * centered, axis=-1, keepdims=True) + 1e-05)
    return (centered * inv_std, inv_std)


def norm_back(grad_norm, normalized, inv_std, gain):
    scaled = grad_norm * gain
    first_mean = jnp.mean(scaled, axis=-1, keepdims=True)
    second_mean = jnp.mean(scaled * normalized, axis=-1, keepdims=True)
    return inv_std * (scaled - first_mean - normalized * second_mean)


def bin_hot(query_pos, key_pos):
    offset = jnp.floor_divide(key_pos[:, None, :] - query_pos[:, :, None], BIN_PX)
    bins = jnp.clip(offset, -(BUCKETS // 2), BUCKETS // 2 - 1) + BUCKETS // 2
    levels = jnp.arange(BUCKETS, dtype=jnp.int32)[:, None, None, None]
    return (levels == bins[None]).astype(jnp.bfloat16)


def group_scores(heads_q, heads_k, q_x, q_y, q_page, k_x, k_y, k_page, table_x, table_y):
    hot_x = bin_hot(q_x, k_x)
    hot_y = bin_hot(q_y, k_y)
    raw = jnp.einsum(
        "gqhd,gkhd->ghqk", heads_q, heads_k, preferred_element_type=jnp.float32
    ) * HEAD_DIM ** (-0.5)
    bias_x = jnp.einsum(
        "bgqk,bh->ghqk",
        hot_x,
        table_x,
        precision=lax.Precision.HIGHEST,
        preferred_element_type=jnp.float32,
    )
    bias_y = jnp.einsum(
        "bgqk,bh->ghqk",
        hot_y,
        table_y,
        precision=lax.Precision.HIGHEST,
        preferred_element_type=jnp.float32,
    )
    scores = raw + bias_x + bias_y
    same = (q_page[:, :, None] == k_page[:, None, :])[:, None]
    return (jnp.where(same, scores, -1e30), hot_x, hot_y)


def pack_flat(pieces):
    flat = jnp.concatenate([piece.reshape(-1) for piece in pieces])
    return jnp.pad(flat, (0, -flat.shape[0] % 1024))


def unpack_flat(flat, shapes):
    results = []
    offset = 0
    for shape in shapes:
        length = math.prod(shape)
        results.append(flat[offset : offset + length].reshape(shape))
        offset += length
    return results


def contract_rows(left, right):
    return lax.dot_general(
        left, right, (((0,), (0,)), ((), ())), preferred_element_type=jnp.float32
    )


def contract_cols(left, right):
    return lax.dot_general(
        left, right, (((1,), (1,)), ((), ())), preferred_element_type=jnp.float32
    )


def gelu_exact(values):
    return jax.nn.gelu(values, approximate=False)


def per_device(
    inputs,
    ln1_gain,
    ln1_shift,
    w_qkv,
    q_bias,
    v_bias,
    w_out,
    out_bias,
    table_x,
    table_y,
    ln2_gain,
    ln2_shift,
    w_up,
    up_bias,
    w_down,
    down_bias,
    cotangent,
    page_ids,
    corners,
):
    row_count, local_len, width_dim = inputs.shape
    full_len = page_ids.shape[1]
    token_count = row_count * local_len
    group_rows = min(4, row_count)
    group_count = row_count // group_rows
    scale = HEAD_DIM ** (-0.5)

    def grouped(array):
        return array.reshape((group_count, group_rows) + array.shape[1:])

    tokens = inputs.reshape(token_count, width_dim).astype(jnp.float32)
    normed_one, inv_one = layer_stats(tokens)
    xn_one = (normed_one * ln1_gain + ln1_shift).astype(jnp.bfloat16)
    joined = jnp.dot(xn_one, w_qkv, preferred_element_type=jnp.float32)
    query = (joined[:, :width_dim] + q_bias).astype(jnp.bfloat16)
    key = joined[:, width_dim : 2 * width_dim].astype(jnp.bfloat16)
    value = (joined[:, 2 * width_dim :] + v_bias).astype(jnp.bfloat16)
    query_rows = query.reshape(row_count, local_len, width_dim)
    key_rows = key.reshape(row_count, local_len, width_dim)
    value_rows = value.reshape(row_count, local_len, width_dim)
    start_pos = lax.axis_index("blk") * local_len
    q_corners = lax.dynamic_slice_in_dim(corners, start_pos, local_len, 2)
    q_pages = lax.dynamic_slice_in_dim(page_ids, start_pos, local_len, 1)
    position_pieces = (
        grouped(q_corners[0]),
        grouped(q_corners[1]),
        grouped(q_pages),
        grouped(corners[0]),
        grouped(corners[1]),
        grouped(page_ids),
    )
    gathered_k, gathered_v = (
        lax.all_gather(key_rows, "blk", axis=1, tiled=True),
        lax.all_gather(value_rows, "blk", axis=1, tiled=True),
    )

    def attend(pieces):
        part_q, part_k, part_v, q_x, q_y, q_page, k_x, k_y, k_page = pieces
        heads_q = part_q.reshape(group_rows, local_len, HEADS, HEAD_DIM)
        heads_k = part_k.reshape(group_rows, full_len, HEADS, HEAD_DIM)
        heads_v = part_v.reshape(group_rows, full_len, HEADS, HEAD_DIM)
        masked, hot_x, hot_y = group_scores(
            heads_q, heads_k, q_x, q_y, q_page, k_x, k_y, k_page, table_x, table_y
        )
        row_max = jnp.max(masked, axis=-1, keepdims=True)
        exp_terms = jnp.exp(masked - row_max)
        row_sum = jnp.sum(exp_terms, axis=-1, keepdims=True)
        weights = (exp_terms / row_sum).astype(jnp.bfloat16)
        mixed = jnp.einsum("ghqk,gkhd->gqhd", weights, heads_v, preferred_element_type=jnp.float32)
        log_sum = (row_max + jnp.log(row_sum))[..., 0]
        return (mixed.reshape(group_rows, local_len, width_dim).astype(jnp.bfloat16), log_sum)

    mixed_all, log_sums = lax.map(
        attend, (grouped(query_rows), grouped(gathered_k), grouped(gathered_v)) + position_pieces
    )
    attended = mixed_all.reshape(token_count, width_dim)
    middle = tokens + (jnp.dot(attended, w_out, preferred_element_type=jnp.float32) + out_bias)
    normed_two, inv_two = layer_stats(middle)
    xn_two = (normed_two * ln2_gain + ln2_shift).astype(jnp.bfloat16)
    hidden = jnp.dot(xn_two, w_up, preferred_element_type=jnp.float32) + up_bias
    active, gelu_pull = jax.vjp(gelu_exact, hidden)
    active_low = active.astype(jnp.bfloat16)
    output = middle + (jnp.dot(active_low, w_down, preferred_element_type=jnp.float32) + down_bias)
    grad_out = cotangent.reshape(token_count, width_dim)
    grad_down_bias = jnp.sum(grad_out, axis=0, dtype=jnp.float32)
    place = lax.axis_index("blk")
    part_down = contract_rows(half_with_sibling(active_low, 1536, place), with_sibling(grad_out)).astype(jnp.bfloat16)
    grad_active = contract_cols(grad_out, w_down)
    grad_hidden = gelu_pull(grad_active)[0].astype(jnp.bfloat16)
    grad_up_bias = jnp.sum(grad_hidden, axis=0, dtype=jnp.float32)
    part_up = contract_rows(with_sibling(xn_two), half_with_sibling(grad_hidden, 1536, place)).astype(jnp.bfloat16)
    grad_xn_two = contract_cols(grad_hidden, w_up)
    grad_ln2_gain = jnp.sum(grad_xn_two * normed_two, axis=0)
    grad_ln2_shift = jnp.sum(grad_xn_two, axis=0)
    grad_middle = grad_out.astype(jnp.float32) + norm_back(
        grad_xn_two, normed_two, inv_two, ln2_gain
    )
    grad_branch = grad_middle.astype(jnp.bfloat16)
    grad_out_bias = jnp.sum(grad_branch, axis=0, dtype=jnp.float32)
    part_out = contract_rows(with_sibling(attended), half_with_sibling(grad_branch, 384, place)).astype(jnp.bfloat16)
    grad_attended = contract_cols(grad_branch, w_out).astype(jnp.bfloat16)
    back_k, back_v = (gathered_k, gathered_v)

    def attend_back(carry, pieces):
        part_q, part_k, part_v, grad_mix, log_sum, q_x, q_y, q_page, k_x, k_y, k_page = pieces
        heads_q = part_q.reshape(group_rows, local_len, HEADS, HEAD_DIM)
        heads_k = part_k.reshape(group_rows, full_len, HEADS, HEAD_DIM)
        heads_v = part_v.reshape(group_rows, full_len, HEADS, HEAD_DIM)
        grad_heads = grad_mix.reshape(group_rows, local_len, HEADS, HEAD_DIM)
        masked, hot_x, hot_y = group_scores(
            heads_q, heads_k, q_x, q_y, q_page, k_x, k_y, k_page, table_x, table_y
        )
        probs = jnp.exp(masked - log_sum[..., None])
        grad_probs = jnp.einsum(
            "gqhd,gkhd->ghqk", grad_heads, heads_v, preferred_element_type=jnp.float32
        )
        inner = jnp.sum(probs * grad_probs, axis=-1, keepdims=True)
        grad_scores = (probs * (grad_probs - inner)).astype(jnp.bfloat16)
        grad_query = (
            jnp.einsum("ghqk,gkhd->gqhd", grad_scores, heads_k, preferred_element_type=jnp.float32)
            * scale
        ).astype(jnp.bfloat16)
        grad_key = (
            jnp.einsum("ghqk,gqhd->gkhd", grad_scores, heads_q, preferred_element_type=jnp.float32)
            * scale
        )
        grad_value = jnp.einsum(
            "ghqk,gqhd->gkhd",
            probs.astype(jnp.bfloat16),
            grad_heads,
            preferred_element_type=jnp.float32,
        )
        table_gx = carry[0] + jnp.einsum(
            "bgqk,ghqk->bh", hot_x, grad_scores, preferred_element_type=jnp.float32
        )
        table_gy = carry[1] + jnp.einsum(
            "bgqk,ghqk->bh", hot_y, grad_scores, preferred_element_type=jnp.float32
        )
        return (
            (table_gx, table_gy),
            (
                grad_query.reshape(group_rows, local_len, width_dim),
                grad_key.reshape(group_rows, full_len, width_dim),
                grad_value.reshape(group_rows, full_len, width_dim),
            ),
        )

    table_zero = jnp.zeros((BUCKETS, HEADS), jnp.float32)
    tables_grad, back_parts = lax.scan(
        attend_back,
        (table_zero, table_zero),
        (
            grouped(query_rows),
            grouped(back_k),
            grouped(back_v),
            grouped(grad_attended.reshape(row_count, local_len, width_dim)),
            log_sums,
        )
        + position_pieces,
    )
    grad_query_all, grad_key_all, grad_value_all = back_parts
    own_key, own_value = (
        lax.psum_scatter(
            grad_key_all.reshape(row_count, full_len, width_dim),
            "blk",
            scatter_dimension=1,
            tiled=True,
        ),
        lax.psum_scatter(
            grad_value_all.reshape(row_count, full_len, width_dim),
            "blk",
            scatter_dimension=1,
            tiled=True,
        ),
    )
    grad_q_low = grad_query_all.reshape(token_count, width_dim)
    grad_k_low = own_key.reshape(token_count, width_dim).astype(jnp.bfloat16)
    grad_v_low = own_value.reshape(token_count, width_dim).astype(jnp.bfloat16)
    grad_joined = jnp.concatenate((grad_q_low, grad_k_low, grad_v_low), axis=1)
    grad_q_bias = jnp.sum(grad_q_low, axis=0, dtype=jnp.float32)
    grad_v_bias = jnp.sum(grad_v_low, axis=0, dtype=jnp.float32)
    part_qkv = contract_rows(with_sibling(xn_one), half_with_sibling(grad_joined, 1152, place)).astype(jnp.bfloat16)
    grad_xn_one = contract_cols(grad_joined, w_qkv)
    grad_ln1_gain = jnp.sum(grad_xn_one * normed_one, axis=0)
    grad_ln1_shift = jnp.sum(grad_xn_one, axis=0)
    grad_inputs = grad_middle + norm_back(grad_xn_one, normed_one, inv_one, ln1_gain)
    small_list = [
        grad_ln1_gain,
        grad_ln1_shift,
        grad_q_bias,
        grad_v_bias,
        grad_out_bias,
        tables_grad[0],
        tables_grad[1],
        grad_ln2_gain,
        grad_ln2_shift,
        grad_up_bias,
        grad_down_bias,
    ]
    small_shapes = [piece.shape for piece in small_list]
    small_flat = pack_flat(small_list).reshape(-1, 128)
    full_up, full_down, full_qkv, full_out, full_small = reduce_gradients(
        part_up, part_down, part_qkv, part_out, small_flat
    )
    flat_small = full_small.reshape(-1)
    smalls = unpack_flat(flat_small, small_shapes)
    return (
        output.reshape(row_count, local_len, width_dim),
        grad_inputs.reshape(row_count, local_len, width_dim),
        smalls[0],
        smalls[1],
        full_qkv.astype(jnp.float32),
        smalls[2],
        smalls[3],
        full_out.astype(jnp.float32),
        smalls[4],
        smalls[5],
        smalls[6],
        smalls[7],
        smalls[8],
        full_up.astype(jnp.float32),
        smalls[9],
        full_down.astype(jnp.float32),
        smalls[10],
    )


def solution(mesh):
    placed = (
        P("wide", "blk", None),
        P(),
        P(),
        P(),
        P(),
        P(),
        P(),
        P(),
        P(),
        P(),
        P(),
        P(),
        P(),
        P(),
        P(),
        P(),
        P("wide", "blk", None),
        P("wide", None),
        P(None, "wide", None),
    )
    return jax.shard_map(
        per_device,
        mesh=mesh,
        in_specs=placed,
        out_specs=(
            P("wide", "blk", None),
            P("wide", "blk", None),
            P(),
            P(),
            P(),
            P(),
            P(),
            P(),
            P(),
            P(),
            P(),
            P(),
            P(),
            P(),
            P(),
            P(),
            P(),
        ),
        check_vma=False,
    )
```

```python
import functools
import math

import jax
import jax.numpy as jnp
from jax import lax
from jax.experimental import pallas as pl
from jax.experimental.pallas import tpu as pltpu
from jax.sharding import PartitionSpec as P

HEADS = 12
HEAD_DIM = 64
BUCKETS = 64
BIN_PX = 16
MASKED = -1e30
EPS = 1e-05
MESH = pl.DeviceIdType.MESH
MIB = 1024 * 1024
F32, BF16 = jnp.float32, jnp.bfloat16

BLOCK = 128
OWN = 2 * BLOCK
FULL = 2 * OWN
WIDTH = HEADS * HEAD_DIM
FF = 4 * WIDTH
PAIRS = HEADS // 2

SQUARES = 6
CHUNKS = 2 * SQUARES
SIDE = WIDTH
HALF = SIDE // 2
PIECE = SIDE // 16
SIBLING = ("blk", 1)
ALONG_Y, ALONG_X, NEAR_Z, FAR_Z = ("blk", 2), ("wide", 1), ("wide", 2), ("wide", 4)
STEPS = {"Y": ALONG_Y, "X": ALONG_X, "1": NEAR_Z, "2": FAR_Z}
NAMES = "abcdefghijkl"
ROUTES = ("YX21", "XY12", "YX12", "2YX1", "XY21", "1XY2", "X1Y2", "1YX2", "XY12", "YX12", "YX21", "XY12")
PLAN = (
    ("ab",), ("cd",), ("",), ("",), ("ef",), ("ghab",), ("",), ("",), ("cefdb",), ("",), ("lg",), ("hb",), ("ae",),
    ("gcdb",), ("jifha",), ("kg",),
    ("cesablgdescjafbsdgeichskajdsfckeslhjafdbglkchijg", "ekblihbkjalfiagjdkgliecefchijlkdifdfljhljhikik"),
)
SMALL_ROWS = 24


def outer_steps(wide):
    return tuple(("wide", 1 << level) for level in range(3, wide.bit_length() - 1))


def step_bit(step):
    axis, mask = step
    return lax.rem(lax.div(lax.axis_index(axis), mask), 2)


def step_target(step):
    axis, mask = step
    return {axis: lax.axis_index(axis) + mask * (1 - 2 * step_bit(step))}


def remote(source, target, sems, step):
    return pltpu.make_async_remote_copy(
        source, target, sems.at[0], sems.at[1], device_id=step_target(step), device_id_type=MESH
    )


def greet(steps):
    for step in steps:
        pl.semaphore_signal(
            pltpu.get_barrier_semaphore(), inc=1, device_id=step_target(step), device_id_type=MESH
        )


def lanes(first, size):
    return pl.ds(pl.multiple_of(first, 128), size)


def rows(first, size):
    return pl.ds(pl.multiple_of(first, 16), size)


def dot(left, right):
    return jnp.dot(left, right, preferred_element_type=F32)


def dot_cols(left, right):
    return lax.dot_general(left, right, (((1,), (1,)), ((), ())), preferred_element_type=F32)


def dot_rows(left, right):
    return lax.dot_general(left, right, (((0,), (0,)), ((), ())), preferred_element_type=F32)


def normalize(values):
    mean_val = jnp.mean(values, axis=-1, keepdims=True)
    centered = values - mean_val
    inv_std = lax.rsqrt(jnp.mean(centered * centered, axis=-1, keepdims=True) + EPS)
    return centered * inv_std, inv_std


def norm_back(grad, normed, inv_std, gain):
    scaled = grad * gain
    first_mean = jnp.mean(scaled, axis=-1, keepdims=True)
    second_mean = jnp.mean(scaled * normed, axis=-1, keepdims=True)
    return inv_std * (scaled - first_mean - normed * second_mean)


def add_rows(total, first, inbox, box, count):
    block = min(count, 4 * PIECE)

    def body(i, carry):
        here = rows(first + i * block, block)
        both = total[here, :].astype(F32) + inbox[rows(box + i * block, block), :].astype(F32)
        total[here, :] = both.astype(total.dtype)
        return carry

    lax.fori_loop(0, count // block, body, 0)


def chunk_task(route, outer, mine, inbox, sems, place):
    first, size, box = 0, SIDE, 0
    firsts = []
    free = iter(range(sems.shape[0]))
    for step in route:
        half = size // 2
        bit = step_bit(step)
        keep, give = first + bit * half, first + (1 - bit) * half
        copy = remote(mine.at[rows(give, half), :], inbox.at[pl.ds(box, half), :], sems.at[next(free)], step)
        copy.start()
        yield
        copy.wait()
        add_rows(mine, keep, inbox, box, half)
        firsts.append(first)
        first, size, box = keep, half, box + half
    for step in outer:
        copy = remote(mine.at[rows(first, size), :], inbox.at[pl.ds(box, size), :], sems.at[next(free)], step)
        copy.start()
        copy.wait()
        add_rows(mine, first, inbox, box, size)
        box += size
    kept = pltpu.make_async_copy(mine.at[rows(first, size), :], place(first, size), sems.at[next(free), 0])
    kept.start()
    for step, before in zip(reversed(route), reversed(firsts)):
        source = mine.at[rows(first, size), :] if size == PIECE else place(first, size)
        copy = remote(source, place(first, size), sems.at[next(free)], step)
        copy.start()
        yield
        copy.wait()
        if size == PIECE:
            kept.wait()
        first, size = before, size * 2
    copy = remote(place(0, SIDE), place(0, SIDE), sems.at[next(free)], SIBLING)
    copy.start()
    yield
    copy.wait()


def small_task(steps, total, inbox, sems):
    for slot, step in enumerate(steps):
        copy = remote(total, inbox.at[slot], sems.at[slot], step)
        copy.start()
        yield
        copy.wait()
        total[...] += inbox[slot]


def landing(index, side, o_up, o_down, o_qkv, o_out):
    square, right = divmod(index, 2)
    if square in (0, 2):
        start = side * (2 * SIDE) + square // 2 * SIDE
        return lambda first, size: o_down.at[rows(start + first, size), pl.ds(right * HALF, HALF)]
    if square in (1, 3):
        array, start = o_up, side * (2 * SIDE) + square // 2 * SIDE + right * HALF
    elif index < CHUNKS - 1:
        array, start = o_qkv, side * (3 * HALF) + (index - 8) * HALF
    else:
        array, start = o_out, side * HALF
    return lambda first, size: array.at[rows(first, size), lanes(start, HALF)]


def layer_kernel(
    outer,
    x_in, ln1_gain, ln1_shift, w_qkv_in, q_bias, v_bias, w_out_in, out_bias, table_x, table_y, ln2_gain, ln2_shift,
    w_up_in, up_bias, w_down_in, down_bias, cot_in, page_ids, corners,
    o_output, o_inputs, o_up, o_down, o_qkv, o_out, small,
    w_qkv, w_out, w_up, w_down, mine, inbox, small_in,
    probs, low_a, low_b, low_c, low_d,
    wide_f, key_f, x_all, g_all, xn1, xn2, att, query, keys, values, act, gh, act_give, gh_give,
    gb, gb_all, gatt, gj, gj_all, index_x, index_y, col, one_key, one_query, tables, out_give, out_far, in_give, in_far,
    load_sems, ex_sems, sems, small_sems,
):
    inner = (SIBLING, ALONG_Y, ALONG_X, NEAR_Z, FAR_Z)
    place = lax.axis_index("blk")
    side = step_bit(SIBLING)
    row = step_bit(ALONG_Y)
    other = 1 - row
    blocks = (place, place + 2 - 4 * row, place + 1 - 2 * side, place + 2 - 4 * row + 1 - 2 * side)
    low_lane = lax.broadcasted_iota(jnp.int32, (OWN, 128), 1) < HEAD_DIM
    exchanges = []

    def exchange(source, target, step):
        copy = remote(source, target, ex_sems.at[len(exchanges)], step)
        copy.start()
        exchanges.append(copy)
        return copy

    loads = []
    for slot, (array, held) in enumerate(((w_qkv_in, w_qkv), (w_out_in, w_out), (w_up_in, w_up), (w_down_in, w_down))):
        copy = pltpu.make_async_copy(array, held, load_sems.at[slot])
        copy.start()
        loads.append(copy)

    greet(inner + outer)
    x_all[0:BLOCK, :] = x_in[row]
    g_all[0:BLOCK, :] = cot_in[row]

    tables[0:HEADS, 0:BUCKETS] = table_x[...]
    tables[0:HEADS, BUCKETS : 2 * BUCKETS] = table_y[...]

    def along(kind, block):
        here = lanes(block * BLOCK, BLOCK)
        source = page_ids[:, here] if kind == 2 else corners[kind, :, here]
        return jnp.broadcast_to(jnp.where(row == 0, source[0:1], source[1:2]), (BLOCK, BLOCK))

    for kind in range(3):
        for slot, block in enumerate(blocks):
            down = along(kind, block).astype(F32).T.astype(jnp.int32)
            col[kind, slot * BLOCK : (slot + 1) * BLOCK, :] = down
    lane = lax.broadcasted_iota(jnp.int32, (BLOCK, BLOCK), 1)
    line = lax.broadcasted_iota(jnp.int32, (BLOCK, BLOCK), 0)
    for slot, block in enumerate(blocks):
        part = slice(slot * BLOCK, (slot + 1) * BLOCK)
        bins_x = lax.shift_right_arithmetic(col[0, part, :], 4) + 1
        bins_y = lax.shift_right_arithmetic(col[1, part, :], 4) + 1 + BUCKETS
        one_key[part, :] = jnp.where(lane == jnp.where(lane < BUCKETS, bins_x, bins_y), 1.0, 0.0).astype(BF16)
        if slot < 2:
            turned_x = BUCKETS - 1 - lax.shift_right_arithmetic(along(0, block), 4)
            turned_y = 2 * BUCKETS - 1 - lax.shift_right_arithmetic(along(1, block), 4)
            one_query[:, part] = jnp.where(line == jnp.where(line < BUCKETS, turned_x, turned_y), 1.0, 0.0).astype(BF16)
        for upper in range(2):
            q_part = slice(upper * BLOCK, (upper + 1) * BLOCK)

            def bucket(kind):
                away = lax.shift_right_arithmetic(along(kind, block) - col[kind, q_part, :], 4)
                return jnp.clip(away, -(BUCKETS // 2), BUCKETS // 2 - 1) + BUCKETS // 2

            same = along(2, block) == col[2, q_part, :]
            index_x[q_part, part] = bucket(0)
            index_y[q_part, part] = jnp.where(same, bucket(1) + BUCKETS, -1)

    pl.semaphore_wait(pltpu.get_barrier_semaphore(), len(inner + outer))
    x_copy = exchange(x_in.at[other], x_all.at[pl.ds(BLOCK, BLOCK), :], ALONG_Y)
    g_copy = exchange(cot_in.at[other], g_all.at[pl.ds(BLOCK, BLOCK), :], ALONG_Y)

    def bias_pair(pair, carry):
        for odd in range(2):
            table = tables[pl.ds(2 * pair + odd, 1), :]
            table = jnp.broadcast_to(table, (OWN, 128))
            for slot in range(4):
                part = slice(slot * BLOCK, (slot + 1) * BLOCK)
                at_y = index_y[:, part]
                bias = jnp.take_along_axis(table, index_x[:, part], axis=1, mode="promise_in_bounds") + jnp.take_along_axis(
                    table, jnp.bitwise_and(at_y, 127), axis=1, mode="promise_in_bounds"
                )
                probs[pair, odd * OWN : (odd + 1) * OWN, part] = jnp.where(at_y >= 0, bias, MASKED)
        return carry

    lax.fori_loop(0, 4, bias_pair, 0)

    gain1, shift1 = ln1_gain[...].reshape(1, WIDTH), ln1_shift[...].reshape(1, WIDTH)
    gain2, shift2 = ln2_gain[...].reshape(1, WIDTH), ln2_shift[...].reshape(1, WIDTH)

    def first_norm(part):
        normed, _ = normalize(x_all[part, :].astype(F32))
        xn1[part, :] = (normed * gain1 + shift1).astype(BF16)

    first_norm(slice(0, BLOCK))
    x_copy.wait()
    first_norm(slice(BLOCK, OWN))
    loads[0].wait()
    keys[0:OWN, :] = dot(xn1[0:OWN, :], w_qkv[:, WIDTH : 2 * WIDTH]).astype(BF16)
    k_copy = exchange(keys.at[pl.ds(0, OWN), :], keys.at[pl.ds(OWN, OWN), :], SIBLING)
    values[0:OWN, :] = (dot(xn1[0:OWN, :], w_qkv[:, 2 * WIDTH :]) + v_bias[...].reshape(1, WIDTH)).astype(BF16)
    v_copy = exchange(values.at[pl.ds(0, OWN), :], values.at[pl.ds(OWN, OWN), :], SIBLING)
    xn1_copy = exchange(xn1.at[pl.ds(0, OWN), :], xn1.at[pl.ds(OWN, OWN), :], SIBLING)
    joined = (dot(xn1[0:OWN, :], w_qkv[:, 0:WIDTH]) + q_bias[...].reshape(1, WIDTH)).astype(BF16)
    query[...] = joined * jnp.asarray(HEAD_DIM**-0.5, BF16)
    g_copy.wait()
    gs_copy = exchange(g_all.at[pl.ds(0, OWN), :], g_all.at[pl.ds(OWN, OWN), :], SIBLING)
    lax.fori_loop(4, PAIRS, bias_pair, 0)
    k_copy.wait()
    v_copy.wait()

    def split_heads(two):
        none = jnp.zeros_like(two)
        return jnp.concatenate((jnp.where(low_lane, two, none), jnp.where(low_lane, none, two)), axis=0)

    def join_heads(stacked):
        return jnp.where(low_lane, stacked[0:OWN], stacked[OWN:])

    def attend(pair, carry):
        here = lanes(pair * 128, 128)
        q_two = split_heads(query[:, here])
        for part in quarters:
            masked = dot_cols(q_two[part], keys[:, here]) + probs[pair, part, :]
            terms = jnp.exp(masked - jnp.max(masked, axis=-1, keepdims=True))
            weights = terms * (1.0 / jnp.sum(terms, axis=-1, keepdims=True))
            probs[pair, part, :] = weights
            low_a[part, :] = weights.astype(BF16)
        att[0:OWN, here] = join_heads(dot(low_a[...], values[:, here])).astype(BF16)
        return carry

    quarters = [slice(k * BLOCK, (k + 1) * BLOCK) for k in range(4)]
    lax.fori_loop(0, PAIRS, attend, 0)
    att_copy = exchange(att.at[pl.ds(0, OWN), :], att.at[pl.ds(OWN, OWN), :], SIBLING)
    middle, total, back = wide_f.at[0], wide_f.at[1], wide_f.at[2]
    loads[1].wait()
    total[...] = dot(att[0:OWN, :], w_out[...])

    def second_norm(part):
        here = x_all[part, :].astype(F32) + (total[part, :] + out_bias[...].reshape(1, WIDTH))
        middle[part, :] = here
        normed, _ = normalize(here)
        xn2[part, :] = (normed * gain2 + shift2).astype(BF16)

    for part in quarters[0:2]:
        second_norm(part)
    xn2_copy = exchange(xn2.at[pl.ds(0, OWN), :], xn2.at[pl.ds(OWN, OWN), :], SIBLING)
    loads[2].wait()
    loads[3].wait()

    def feed(number, first, act_to, gh_to):
        for third in range(3):
            here = lanes(first + third * 256, 256)
            there = slice(third * 256, (third + 1) * 256)
            value = dot(xn2[0:OWN, :], w_up[:, here]) + up_bias[here].reshape(1, 256)
            grad = dot_cols(g_all[0:OWN, :], w_down[rows(first + third * 256, 256), :])
            below = 0.5 * (1.0 + lax.erf(value * math.sqrt(0.5)))
            slope = below + value * (jnp.exp(-0.5 * value * value) * (1.0 / math.sqrt(2.0 * math.pi)))
            act_to[:, there] = (value * below).astype(BF16)
            grad_hidden = (grad * slope).astype(BF16)
            gh_to[:, there] = grad_hidden
            small[pl.ds(8 + lax.div(first, WIDTH), 1), there] = jnp.sum(grad_hidden.astype(F32), axis=0, keepdims=True)
        forward = dot(act_to[...], w_down[rows(first, WIDTH), :])
        backward = dot_cols(gh_to[...], w_up[:, lanes(first, WIDTH)])
        if number:
            total[...] += forward
            back[...] += backward
        else:
            total[...] = forward
            back[...] = backward

    def contract(index, first, left, right, width):
        def body(i, carry):
            here = lanes(i * 256, 256)
            mine[index, rows(i * 256, 256), first : first + width] = dot_rows(left[:, here], right[...]).astype(BF16)
            return carry

        lax.fori_loop(0, SIDE // 256, body, 0)

    tasks = {
        name: chunk_task(
            [STEPS[step] for step in ROUTES[k]], outer, mine.at[k // 2, :, pl.ds(k % 2 * HALF, HALF)], inbox.at[k],
            sems.at[k], landing(k, side, o_up, o_down, o_qkv, o_out),
        )
        for k, name in enumerate(NAMES)
    }
    tasks["s"] = small_task(inner + outer, small, small_in, small_sems)
    plan = iter(PLAN)

    def pump():
        for names in next(plan):
            for name in names:
                next(tasks[name], None)

    def feed_half(half):
        given = (1 - side) * (2 * WIDTH) + half * WIDTH
        kept = side * (2 * WIDTH) + half * WIDTH
        feed(2 * half, given, act_give.at[half], gh_give.at[half])
        act_copy = exchange(act_give.at[half], act.at[half, pl.ds(OWN, OWN), :], SIBLING)
        gh_copy = exchange(gh_give.at[half], gh.at[half, pl.ds(OWN, OWN), :], SIBLING)
        if half:
            pump()
        feed(2 * half + 1, kept, act.at[half, pl.ds(0, OWN), :], gh.at[half, pl.ds(0, OWN), :])
        if half:
            pump()
        else:
            gs_copy.wait()
            xn2_copy.wait()
        act_copy.wait()
        contract(2 * half, 0, act.at[half], g_all, WIDTH)
        pump()
        gh_copy.wait()
        contract(2 * half + 1, 0, xn2, gh.at[half], WIDTH)
        pump()

    feed_half(0)
    feed_half(1)

    def second_back(part):
        normed, inv_std = normalize(middle[part, :])
        total[part, :] = middle[part, :] + (total[part, :] + down_bias[...].reshape(1, WIDTH))
        grad = back[part, :]
        grad_out = g_all[part, :].astype(F32)
        grad_middle = grad_out + norm_back(grad, normed, inv_std, gain2)
        middle[part, :] = grad_middle
        low = grad_middle.astype(BF16)
        gb[part, :] = low
        return grad * normed, grad, grad_out, low.astype(F32)

    def sum_up(slots, work):
        for number, part in enumerate(quarters[0:2]):
            for slot, value in zip(slots, work(part)):
                value = jnp.sum(value, axis=0, keepdims=True)
                small[slot : slot + 1, :] = small[slot : slot + 1, :] + value if number else value

    sum_up((5, 6, 7, 4), second_back)
    out_give[...] = total[BLOCK:OWN, :].astype(BF16)
    out_copy = exchange(out_give, out_far, ALONG_Y)
    own_out = pltpu.make_async_copy(total.at[pl.ds(0, BLOCK), :], o_output.at[row], load_sems.at[4])
    own_out.start()
    gb_all[0:OWN, :] = gb[:, lanes(side * 384, 384)]
    gb_copy = exchange(gb.at[:, lanes((1 - side) * 384, 384)], gb_all.at[pl.ds(OWN, OWN), :], SIBLING)
    gatt[...] = dot_cols(gb[...], w_out[...]).astype(BF16)
    pump()

    rest = [jnp.concatenate([along(kind, block)[0:1] for block in blocks], axis=1) for kind in range(2)]
    rest_x, rest_y = (jnp.bitwise_and(value, BIN_PX - 1) for value in rest)

    def attend_back(pair):
        here = slice(pair * 128, pair * 128 + 128)
        q_two, grad_two = split_heads(query[:, here]), split_heads(gatt[:, here])
        for number, part in enumerate(quarters):
            weights = probs[pair, part, :]
            grad_probs = dot_cols(grad_two[part], values[:, here])
            inner_sum = jnp.sum(weights * grad_probs, axis=-1, keepdims=True)
            grad_scores = weights * (grad_probs - inner_sum)
            low_a[part, :] = weights.astype(BF16)
            low_b[part, :] = grad_scores.astype(BF16)
            for kind, key_rest, low in ((0, rest_x, low_c), (1, rest_y, low_d)):
                own_rest = jnp.bitwise_and(col[kind, quarters[number % 2], :], BIN_PX - 1)
                less = key_rest < jnp.concatenate([own_rest] * 4, axis=1)
                low[part, :] = jnp.where(less, grad_scores, 0.0).astype(BF16)
        grad_scores = low_b[...]
        grad_query = join_heads(dot(grad_scores, keys[:, here])) * HEAD_DIM**-0.5
        gj[:, here] = grad_query.astype(BF16)
        grad_key = dot(q_two.T, grad_scores).T
        grad_value = dot(grad_two.T, low_a[...]).T
        total_k, total_v = key_f.at[0], key_f.at[1]
        give_k, give_v = wide_f.at[3], wide_f.at[4]
        total_k[:, here], give_k[:, here] = grad_key[0:OWN], grad_key[OWN:]
        total_v[:, here], give_v[:, here] = grad_value[0:OWN], grad_value[OWN:]
        shared.append(exchange(give_k.at[:, here], key_f.at[2, :, here], SIBLING))
        shared.append(exchange(give_v.at[:, here], key_f.at[3, :, here], SIBLING))

        every = dot(grad_scores, one_key[...])
        both = lax.broadcasted_iota(jnp.int32, (FULL, 128), 1) < BUCKETS
        less = jnp.where(both, dot(low_c[...], one_key[...]), dot(low_d[...], one_key[...]))
        by_key = every - less + pltpu.roll(less, 127, 1)
        upper = by_key.astype(BF16)
        lower = (by_key - upper.astype(F32)).astype(BF16)
        left_half = lax.broadcasted_iota(jnp.int32, (BUCKETS, 128), 1) < BUCKETS
        spot = lax.broadcasted_iota(jnp.int32, (1, 128), 1)
        for odd in range(2):
            mine_part = slice(odd * OWN, (odd + 1) * OWN)
            table = dot(one_query[...], upper[mine_part]) + dot(one_query[...], lower[mine_part])
            found = []
            for part in (table[0:BUCKETS], pltpu.roll(table[BUCKETS:], BUCKETS, 1)):
                skewed = pltpu.roll(jnp.where(left_half, part, 0.0), 0, 1, stride=1, stride_axis=0)
                line_sum = jnp.sum(skewed, axis=0, keepdims=True)
                below = jnp.sum(jnp.where(spot <= 32, line_sum, 0.0), axis=-1, keepdims=True)
                above = jnp.sum(jnp.where(spot >= 95, line_sum, 0.0), axis=-1, keepdims=True)
                inside = pltpu.roll(line_sum, 96, 1)
                found.append(jnp.where(spot == 0, below, jnp.where(spot == BUCKETS - 1, above, inside)))
            merged = jnp.where(spot < BUCKETS, found[0], pltpu.roll(found[1], BUCKETS, 1))
            at = 12 + 2 * pair + odd
            small[at : at + 1, :] = jnp.concatenate((merged, jnp.zeros((1, WIDTH - 128), F32)), axis=1)

    shared = []
    for pair in range(PAIRS):
        attend_back(pair)
        if pair == 0:
            att_copy.wait()
            gb_copy.wait()
            contract(5, HALF, att, gb_all, HALF)
        pump()
    xn1_copy.wait()
    for copy in shared:
        copy.wait()

    def join_kv(part):
        low_k = (key_f[0, part, :] + key_f[2, part, :]).astype(BF16)
        low_v = (key_f[1, part, :] + key_f[3, part, :]).astype(BF16)
        gj[part, WIDTH : 2 * WIDTH] = low_k
        gj[part, 2 * WIDTH :] = low_v
        return gj[part, 0:WIDTH].astype(F32), low_v.astype(F32)

    sum_up((2, 3), join_kv)
    gj_copy = exchange(gj.at[:, lanes((1 - side) * 1152, 1152)], gj_all.at[pl.ds(OWN, OWN), :], SIBLING)
    gj_all[0:OWN, :] = gj[:, lanes(side * 1152, 1152)]
    back[...] = (
        dot_cols(gj[:, 0:WIDTH], w_qkv[:, 0:WIDTH])
        + dot_cols(gj[:, WIDTH : 2 * WIDTH], w_qkv[:, WIDTH : 2 * WIDTH])
        + dot_cols(gj[:, 2 * WIDTH :], w_qkv[:, 2 * WIDTH :])
    )
    gj_copy.wait()
    pump()
    contract(4, 0, xn1, gj_all.at[:, pl.ds(0, WIDTH)], WIDTH)
    pump()
    contract(5, 0, xn1, gj_all.at[:, pl.ds(WIDTH, HALF)], HALF)
    pump()

    def first_back(part):
        normed, inv_std = normalize(x_all[part, :].astype(F32))
        grad = back[part, :]
        middle[part, :] = middle[part, :] + norm_back(grad, normed, inv_std, gain1)
        return grad * normed, grad

    sum_up((0, 1), first_back)
    in_give[...] = middle[BLOCK:OWN, :].astype(BF16)
    in_copy = exchange(in_give, in_far, ALONG_Y)
    own_in = pltpu.make_async_copy(middle.at[pl.ds(0, BLOCK), :], o_inputs.at[row], load_sems.at[5])
    own_in.start()

    pump()
    out_copy.wait()
    own_out.wait()
    in_copy.wait()
    own_in.wait()
    total[0:BLOCK, :] = out_far[...].astype(F32)
    middle[0:BLOCK, :] = in_far[...].astype(F32)
    last = (
        pltpu.make_async_copy(total.at[pl.ds(0, BLOCK), :], o_output.at[other], load_sems.at[4]),
        pltpu.make_async_copy(middle.at[pl.ds(0, BLOCK), :], o_inputs.at[other], load_sems.at[5]),
    )
    for copy in last:
        copy.start()
    for copy in last:
        copy.wait()


def per_device(
    inputs, ln1_gain, ln1_shift, w_qkv, q_bias, v_bias, w_out, out_bias, table_x, table_y, ln2_gain, ln2_shift,
    w_up, up_bias, w_down, down_bias, cotangent, page_ids, corners,
):
    outer = outer_steps(lax.axis_size("wide"))
    slots = 10 + len(outer)
    assert inputs.shape == (2, BLOCK, WIDTH) and lax.axis_size("blk") == 4 and lax.axis_size("wide") >= 8
    hbm = pl.BlockSpec(memory_space=pl.ANY)
    vmem = pl.BlockSpec(memory_space=pltpu.VMEM)
    shape = jax.ShapeDtypeStruct
    args = (
        inputs, ln1_gain, ln1_shift, w_qkv, q_bias, v_bias, w_out, out_bias, table_x.T, table_y.T, ln2_gain, ln2_shift,
        w_up, up_bias, w_down, down_bias, cotangent, page_ids, corners,
    )
    large = (3, 6, 12, 14)
    output, grad_inputs, full_up, full_down, full_qkv, full_out, small = pl.pallas_call(
        functools.partial(layer_kernel, outer),
        out_shape=(
            shape(inputs.shape, F32), shape(inputs.shape, F32),
            shape(w_up.shape, BF16), shape(w_down.shape, BF16), shape(w_qkv.shape, BF16), shape(w_out.shape, BF16),
            shape((SMALL_ROWS, WIDTH), F32),
        ),
        in_specs=[hbm if k in large else vmem for k in range(len(args))],
        out_specs=(hbm,) * 6 + (vmem,),
        scratch_shapes=[
            pltpu.VMEM(w_qkv.shape, BF16), pltpu.VMEM(w_out.shape, BF16),
            pltpu.VMEM(w_up.shape, BF16), pltpu.VMEM(w_down.shape, BF16),
            pltpu.VMEM((SQUARES, SIDE, SIDE), BF16),
            pltpu.VMEM((CHUNKS, SIDE - PIECE + PIECE * len(outer), HALF), BF16),
            pltpu.VMEM((5 + len(outer), SMALL_ROWS, WIDTH), F32),
            pltpu.VMEM((PAIRS, FULL, FULL), F32),
            pltpu.VMEM((FULL, FULL), BF16), pltpu.VMEM((FULL, FULL), BF16),
            pltpu.VMEM((FULL, FULL), BF16), pltpu.VMEM((FULL, FULL), BF16),
            pltpu.VMEM((5, OWN, WIDTH), F32), pltpu.VMEM((4, OWN, WIDTH), F32),
            pltpu.VMEM((OWN, WIDTH), BF16), pltpu.VMEM((FULL, WIDTH), BF16),
            pltpu.VMEM((FULL, WIDTH), BF16), pltpu.VMEM((FULL, WIDTH), BF16), pltpu.VMEM((FULL, WIDTH), BF16),
            pltpu.VMEM((OWN, WIDTH), BF16), pltpu.VMEM((FULL, WIDTH), BF16), pltpu.VMEM((FULL, WIDTH), BF16),
            pltpu.VMEM((2, FULL, WIDTH), BF16), pltpu.VMEM((2, FULL, WIDTH), BF16),
            pltpu.VMEM((2, OWN, WIDTH), BF16), pltpu.VMEM((2, OWN, WIDTH), BF16),
            pltpu.VMEM((OWN, WIDTH), BF16), pltpu.VMEM((FULL, 384), BF16), pltpu.VMEM((OWN, WIDTH), BF16),
            pltpu.VMEM((OWN, 3 * WIDTH), BF16), pltpu.VMEM((FULL, 1152), BF16),
            pltpu.VMEM((OWN, FULL), jnp.int32), pltpu.VMEM((OWN, FULL), jnp.int32),
            pltpu.VMEM((3, FULL, 128), jnp.int32),
            pltpu.VMEM((FULL, 128), BF16), pltpu.VMEM((128, OWN), BF16), pltpu.VMEM((HEADS, 128), F32),
            pltpu.VMEM((BLOCK, WIDTH), BF16), pltpu.VMEM((BLOCK, WIDTH), BF16),
            pltpu.VMEM((BLOCK, WIDTH), BF16), pltpu.VMEM((BLOCK, WIDTH), BF16),
            pltpu.SemaphoreType.DMA((6,)),
            pltpu.SemaphoreType.DMA((32, 2)),
            pltpu.SemaphoreType.DMA((CHUNKS, slots, 2)),
            pltpu.SemaphoreType.DMA((5 + len(outer), 2)),
        ],
        compiler_params=pltpu.CompilerParams(
            collective_id=0, has_side_effects=True, vmem_limit_bytes=63 * MIB
        ),
        cost_estimate=pl.CostEstimate(flops=13 * 10**9, bytes_accessed=3 * 10**7, transcendentals=10**7),
    )(*args)
    ended = finish(full_up, full_down, full_qkv, full_out, output, grad_inputs, small)
    f_up, f_down, f_qkv, f_out, output, grad_inputs, grad_x, grad_y, f_upb = ended[:9]
    f_ln1g, f_ln1s, f_qb, f_vb, f_outb, f_ln2g, f_ln2s, f_downb = ended[9:]
    return (
        output, grad_inputs, f_ln1g, f_ln1s, f_qkv, f_qb, f_vb, f_out, f_outb, grad_x.T, grad_y.T, f_ln2g, f_ln2s,
        f_up, f_upb, f_down, f_downb,
    )


def finish_kernel(*refs):
    small, outs = refs[6], refs[7:]
    for source, target in zip(refs[:6], outs[:6]):
        target[...] = source[...].astype(target.dtype)

    @pl.when(pl.program_id(0) == 0)
    def _():
        outs[6][...] = small[12:SMALL_ROWS, 0:BUCKETS]
        outs[7][...] = small[12:SMALL_ROWS, BUCKETS : 2 * BUCKETS]
        for part in range(FF // WIDTH):
            outs[8][part * WIDTH : (part + 1) * WIDTH] = small[8 + part, :]
        for slot in range(8):
            outs[9 + slot][...] = small[slot, :]


def finish(*arrays):
    steps = 16

    def slab(array):
        if array.ndim == 3:
            return pl.BlockSpec((array.shape[0], array.shape[1] // steps, array.shape[2]), lambda i: (0, i, 0))
        return pl.BlockSpec((array.shape[0] // steps, array.shape[1]), lambda i: (i, 0))

    def whole(shape):
        return pl.BlockSpec(shape, lambda i: (0,) * len(shape))

    little = [(HEADS, BUCKETS)] * 2 + [(FF,)] + [(WIDTH,)] * 8
    slabs = [slab(array) for array in arrays[:6]]
    return pl.pallas_call(
        finish_kernel,
        grid=(steps,),
        out_shape=[jax.ShapeDtypeStruct(array.shape, F32) for array in arrays[:6]]
        + [jax.ShapeDtypeStruct(shape, F32) for shape in little],
        in_specs=slabs + [whole((SMALL_ROWS, WIDTH))],
        out_specs=slabs + [whole(shape) for shape in little],
        compiler_params=pltpu.CompilerParams(vmem_limit_bytes=60 * MIB),
        cost_estimate=pl.CostEstimate(flops=10**7, bytes_accessed=45 * 10**6, transcendentals=0),
    )(*arrays)


def solution(mesh):
    tokens, row_of_blk = P("wide", "blk", None), P("wide", None)
    return jax.shard_map(
        per_device,
        mesh=mesh,
        in_specs=(tokens,) + (P(),) * 15 + (tokens, row_of_blk, P(None, "wide", None)),
        out_specs=(tokens, tokens) + (P(),) * 15,
        check_vma=False,
    )
```

```python
import functools
import math

import jax
import jax.numpy as jnp
from jax import lax
from jax.experimental import pallas as pl
from jax.experimental.pallas import tpu as pltpu
from jax.sharding import PartitionSpec as P

HEADS = 12
HEAD_DIM = 64
BUCKETS = 64
BIN_PX = 16
MASKED = -1e30
EPS = 1e-05
MESH = pl.DeviceIdType.MESH
MIB = 1024 * 1024
F32, BF16 = jnp.float32, jnp.bfloat16

BLOCK = 128
OWN = 2 * BLOCK
FULL = 2 * OWN
WIDTH = HEADS * HEAD_DIM
FF = 4 * WIDTH
PAIRS = HEADS // 2

SQUARES = 6
CHUNKS = 2 * SQUARES
SIDE = WIDTH
HALF = SIDE // 2
PIECE = SIDE // 16
SIBLING = ("blk", 1)
ALONG_Y, ALONG_X, NEAR_Z, FAR_Z = ("blk", 2), ("wide", 1), ("wide", 2), ("wide", 4)
STEPS = {"Y": ALONG_Y, "X": ALONG_X, "1": NEAR_Z, "2": FAR_Z}
NAMES = "abcdefghijkl"
ROUTES = ("XY21", "YX12", "1X2Y", "YX12", "XY12", "YX12", "YX12", "1YX2", "XY12", "XY21", "YX12", "12YX")
PLAN = (
    ("ab",), ("cd",), ("",), ("",), ("ef",), ("h",), ("abc",), ("lde",), ("hb",), ("fc",), ("gld",), ("b",),
    ("fac",), ("ed",), ("ijhl",), ("kbf",),
    ("segacsdlbifaedbkajfhedcgsflaheibgjckhiadgsekjfil", "gsjcbkhigbjsdadacfkicelfkejghikljhhigilgljkjk"),
)
SMALL_ROWS = 24

SLAB = 384 * WIDTH
SLOTS = 8


def outer_steps(wide):
    return tuple(("wide", 1 << level) for level in range(3, wide.bit_length() - 1))


def step_bit(step):
    axis, mask = step
    return lax.rem(lax.div(lax.axis_index(axis), mask), 2)


def step_target(step):
    axis, mask = step
    return {axis: lax.axis_index(axis) + mask * (1 - 2 * step_bit(step))}


def remote(source, target, sems, step):
    return pltpu.make_async_remote_copy(
        source, target, sems.at[0], sems.at[1], device_id=step_target(step), device_id_type=MESH
    )


def greet(steps):
    for step in steps:
        pl.semaphore_signal(
            pltpu.get_barrier_semaphore(), inc=1, device_id=step_target(step), device_id_type=MESH
        )


def lanes(first, size):
    return pl.ds(pl.multiple_of(first, 128), size)


def rows(first, size):
    return pl.ds(pl.multiple_of(first, 16), size)


def dot(left, right):
    return jnp.dot(left, right, preferred_element_type=F32)


def dot_cols(left, right):
    return lax.dot_general(left, right, (((1,), (1,)), ((), ())), preferred_element_type=F32)


def dot_rows(left, right):
    return lax.dot_general(left, right, (((0,), (0,)), ((), ())), preferred_element_type=F32)


def normalize(values):
    mean_val = jnp.mean(values, axis=-1, keepdims=True)
    centered = values - mean_val
    inv_std = lax.rsqrt(jnp.mean(centered * centered, axis=-1, keepdims=True) + EPS)
    return centered * inv_std, inv_std


def norm_back(grad, normed, inv_std, gain):
    scaled = grad * gain
    first_mean = jnp.mean(scaled, axis=-1, keepdims=True)
    second_mean = jnp.mean(scaled * normed, axis=-1, keepdims=True)
    return inv_std * (scaled - first_mean - normed * second_mean)


def add_rows(total, first, inbox, box, count):
    block = min(count, 4 * PIECE)

    def body(i, carry):
        here = rows(first + i * block, block)
        both = total[here, :].astype(F32) + inbox[rows(box + i * block, block), :].astype(F32)
        total[here, :] = both.astype(total.dtype)
        return carry

    lax.fori_loop(0, count // block, body, 0)


def chunk_task(route, outer, mine, inbox, sems, place):
    first, size, box = 0, SIDE, 0
    firsts = []
    free = iter(range(sems.shape[0]))
    for step in route:
        half = size // 2
        bit = step_bit(step)
        keep, give = first + bit * half, first + (1 - bit) * half
        copy = remote(mine.at[rows(give, half), :], inbox.at[pl.ds(box, half), :], sems.at[next(free)], step)
        copy.start()
        yield
        copy.wait()
        add_rows(mine, keep, inbox, box, half)
        firsts.append(first)
        first, size, box = keep, half, box + half
    for step in outer:
        copy = remote(mine.at[rows(first, size), :], inbox.at[pl.ds(box, size), :], sems.at[next(free)], step)
        copy.start()
        copy.wait()
        add_rows(mine, first, inbox, box, size)
        box += size
    kept = pltpu.make_async_copy(mine.at[rows(first, size), :], place(first, size), sems.at[next(free), 0])
    kept.start()
    for step, before in zip(reversed(route), reversed(firsts)):
        source = mine.at[rows(first, size), :] if size == PIECE else place(first, size)
        copy = remote(source, place(first, size), sems.at[next(free)], step)
        copy.start()
        yield
        copy.wait()
        if size == PIECE:
            kept.wait()
        first, size = before, size * 2
    copy = remote(place(0, SIDE), place(0, SIDE), sems.at[next(free)], SIBLING)
    copy.start()
    yield
    copy.wait()


def small_task(steps, total, inbox, sems):
    for slot, step in enumerate(steps):
        copy = remote(total, inbox.at[slot], sems.at[slot], step)
        copy.start()
        yield
        copy.wait()
        total[...] += inbox[slot]


def landing(index, side, o_up, o_down, o_qkv, o_out):
    square, right = divmod(index, 2)
    if square in (0, 2):
        start = side * (2 * SIDE) + square // 2 * SIDE
        return lambda first, size: o_down.at[rows(start + first, size), pl.ds(right * HALF, HALF)]
    if square in (1, 3):
        array, start = o_up, side * (2 * SIDE) + square // 2 * SIDE + right * HALF
    elif index < CHUNKS - 1:
        array, start = o_qkv, side * (3 * HALF) + (index - 8) * HALF
    else:
        array, start = o_out, side * HALF
    return lambda first, size: array.at[rows(first, size), lanes(start, HALF)]


def layer_kernel(
    outer,
    x_in, ln1_gain_in, ln1_shift_in, w_qkv_in, q_bias_in, v_bias_in, w_out_in, out_bias_in, table_x_in, table_y_in,
    ln2_gain_in, ln2_shift_in, w_up_in, up_bias_in, w_down_in, down_bias_in, cot_in, page_ids_in, corners_in,
    o_output, o_inputs, o_up, o_down, o_qkv, o_out, o_small,
    ln1_gain, ln1_shift, q_bias, v_bias, out_bias, ln2_gain, ln2_shift, down_bias, up_bias, table_x, table_y,
    page_ids, corners, small,
    w_qkv, w_out, w_up, w_down, mine, inbox, small_in,
    probs, low_a, low_b, low_c, low_d,
    wide_f, key_f, x_all, g_all, xn1, xn2, att, query, keys, values, act, gh, act_give, gh_give,
    gb, gb_all, gatt, gj, gj_all, col, key_twice, one_key, one_query, tables, out_give, out_far, in_give, in_far,
    load_sems, ex_sems, sems, small_sems,
):
    inner = (SIBLING, ALONG_Y, ALONG_X, NEAR_Z, FAR_Z)
    place = lax.axis_index("blk")
    side = step_bit(SIBLING)
    row = step_bit(ALONG_Y)
    other = 1 - row
    blocks = (place, place + 2 - 4 * row, place + 1 - 2 * side, place + 2 - 4 * row + 1 - 2 * side)
    low_lane = lax.broadcasted_iota(jnp.int32, (OWN, 128), 1) < HEAD_DIM
    exchanges = []

    def exchange(source, target, step):
        copy = remote(source, target, ex_sems.at[len(exchanges)], step)
        copy.start()
        exchanges.append(copy)
        return copy

    greet(inner + outer)
    pairs = (
        (corners_in, corners), (page_ids_in, page_ids), (table_x_in, table_x), (table_y_in, table_y),
        (x_in.at[row], x_all.at[pl.ds(0, BLOCK), :]),
        (ln1_gain_in, ln1_gain), (ln1_shift_in, ln1_shift), (v_bias_in, v_bias),
        (w_qkv_in, w_qkv),
        (q_bias_in, q_bias), (cot_in.at[row], g_all.at[pl.ds(0, BLOCK), :]), (out_bias_in, out_bias),
        (ln2_gain_in, ln2_gain), (ln2_shift_in, ln2_shift), (down_bias_in, down_bias), (up_bias_in, up_bias),
        (w_out_in, w_out), (w_up_in, w_up), (w_down_in, w_down),
    )
    loads = [pltpu.make_async_copy(source, held, load_sems.at[k]) for k, (source, held) in enumerate(pairs)]
    waited = iter(loads)

    def loaded(count):
        for _ in range(count):
            next(waited).wait()

    for copy in loads:
        copy.start()
    pl.semaphore_wait(pltpu.get_barrier_semaphore(), len(inner + outer))
    x_copy = exchange(x_in.at[other], x_all.at[pl.ds(BLOCK, BLOCK), :], ALONG_Y)
    g_copy = exchange(cot_in.at[other], g_all.at[pl.ds(BLOCK, BLOCK), :], ALONG_Y)
    loaded(4)

    def along(kind, block):
        here = lanes(block * BLOCK, BLOCK)
        source = page_ids[:, here] if kind == 2 else corners[kind, :, here]
        return jnp.broadcast_to(jnp.where(row == 0, source[0:1], source[1:2]), (BLOCK, BLOCK))

    for kind in range(3):
        for slot, block in enumerate(blocks):
            down = along(kind, block).astype(F32).T.astype(jnp.int32)
            col[kind, slot * BLOCK : (slot + 1) * BLOCK, :] = down
    lane = lax.broadcasted_iota(jnp.int32, (BLOCK, BLOCK), 1)
    line = lax.broadcasted_iota(jnp.int32, (BLOCK, BLOCK), 0)
    for slot, block in enumerate(blocks):
        part = slice(slot * BLOCK, (slot + 1) * BLOCK)
        bins_x = lax.shift_right_arithmetic(col[0, part, :], 4) + 1
        bins_y = lax.shift_right_arithmetic(col[1, part, :], 4) + 1 + BUCKETS
        one_key[part, :] = jnp.where(lane == jnp.where(lane < BUCKETS, bins_x, bins_y), 1.0, 0.0).astype(BF16)
        if slot < 2:
            turned_x = BUCKETS - 1 - lax.shift_right_arithmetic(along(0, block), 4)
            turned_y = 2 * BUCKETS - 1 - lax.shift_right_arithmetic(along(1, block), 4)
            one_query[:, part] = jnp.where(line == jnp.where(line < BUCKETS, turned_x, turned_y), 1.0, 0.0).astype(BF16)
    key_rows = [jnp.concatenate([along(kind, block)[0:1] for block in blocks], axis=1) for kind in range(3)]
    rest_x, rest_y = (jnp.bitwise_and(key_rows[kind], BIN_PX - 1) for kind in range(2))

    def own_lanes(kind, part, mask):
        return jnp.concatenate([jnp.bitwise_and(col[kind, part, :], mask)] * 4, axis=1)


    at = lax.broadcasted_iota(jnp.int32, (16, 128), 1)
    at = jnp.where(at < BUCKETS, jnp.minimum(at, BUCKETS // 2 - 1), jnp.maximum(at - 128, -(BUCKETS // 2))) + BUCKETS // 2
    for kind, table in enumerate((table_x, table_y)):
        tables[0, 0:HEADS, kind * BUCKETS : (kind + 1) * BUCKETS] = table[...]
    for kind in range(2):
        distance = jnp.take_along_axis(tables[0], at + kind * BUCKETS, axis=1, mode="promise_in_bounds")
        for slot, value in ((1, distance), (3, pltpu.roll(distance, 1, 1) - distance)):
            upper = value.astype(BF16).astype(F32)
            tables[kind * 4 + slot] = upper
            tables[kind * 4 + slot + 1] = value - upper

    square_lane = lax.broadcasted_iota(jnp.int32, (128, 128), 1) < BUCKETS
    square_line = lax.broadcasted_iota(jnp.int32, (128, 128), 0) < BUCKETS
    diagonal = square_lane == square_line
    lane_x = jnp.bitwise_and(lax.broadcasted_iota(jnp.int32, (OWN, 256), 1), 127) < BUCKETS
    key_twice[...] = jnp.concatenate((one_key[...], one_key[...]), axis=1)

    def bias_pair(pair, carry):
        for odd in range(2):
            squares = []
            for slot in range(1, 5):
                both = [jnp.broadcast_to(tables[kind * 4 + slot, pl.ds(2 * pair + odd, 1), :], (BUCKETS, 128)) for kind in range(2)]
                moved = pltpu.roll(jnp.concatenate(both, axis=0), 0, 1, stride=1, stride_axis=0)
                squares.append(jnp.where(diagonal, moved, 0.0).astype(BF16))
            picked = dot(one_key[0:OWN, :], jnp.concatenate(squares, axis=1))
            plain, change = picked[:, 0:256].astype(BF16), picked[:, 256:512]
            change_x = jnp.where(lane_x, change, 0.0).astype(BF16)
            change_y = jnp.where(lane_x, 0.0, change).astype(BF16)
            terms = dot_cols(jnp.concatenate((plain, change_x, change_y), axis=0), key_twice[...])
            for number in range(2):
                part = quarters[number]
                bias = terms[part]
                bias += jnp.where(rest_x < own_lanes(0, part, BIN_PX - 1), terms[OWN : 2 * OWN][part], 0.0)
                bias += jnp.where(rest_y < own_lanes(1, part, BIN_PX - 1), terms[2 * OWN :][part], 0.0)
                same = key_rows[2] == own_lanes(2, part, 7)
                probs[pair, odd * OWN + number * BLOCK : odd * OWN + (number + 1) * BLOCK, :] = jnp.where(same, bias, MASKED)
        return carry

    quarters = [slice(k * BLOCK, (k + 1) * BLOCK) for k in range(4)]
    loaded(5)
    gain1, shift1 = ln1_gain[...].reshape(1, WIDTH), ln1_shift[...].reshape(1, WIDTH)
    shared = []

    def first_norm(part):
        normed, _ = normalize(x_all[part, :].astype(F32))
        xn1[part, :] = (normed * gain1 + shift1).astype(BF16)
        keys[part, :] = dot(xn1[part, :], w_qkv[:, WIDTH : 2 * WIDTH]).astype(BF16)
        values[part, :] = (dot(xn1[part, :], w_qkv[:, 2 * WIDTH :]) + v_bias[...].reshape(1, WIDTH)).astype(BF16)
        for held in (keys, values):
            shared.append(exchange(held.at[part, :], held.at[pl.ds(OWN + part.start, BLOCK), :], SIBLING))

    first_norm(quarters[0])
    lax.fori_loop(0, 4, bias_pair, 0)

    loaded(8)
    gain2, shift2 = ln2_gain[...].reshape(1, WIDTH), ln2_shift[...].reshape(1, WIDTH)
    x_copy.wait()
    first_norm(quarters[1])
    xn1_copy = exchange(xn1.at[pl.ds(0, OWN), :], xn1.at[pl.ds(OWN, OWN), :], SIBLING)
    joined = (dot(xn1[0:OWN, :], w_qkv[:, 0:WIDTH]) + q_bias[...].reshape(1, WIDTH)).astype(BF16)
    query[...] = joined * jnp.asarray(HEAD_DIM**-0.5, BF16)
    lax.fori_loop(4, PAIRS, bias_pair, 0)
    for copy in shared:
        copy.wait()

    def split_heads(two):
        none = jnp.zeros_like(two)
        return jnp.concatenate((jnp.where(low_lane, two, none), jnp.where(low_lane, none, two)), axis=0)

    def join_heads(stacked):
        return jnp.where(low_lane, stacked[0:OWN], stacked[OWN:])

    def attend(pair, carry):
        here = lanes(pair * 128, 128)
        q_two = split_heads(query[:, here])
        for part in quarters:
            masked = dot_cols(q_two[part], keys[:, here]) + probs[pair, part, :]
            terms = jnp.exp(masked - jnp.max(masked, axis=-1, keepdims=True))
            weights = terms * (1.0 / jnp.sum(terms, axis=-1, keepdims=True))
            probs[pair, part, :] = weights
            low_a[part, :] = weights.astype(BF16)
        att[0:OWN, here] = join_heads(dot(low_a[...], values[:, here])).astype(BF16)
        return carry

    lax.fori_loop(0, PAIRS, attend, 0)
    att_copy = exchange(att.at[pl.ds(0, OWN), :], att.at[pl.ds(OWN, OWN), :], SIBLING)
    g_copy.wait()
    gs_copy = exchange(g_all.at[pl.ds(0, OWN), :], g_all.at[pl.ds(OWN, OWN), :], SIBLING)
    middle, total, back = wide_f.at[0], wide_f.at[1], wide_f.at[2]
    total[...] = dot(att[0:OWN, :], w_out[...])

    def second_norm(part):
        here = x_all[part, :].astype(F32) + (total[part, :] + out_bias[...].reshape(1, WIDTH))
        middle[part, :] = here
        normed, _ = normalize(here)
        xn2[part, :] = (normed * gain2 + shift2).astype(BF16)

    for part in quarters[0:2]:
        second_norm(part)
    xn2_copy = exchange(xn2.at[pl.ds(0, OWN), :], xn2.at[pl.ds(OWN, OWN), :], SIBLING)
    loaded(2)

    def feed(first, act_to, gh_to):
        for third in range(3):
            here = lanes(first + third * 256, 256)
            there = slice(third * 256, (third + 1) * 256)
            value = dot(xn2[0:OWN, :], w_up[:, here]) + up_bias[here].reshape(1, 256)
            grad = dot_cols(g_all[0:OWN, :], w_down[rows(first + third * 256, 256), :])
            below = 0.5 * (1.0 + lax.erf(value * math.sqrt(0.5)))
            slope = below + value * (jnp.exp(-0.5 * value * value) * (1.0 / math.sqrt(2.0 * math.pi)))
            act_to[:, there] = (value * below).astype(BF16)
            grad_hidden = (grad * slope).astype(BF16)
            gh_to[:, there] = grad_hidden
            small[pl.ds(8 + lax.div(first, WIDTH), 1), there] = jnp.sum(grad_hidden.astype(F32), axis=0, keepdims=True)

    def gather(number, first, act_from, gh_from):
        forward = dot(act_from[...], w_down[rows(first, WIDTH), :])
        backward = dot_cols(gh_from[...], w_up[:, lanes(first, WIDTH)])
        if number:
            total[...] += forward
            back[...] += backward
        else:
            total[...] = forward
            back[...] = backward

    def contract(index, first, left, right, width):
        def body(i, carry):
            here = lanes(i * 256, 256)
            mine[index, rows(i * 256, 256), first : first + width] = dot_rows(left[:, here], right[...]).astype(BF16)
            return carry

        lax.fori_loop(0, SIDE // 256, body, 0)

    tasks = {
        name: chunk_task(
            [STEPS[step] for step in ROUTES[k]], outer, mine.at[k // 2, :, pl.ds(k % 2 * HALF, HALF)], inbox.at[k],
            sems.at[k], landing(k, side, o_up, o_down, o_qkv, o_out),
        )
        for k, name in enumerate(NAMES)
    }
    tasks["s"] = small_task(inner + outer, small, small_in, small_sems)
    plan = iter(PLAN)

    def pump():
        for names in next(plan):
            for name in names:
                next(tasks[name], None)

    def feed_half(half):
        given = (1 - side) * (2 * WIDTH) + half * WIDTH
        kept = side * (2 * WIDTH) + half * WIDTH
        own_act, own_gh = act.at[half, pl.ds(0, OWN), :], gh.at[half, pl.ds(0, OWN), :]
        feed(given, act_give.at[half], gh_give.at[half])
        act_copy = exchange(act_give.at[half], act.at[half, pl.ds(OWN, OWN), :], SIBLING)
        gh_copy = exchange(gh_give.at[half], gh.at[half, pl.ds(OWN, OWN), :], SIBLING)
        if half:
            pump()
        feed(kept, own_act, own_gh)
        if half:
            pump()
        else:
            gs_copy.wait()
            xn2_copy.wait()
        act_copy.wait()
        contract(2 * half, 0, act.at[half], g_all, WIDTH)
        pump()
        gh_copy.wait()
        contract(2 * half + 1, 0, xn2, gh.at[half], WIDTH)
        pump()
        gather(2 * half, given, act_give.at[half], gh_give.at[half])
        gather(2 * half + 1, kept, own_act, own_gh)

    feed_half(0)
    feed_half(1)

    def second_back(part):
        normed, inv_std = normalize(middle[part, :])
        total[part, :] = middle[part, :] + (total[part, :] + down_bias[...].reshape(1, WIDTH))
        grad = back[part, :]
        grad_out = g_all[part, :].astype(F32)
        grad_middle = grad_out + norm_back(grad, normed, inv_std, gain2)
        middle[part, :] = grad_middle
        low = grad_middle.astype(BF16)
        gb[part, :] = low
        return grad * normed, grad, grad_out, low.astype(F32)

    def sum_up(slots, work):
        for number, part in enumerate(quarters[0:2]):
            for slot, value in zip(slots, work(part)):
                value = jnp.sum(value, axis=0, keepdims=True)
                small[slot : slot + 1, :] = small[slot : slot + 1, :] + value if number else value

    sum_up((5, 6, 7, 4), second_back)
    out_give[...] = total[BLOCK:OWN, :].astype(BF16)
    out_copy = exchange(out_give, out_far, ALONG_Y)
    own_out = pltpu.make_async_copy(total.at[pl.ds(0, BLOCK), :], o_output.at[row], load_sems.at[19])
    own_out.start()
    gb_all[0:OWN, :] = gb[:, lanes(side * 384, 384)]
    gb_copy = exchange(gb.at[:, lanes((1 - side) * 384, 384)], gb_all.at[pl.ds(OWN, OWN), :], SIBLING)
    gatt[...] = dot_cols(gb[...], w_out[...]).astype(BF16)
    pump()

    def attend_back(pair):
        here = slice(pair * 128, pair * 128 + 128)
        q_two, grad_two = split_heads(query[:, here]), split_heads(gatt[:, here])
        for number, part in enumerate(quarters):
            weights = probs[pair, part, :]
            grad_probs = dot_cols(grad_two[part], values[:, here])
            inner_sum = jnp.sum(weights * grad_probs, axis=-1, keepdims=True)
            grad_scores = weights * (grad_probs - inner_sum)
            low_a[part, :] = weights.astype(BF16)
            low_b[part, :] = grad_scores.astype(BF16)
            for kind, key_rest, low in ((0, rest_x, low_c), (1, rest_y, low_d)):
                less = key_rest < own_lanes(kind, quarters[number % 2], BIN_PX - 1)
                low[part, :] = jnp.where(less, grad_scores, 0.0).astype(BF16)
        grad_scores = low_b[...]
        grad_query = join_heads(dot(grad_scores, keys[:, here])) * HEAD_DIM**-0.5
        gj[:, here] = grad_query.astype(BF16)
        grad_key = dot(q_two.T, grad_scores).T
        grad_value = dot(grad_two.T, low_a[...]).T
        total_k, total_v = key_f.at[0], key_f.at[1]
        give_k, give_v = wide_f.at[3], wide_f.at[4]
        total_k[:, here], give_k[:, here] = grad_key[0:OWN], grad_key[OWN:]
        total_v[:, here], give_v[:, here] = grad_value[0:OWN], grad_value[OWN:]
        shared.append(exchange(give_k.at[:, here], key_f.at[2, :, here], SIBLING))
        shared.append(exchange(give_v.at[:, here], key_f.at[3, :, here], SIBLING))

        every = dot(grad_scores, one_key[...])
        both = lax.broadcasted_iota(jnp.int32, (FULL, 128), 1) < BUCKETS
        less = jnp.where(both, dot(low_c[...], one_key[...]), dot(low_d[...], one_key[...]))
        by_key = every - less + pltpu.roll(less, 127, 1)
        upper = by_key.astype(BF16)
        lower = (by_key - upper.astype(F32)).astype(BF16)
        left_half = lax.broadcasted_iota(jnp.int32, (BUCKETS, 128), 1) < BUCKETS
        spot = lax.broadcasted_iota(jnp.int32, (1, 128), 1)
        for odd in range(2):
            mine_part = slice(odd * OWN, (odd + 1) * OWN)
            table = dot(one_query[...], upper[mine_part]) + dot(one_query[...], lower[mine_part])
            found = []
            for part in (table[0:BUCKETS], pltpu.roll(table[BUCKETS:], BUCKETS, 1)):
                skewed = pltpu.roll(jnp.where(left_half, part, 0.0), 0, 1, stride=1, stride_axis=0)
                line_sum = jnp.sum(skewed, axis=0, keepdims=True)
                below = jnp.sum(jnp.where(spot <= 32, line_sum, 0.0), axis=-1, keepdims=True)
                above = jnp.sum(jnp.where(spot >= 95, line_sum, 0.0), axis=-1, keepdims=True)
                inside = pltpu.roll(line_sum, 96, 1)
                found.append(jnp.where(spot == 0, below, jnp.where(spot == BUCKETS - 1, above, inside)))
            merged = jnp.where(spot < BUCKETS, found[0], pltpu.roll(found[1], BUCKETS, 1))
            at = 12 + 2 * pair + odd
            small[at : at + 1, :] = jnp.concatenate((merged, jnp.zeros((1, WIDTH - 128), F32)), axis=1)

    shared = []
    for pair in range(PAIRS):
        attend_back(pair)
        if pair == 0:
            att_copy.wait()
            gb_copy.wait()
            contract(5, HALF, att, gb_all, HALF)
        pump()
    xn1_copy.wait()
    for copy in shared:
        copy.wait()

    def join_kv(part):
        low_k = (key_f[0, part, :] + key_f[2, part, :]).astype(BF16)
        low_v = (key_f[1, part, :] + key_f[3, part, :]).astype(BF16)
        gj[part, WIDTH : 2 * WIDTH] = low_k
        gj[part, 2 * WIDTH :] = low_v
        return gj[part, 0:WIDTH].astype(F32), low_v.astype(F32)

    sum_up((2, 3), join_kv)
    gj_copy = exchange(gj.at[:, lanes((1 - side) * 1152, 1152)], gj_all.at[pl.ds(OWN, OWN), :], SIBLING)
    gj_all[0:OWN, :] = gj[:, lanes(side * 1152, 1152)]
    back[...] = (
        dot_cols(gj[:, 0:WIDTH], w_qkv[:, 0:WIDTH])
        + dot_cols(gj[:, WIDTH : 2 * WIDTH], w_qkv[:, WIDTH : 2 * WIDTH])
        + dot_cols(gj[:, 2 * WIDTH :], w_qkv[:, 2 * WIDTH :])
    )
    gj_copy.wait()
    pump()
    contract(4, 0, xn1, gj_all.at[:, pl.ds(0, WIDTH)], WIDTH)
    pump()
    contract(5, 0, xn1, gj_all.at[:, pl.ds(WIDTH, HALF)], HALF)
    pump()

    def first_back(part):
        normed, inv_std = normalize(x_all[part, :].astype(F32))
        grad = back[part, :]
        middle[part, :] = middle[part, :] + norm_back(grad, normed, inv_std, gain1)
        return grad * normed, grad

    sum_up((0, 1), first_back)
    in_give[...] = middle[BLOCK:OWN, :].astype(BF16)
    in_copy = exchange(in_give, in_far, ALONG_Y)
    own_in = pltpu.make_async_copy(middle.at[pl.ds(0, BLOCK), :], o_inputs.at[row], load_sems.at[20])
    own_in.start()

    pump()
    out_copy.wait()
    own_out.wait()
    in_copy.wait()
    own_in.wait()
    total[0:BLOCK, :] = out_far[...].astype(F32)
    middle[0:BLOCK, :] = in_far[...].astype(F32)
    last = (
        pltpu.make_async_copy(total.at[pl.ds(0, BLOCK), :], o_output.at[other], load_sems.at[19]),
        pltpu.make_async_copy(middle.at[pl.ds(0, BLOCK), :], o_inputs.at[other], load_sems.at[20]),
        pltpu.make_async_copy(small, o_small, load_sems.at[21]),
    )
    for copy in last:
        copy.start()
    for copy in last:
        copy.wait()


def per_device(
    inputs, ln1_gain, ln1_shift, w_qkv, q_bias, v_bias, w_out, out_bias, table_x, table_y, ln2_gain, ln2_shift,
    w_up, up_bias, w_down, down_bias, cotangent, page_ids, corners,
):
    outer = outer_steps(lax.axis_size("wide"))
    slots = 10 + len(outer)
    assert inputs.shape == (2, BLOCK, WIDTH) and lax.axis_size("blk") == 4 and lax.axis_size("wide") >= 8
    hbm = pl.BlockSpec(memory_space=pl.ANY)
    shape = jax.ShapeDtypeStruct
    args = (
        inputs, ln1_gain, ln1_shift, w_qkv, q_bias, v_bias, w_out, out_bias, table_x.T, table_y.T, ln2_gain, ln2_shift,
        w_up, up_bias, w_down, down_bias, cotangent, page_ids, corners,
    )
    output, grad_inputs, full_up, full_down, full_qkv, full_out, small = pl.pallas_call(
        functools.partial(layer_kernel, outer),
        out_shape=(
            shape(inputs.shape, F32), shape(inputs.shape, F32),
            shape(w_up.shape, BF16), shape(w_down.shape, BF16), shape(w_qkv.shape, BF16), shape(w_out.shape, BF16),
            shape((SMALL_ROWS, WIDTH), F32),
        ),
        in_specs=[hbm] * len(args),
        out_specs=(hbm,) * 7,
        scratch_shapes=[pltpu.VMEM((WIDTH,), F32)] * 8
        + [
            pltpu.VMEM((FF,), F32), pltpu.VMEM((HEADS, BUCKETS), F32), pltpu.VMEM((HEADS, BUCKETS), F32),
            pltpu.VMEM(page_ids.shape, jnp.int32), pltpu.VMEM(corners.shape, jnp.int32), pltpu.VMEM((SMALL_ROWS, WIDTH), F32),
            pltpu.VMEM(w_qkv.shape, BF16), pltpu.VMEM(w_out.shape, BF16),
            pltpu.VMEM(w_up.shape, BF16), pltpu.VMEM(w_down.shape, BF16),
            pltpu.VMEM((SQUARES, SIDE, SIDE), BF16),
            pltpu.VMEM((CHUNKS, SIDE - PIECE + PIECE * len(outer), HALF), BF16),
            pltpu.VMEM((5 + len(outer), SMALL_ROWS, WIDTH), F32),
            pltpu.VMEM((PAIRS, FULL, FULL), F32),
            pltpu.VMEM((FULL, FULL), BF16), pltpu.VMEM((FULL, FULL), BF16),
            pltpu.VMEM((FULL, FULL), BF16), pltpu.VMEM((FULL, FULL), BF16),
            pltpu.VMEM((5, OWN, WIDTH), F32), pltpu.VMEM((4, OWN, WIDTH), F32),
            pltpu.VMEM((OWN, WIDTH), BF16), pltpu.VMEM((FULL, WIDTH), BF16),
            pltpu.VMEM((FULL, WIDTH), BF16), pltpu.VMEM((FULL, WIDTH), BF16), pltpu.VMEM((FULL, WIDTH), BF16),
            pltpu.VMEM((OWN, WIDTH), BF16), pltpu.VMEM((FULL, WIDTH), BF16), pltpu.VMEM((FULL, WIDTH), BF16),
            pltpu.VMEM((2, FULL, WIDTH), BF16), pltpu.VMEM((2, FULL, WIDTH), BF16),
            pltpu.VMEM((2, OWN, WIDTH), BF16), pltpu.VMEM((2, OWN, WIDTH), BF16),
            pltpu.VMEM((OWN, WIDTH), BF16), pltpu.VMEM((FULL, 384), BF16), pltpu.VMEM((OWN, WIDTH), BF16),
            pltpu.VMEM((OWN, 3 * WIDTH), BF16), pltpu.VMEM((FULL, 1152), BF16),
            pltpu.VMEM((3, FULL, 128), jnp.int32), pltpu.VMEM((FULL, 256), BF16),
            pltpu.VMEM((FULL, 128), BF16), pltpu.VMEM((128, OWN), BF16), pltpu.VMEM((9, 16, 128), F32),
            pltpu.VMEM((BLOCK, WIDTH), BF16), pltpu.VMEM((BLOCK, WIDTH), BF16),
            pltpu.VMEM((BLOCK, WIDTH), BF16), pltpu.VMEM((BLOCK, WIDTH), BF16),
            pltpu.SemaphoreType.DMA((22,)),
            pltpu.SemaphoreType.DMA((32, 2)),
            pltpu.SemaphoreType.DMA((CHUNKS, slots, 2)),
            pltpu.SemaphoreType.DMA((5 + len(outer), 2)),
        ],
        compiler_params=pltpu.CompilerParams(
            collective_id=0, has_side_effects=True, vmem_limit_bytes=63 * MIB
        ),
        cost_estimate=pl.CostEstimate(flops=13 * 10**9, bytes_accessed=3 * 10**7, transcendentals=10**7),
    )(*args)
    ended = finish(full_up, full_down, full_qkv, full_out, output, grad_inputs, small)
    f_up, f_down, f_qkv, f_out, output, grad_inputs, grad_x, grad_y, f_upb = ended[:9]
    f_ln1g, f_ln1s, f_qb, f_vb, f_outb, f_ln2g, f_ln2s, f_downb = ended[9:]
    return (
        output, grad_inputs, f_ln1g, f_ln1s, f_qkv, f_qb, f_vb, f_out, f_outb, grad_x.T, grad_y.T, f_ln2g, f_ln2s,
        f_up, f_upb, f_down, f_downb,
    )


def finish_kernel(*refs):
    sources, passed, small_from = refs[:4], refs[4:6], refs[6]
    targets, kept, little = refs[7:11], refs[11:13], refs[13:24]
    rings_in, rings_out, outs = refs[24:27], refs[27:30], refs[30:41]
    held, small, sems_in, sems_out, sems_kept = refs[41:]
    small_copy = pltpu.make_async_copy(small_from, small, sems_kept.at[4])
    arrive = [pltpu.make_async_copy(passed[k], held.at[k], sems_kept.at[k]) for k in range(2)]
    leave = [pltpu.make_async_copy(held.at[k], kept[k], sems_kept.at[2 + k]) for k in range(2)]
    leave += [pltpu.make_async_copy(outs[k], little[k], sems_kept.at[5 + k]) for k in range(len(outs))]
    ring_of = (0, 1, 2, 1)
    pieces = []
    for k, source in enumerate(sources):
        tall = SLAB // source.shape[1]
        pieces += [(k, ring_of[k], pl.ds(first, tall)) for first in range(0, source.shape[0], tall)]

    def fetch(n):
        k, ring, part = pieces[n]
        return pltpu.make_async_copy(sources[k].at[part, :], rings_in[ring].at[n % SLOTS], sems_in.at[n])

    def store(n):
        k, ring, part = pieces[n]
        return pltpu.make_async_copy(rings_out[ring].at[n % SLOTS], targets[k].at[part, :], sems_out.at[n])

    small_copy.start()
    for n in range(SLOTS):
        fetch(n).start()
    for copy in arrive:
        copy.start()
    small_copy.wait()
    outs[0][...] = small[12:SMALL_ROWS, 0:BUCKETS]
    outs[1][...] = small[12:SMALL_ROWS, BUCKETS : 2 * BUCKETS]
    for part in range(FF // WIDTH):
        outs[2][part * WIDTH : (part + 1) * WIDTH] = small[8 + part, :]
    for slot in range(8):
        outs[3 + slot][...] = small[slot, :]
    for copy in leave[2:]:
        copy.start()
    for n in range(len(pieces)):
        if n == SLOTS:
            for k in range(2):
                arrive[k].wait()
                leave[k].start()
        fetch(n).wait()
        if n >= SLOTS:
            store(n - SLOTS).wait()
        ring = pieces[n][1]
        rings_out[ring][n % SLOTS] = rings_in[ring][n % SLOTS].astype(F32)
        store(n).start()
        if n + SLOTS < len(pieces):
            fetch(n + SLOTS).start()
    for n in range(len(pieces) - SLOTS, len(pieces)):
        store(n).wait()
    for copy in leave:
        copy.wait()


def finish(*arrays):
    hbm = pl.BlockSpec(memory_space=pl.ANY)
    little = [(HEADS, BUCKETS)] * 2 + [(FF,)] + [(WIDTH,)] * 8
    widths = [array.shape[1] for array in arrays[:3]]
    count = sum(array.size for array in arrays[:4]) // SLAB
    return pl.pallas_call(
        finish_kernel,
        out_shape=[jax.ShapeDtypeStruct(array.shape, F32) for array in arrays[:6]]
        + [jax.ShapeDtypeStruct(shape, F32) for shape in little],
        in_specs=[hbm] * 7,
        out_specs=[hbm] * (6 + len(little)),
        scratch_shapes=[pltpu.VMEM((SLOTS, SLAB // width, width), kind) for kind in (BF16, F32) for width in widths]
        + [pltpu.VMEM(shape, F32) for shape in little]
        + [pltpu.VMEM((2,) + arrays[4].shape, F32), pltpu.VMEM((SMALL_ROWS, WIDTH), F32)]
        + [pltpu.SemaphoreType.DMA((size,)) for size in (count, count, 5 + len(little))],
        compiler_params=pltpu.CompilerParams(vmem_limit_bytes=60 * MIB),
        cost_estimate=pl.CostEstimate(flops=10**7, bytes_accessed=45 * 10**6, transcendentals=0),
    )(*arrays)


def solution(mesh):
    tokens, row_of_blk = P("wide", "blk", None), P("wide", None)
    return jax.shard_map(
        per_device,
        mesh=mesh,
        in_specs=(tokens,) + (P(),) * 15 + (tokens, row_of_blk, P(None, "wide", None)),
        out_specs=(tokens, tokens) + (P(),) * 15,
        check_vma=False,
    )
```

```python
import functools
import math

import jax
import jax.numpy as jnp
from jax import lax
from jax.experimental import pallas as pl
from jax.experimental.pallas import tpu as pltpu
from jax.sharding import PartitionSpec as P

HEADS = 12
HEAD_DIM = 64
BUCKETS = 64
BIN_PX = 16
MASKED = -1e30
EPS = 1e-05
MESH = pl.DeviceIdType.MESH
MIB = 1024 * 1024
F32, BF16 = jnp.float32, jnp.bfloat16

BLOCK = 128
OWN = 2 * BLOCK
FULL = 2 * OWN
WIDTH = HEADS * HEAD_DIM
FF = 4 * WIDTH
PAIRS = HEADS // 2

SQUARES = 6
CHUNKS = 2 * SQUARES
SIDE = WIDTH
HALF = SIDE // 2
PIECE = SIDE // 16
SIBLING = ("blk", 1)
ALONG_Y, ALONG_X, NEAR_Z, FAR_Z = ("blk", 2), ("wide", 1), ("wide", 2), ("wide", 4)
STEPS = {"Y": ALONG_Y, "X": ALONG_X, "1": NEAR_Z, "2": FAR_Z}
NAMES = "abcdefghijkl"
ROUTES = ("XY21", "12YX", "YX21", "12YX", "YX12", "XY21", "X12Y", "YX12", "XY21", "XY12", "YX12", "YX12")
PLAN = (
    ("ab",), ("cd",), ("",), ("",), ("ef",), ("ghab",), ("c",), ("dfe",), ("",), ("lbgh",), ("ca",), ("deg",),
    ("h",), ("cfea",), ("ijhgc",), ("kl",),
    ("sbfdasgechfaiekcfjhseglabdhifkljgcskailjefbdgshi", "kclcjias"),
    ("aklebejdfkifjhghbgiljkdblbilidkdjkj",),
)
SMALL_ROWS = 16

SLAB = 384 * WIDTH
SLOTS = 8


def outer_steps(wide):
    return tuple(("wide", 1 << level) for level in range(3, wide.bit_length() - 1))


def step_bit(step):
    axis, mask = step
    return lax.rem(lax.div(lax.axis_index(axis), mask), 2)


def step_target(step):
    axis, mask = step
    return {axis: lax.axis_index(axis) + mask * (1 - 2 * step_bit(step))}


def remote(source, target, sems, step):
    return pltpu.make_async_remote_copy(
        source, target, sems.at[0], sems.at[1], device_id=step_target(step), device_id_type=MESH
    )


def greet(steps):
    for step in steps:
        pl.semaphore_signal(
            pltpu.get_barrier_semaphore(), inc=1, device_id=step_target(step), device_id_type=MESH
        )


def lanes(first, size):
    return pl.ds(pl.multiple_of(first, 128), size)


def rows(first, size):
    return pl.ds(pl.multiple_of(first, 16), size)


def dot(left, right):
    return jnp.dot(left, right, preferred_element_type=F32)


def dot_cols(left, right):
    return lax.dot_general(left, right, (((1,), (1,)), ((), ())), preferred_element_type=F32)


def dot_rows(left, right):
    return lax.dot_general(left, right, (((0,), (0,)), ((), ())), preferred_element_type=F32)


def normalize(values):
    mean_val = jnp.mean(values, axis=-1, keepdims=True)
    centered = values - mean_val
    inv_std = lax.rsqrt(jnp.mean(centered * centered, axis=-1, keepdims=True) + EPS)
    return centered * inv_std, inv_std


def norm_back(grad, normed, inv_std, gain):
    scaled = grad * gain
    first_mean = jnp.mean(scaled, axis=-1, keepdims=True)
    second_mean = jnp.mean(scaled * normed, axis=-1, keepdims=True)
    return inv_std * (scaled - first_mean - normed * second_mean)


def add_rows(total, first, inbox, box, count):
    block = min(count, 4 * PIECE)

    def body(i, carry):
        here = rows(first + i * block, block)
        both = total[here, :].astype(F32) + inbox[rows(box + i * block, block), :].astype(F32)
        total[here, :] = both.astype(total.dtype)
        return carry

    lax.fori_loop(0, count // block, body, 0)


def chunk_task(route, outer, mine, inbox, sems, place):
    first, size, box = 0, SIDE, 0
    firsts = []
    free = iter(range(sems.shape[0]))
    for step in route:
        half = size // 2
        bit = step_bit(step)
        keep, give = first + bit * half, first + (1 - bit) * half
        copy = remote(mine.at[rows(give, half), :], inbox.at[pl.ds(box, half), :], sems.at[next(free)], step)
        copy.start()
        yield
        copy.wait()
        add_rows(mine, keep, inbox, box, half)
        firsts.append(first)
        first, size, box = keep, half, box + half
    for step in outer:
        copy = remote(mine.at[rows(first, size), :], inbox.at[pl.ds(box, size), :], sems.at[next(free)], step)
        copy.start()
        copy.wait()
        add_rows(mine, first, inbox, box, size)
        box += size
    kept = pltpu.make_async_copy(mine.at[rows(first, size), :], place(first, size), sems.at[next(free), 0])
    kept.start()
    copies = []
    for step, before in zip(reversed(route), reversed(firsts)):
        source = mine.at[rows(first, size), :] if size == PIECE else place(first, size)
        copies.append(remote(source, place(first, size), sems.at[next(free)], step))
        if size == SIDE // 2:
            copies.append(remote(source, source, sems.at[next(free)], SIBLING))
        for copy in copies:
            copy.start()
        yield
        copies.pop(0).wait()
        if size == PIECE:
            kept.wait()
        first, size, arrived = before, size * 2, before + size - (first - before)
    late = place(arrived, SIDE // 2)
    copies.append(remote(late, late, sems.at[next(free)], SIBLING))
    copies[1].start()
    yield
    for copy in copies:
        copy.wait()


def small_task(steps, total, inbox, sems):
    for slot, step in enumerate(steps):
        copy = remote(total, inbox.at[slot], sems.at[slot], step)
        copy.start()
        yield
        copy.wait()
        total[...] += inbox[slot]


def landing(index, side, o_up, o_down, o_qkv, o_out):
    square, right = divmod(index, 2)
    if square in (0, 2):
        start = side * (2 * SIDE) + square // 2 * SIDE
        return lambda first, size: o_down.at[rows(start + first, size), pl.ds(right * HALF, HALF)]
    if square in (1, 3):
        array, start = o_up, side * (2 * SIDE) + square // 2 * SIDE + right * HALF
    elif index < CHUNKS - 1:
        array, start = o_qkv, side * (3 * HALF) + (index - 8) * HALF
    else:
        array, start = o_out, side * HALF
    return lambda first, size: array.at[rows(first, size), lanes(start, HALF)]


def layer_kernel(
    outer,
    x_in, ln1_gain_in, ln1_shift_in, w_qkv_in, q_bias_in, v_bias_in, w_out_in, out_bias_in, table_x_in, table_y_in,
    ln2_gain_in, ln2_shift_in, w_up_in, up_bias_in, w_down_in, down_bias_in, cot_in, page_ids_in, corners_in,
    o_output, o_inputs, o_up, o_down, o_qkv, o_out, o_small,
    ln1_gain, ln1_shift, q_bias, v_bias, out_bias, ln2_gain, ln2_shift, down_bias, up_bias, table_x, table_y,
    page_ids, corners, small,
    w_qkv, w_out, w_up, w_down, mine, inbox, small_in,
    probs, low_a, low_b, low_c, low_d,
    wide_f, key_f, x_all, g_all, xn1, xn2, att, query, keys, values, act, gh, act_give, gh_give,
    gb, gb_all, gatt, gj, gj_all, col, key_twice, one_key, one_query, tables, out_give, out_far, in_give, in_far,
    load_sems, ex_sems, sems, small_sems,
):
    inner = (SIBLING, ALONG_Y, ALONG_X, NEAR_Z, FAR_Z)
    place = lax.axis_index("blk")
    side = step_bit(SIBLING)
    row = step_bit(ALONG_Y)
    other = 1 - row
    blocks = (place, place + 2 - 4 * row, place + 1 - 2 * side, place + 2 - 4 * row + 1 - 2 * side)
    low_lane = lax.broadcasted_iota(jnp.int32, (OWN, 128), 1) < HEAD_DIM
    exchanges = []

    def exchange(source, target, step):
        copy = remote(source, target, ex_sems.at[len(exchanges)], step)
        copy.start()
        exchanges.append(copy)
        return copy

    greet(inner + outer)
    pairs = (
        (corners_in, corners), (page_ids_in, page_ids), (table_x_in, table_x), (table_y_in, table_y),
        (x_in.at[row], x_all.at[pl.ds(0, BLOCK), :]),
        (ln1_gain_in, ln1_gain), (ln1_shift_in, ln1_shift), (v_bias_in, v_bias),
        (w_qkv_in, w_qkv),
        (q_bias_in, q_bias), (cot_in.at[row], g_all.at[pl.ds(0, BLOCK), :]), (out_bias_in, out_bias),
        (ln2_gain_in, ln2_gain), (ln2_shift_in, ln2_shift), (down_bias_in, down_bias), (up_bias_in, up_bias),
        (w_out_in, w_out), (w_up_in, w_up), (w_down_in, w_down),
    )
    loads = [pltpu.make_async_copy(source, held, load_sems.at[k]) for k, (source, held) in enumerate(pairs)]
    waited = iter(loads)

    def loaded(count):
        for _ in range(count):
            next(waited).wait()

    for copy in loads:
        copy.start()
    small[...] = jnp.zeros_like(small)
    loaded(4)

    def along(kind, block):
        here = lanes(block * BLOCK, BLOCK)
        source = page_ids[:, here] if kind == 2 else corners[kind, :, here]
        return jnp.broadcast_to(jnp.where(row == 0, source[0:1], source[1:2]), (BLOCK, BLOCK))

    for kind in range(3):
        for slot, block in enumerate(blocks):
            down = along(kind, block).astype(F32).T.astype(jnp.int32)
            col[kind, slot * BLOCK : (slot + 1) * BLOCK, :] = down
    lane = lax.broadcasted_iota(jnp.int32, (BLOCK, BLOCK), 1)
    line = lax.broadcasted_iota(jnp.int32, (BLOCK, BLOCK), 0)
    for slot, block in enumerate(blocks):
        part = slice(slot * BLOCK, (slot + 1) * BLOCK)
        bins_x = lax.shift_right_arithmetic(col[0, part, :], 4) + 1
        bins_y = lax.shift_right_arithmetic(col[1, part, :], 4) + 1 + BUCKETS
        one_key[part, :] = jnp.where(lane == jnp.where(lane < BUCKETS, bins_x, bins_y), 1.0, 0.0).astype(BF16)
        if slot < 2:
            turned_x = BUCKETS - 1 - lax.shift_right_arithmetic(along(0, block), 4)
            turned_y = 2 * BUCKETS - 1 - lax.shift_right_arithmetic(along(1, block), 4)
            one_query[:, part] = jnp.where(line == jnp.where(line < BUCKETS, turned_x, turned_y), 1.0, 0.0).astype(BF16)
    key_rows = [jnp.concatenate([along(kind, block)[0:1] for block in blocks], axis=1) for kind in range(3)]
    rest_x, rest_y = (jnp.bitwise_and(key_rows[kind], BIN_PX - 1) for kind in range(2))

    def own_lanes(kind, part, mask):
        return jnp.concatenate([jnp.bitwise_and(col[kind, part, :], mask)] * 4, axis=1)

    pl.semaphore_wait(pltpu.get_barrier_semaphore(), len(inner + outer))
    x_copy = exchange(x_in.at[other], x_all.at[pl.ds(BLOCK, BLOCK), :], ALONG_Y)

    at = lax.broadcasted_iota(jnp.int32, (16, 128), 1)
    at = jnp.where(at < BUCKETS, jnp.minimum(at, BUCKETS // 2 - 1), jnp.maximum(at - 128, -(BUCKETS // 2))) + BUCKETS // 2
    for kind, table in enumerate((table_x, table_y)):
        tables[0, 0:HEADS, kind * BUCKETS : (kind + 1) * BUCKETS] = table[...]
    for kind in range(2):
        distance = jnp.take_along_axis(tables[0], at + kind * BUCKETS, axis=1, mode="promise_in_bounds")
        for slot, value in ((1, distance), (3, pltpu.roll(distance, 1, 1) - distance)):
            upper = value.astype(BF16).astype(F32)
            tables[kind * 4 + slot] = upper
            tables[kind * 4 + slot + 1] = value - upper

    square_lane = lax.broadcasted_iota(jnp.int32, (128, 128), 1) < BUCKETS
    square_line = lax.broadcasted_iota(jnp.int32, (128, 128), 0) < BUCKETS
    diagonal = square_lane == square_line
    lane_x = jnp.bitwise_and(lax.broadcasted_iota(jnp.int32, (OWN, 256), 1), 127) < BUCKETS
    key_twice[...] = jnp.concatenate((one_key[...], one_key[...]), axis=1)

    def bias_pair(pair, carry):
        for odd in range(2):
            squares = []
            for slot in range(1, 5):
                both = [jnp.broadcast_to(tables[kind * 4 + slot, pl.ds(2 * pair + odd, 1), :], (BUCKETS, 128)) for kind in range(2)]
                moved = pltpu.roll(jnp.concatenate(both, axis=0), 0, 1, stride=1, stride_axis=0)
                squares.append(jnp.where(diagonal, moved, 0.0).astype(BF16))
            picked = dot(one_key[0:OWN, :], jnp.concatenate(squares, axis=1))
            plain, change = picked[:, 0:256].astype(BF16), picked[:, 256:512]
            change_x = jnp.where(lane_x, change, 0.0).astype(BF16)
            change_y = jnp.where(lane_x, 0.0, change).astype(BF16)
            terms = dot_cols(jnp.concatenate((plain, change_x, change_y), axis=0), key_twice[...])
            for number in range(2):
                part = quarters[number]
                bias = terms[part]
                bias += jnp.where(rest_x < own_lanes(0, part, BIN_PX - 1), terms[OWN : 2 * OWN][part], 0.0)
                bias += jnp.where(rest_y < own_lanes(1, part, BIN_PX - 1), terms[2 * OWN :][part], 0.0)
                same = key_rows[2] == own_lanes(2, part, 7)
                probs[pair, odd * OWN + number * BLOCK : odd * OWN + (number + 1) * BLOCK, :] = jnp.where(same, bias, MASKED)
        return carry

    quarters = [slice(k * BLOCK, (k + 1) * BLOCK) for k in range(4)]
    loaded(5)
    gain1, shift1 = ln1_gain[...].reshape(1, WIDTH), ln1_shift[...].reshape(1, WIDTH)
    shared = []

    def first_norm(part):
        normed, _ = normalize(x_all[part, :].astype(F32))
        xn1[part, :] = (normed * gain1 + shift1).astype(BF16)
        keys[part, :] = dot(xn1[part, :], w_qkv[:, WIDTH : 2 * WIDTH]).astype(BF16)
        values[part, :] = (dot(xn1[part, :], w_qkv[:, 2 * WIDTH :]) + v_bias[...].reshape(1, WIDTH)).astype(BF16)
        for held in (keys, values):
            shared.append(exchange(held.at[part, :], held.at[pl.ds(OWN + part.start, BLOCK), :], SIBLING))

    first_norm(quarters[0])
    lax.fori_loop(0, PAIRS - 1, bias_pair, 0)

    loaded(8)
    gain2, shift2 = ln2_gain[...].reshape(1, WIDTH), ln2_shift[...].reshape(1, WIDTH)
    x_copy.wait()
    g_copy = exchange(cot_in.at[other], g_all.at[pl.ds(BLOCK, BLOCK), :], ALONG_Y)
    first_norm(quarters[1])
    xn1_copy = exchange(xn1.at[pl.ds(0, OWN), :], xn1.at[pl.ds(OWN, OWN), :], SIBLING)
    joined = (dot(xn1[0:OWN, :], w_qkv[:, 0:WIDTH]) + q_bias[...].reshape(1, WIDTH)).astype(BF16)
    query[...] = joined * jnp.asarray(HEAD_DIM**-0.5, BF16)
    bias_pair(PAIRS - 1, 0)
    for copy in shared:
        copy.wait()

    def split_heads(two):
        none = jnp.zeros_like(two)
        return jnp.concatenate((jnp.where(low_lane, two, none), jnp.where(low_lane, none, two)), axis=0)

    def join_heads(stacked):
        return jnp.where(low_lane, stacked[0:OWN], stacked[OWN:])

    for pair in range(PAIRS):
        here = slice(pair * 128, pair * 128 + 128)
        q_two, low = split_heads(query[:, here]), (low_a, low_b)[pair % 2]
        for part in quarters:
            masked = dot_cols(q_two[part], keys[:, here]) + probs[pair, part, :]
            terms = jnp.exp(masked - jnp.max(masked, axis=-1, keepdims=True))
            weights = terms * (1.0 / jnp.sum(terms, axis=-1, keepdims=True))
            probs[pair, part, :] = weights
            low[part, :] = weights.astype(BF16)
        att[0:OWN, here] = join_heads(dot(low[...], values[:, here])).astype(BF16)

    att_copy = exchange(att.at[pl.ds(0, OWN), :], att.at[pl.ds(OWN, OWN), :], SIBLING)
    g_copy.wait()
    gs_copy = exchange(g_all.at[pl.ds(0, OWN), :], g_all.at[pl.ds(OWN, OWN), :], SIBLING)
    middle, total, back = wide_f.at[0], wide_f.at[1], wide_f.at[2]
    total[...] = dot(att[0:OWN, :], w_out[...])

    def second_norm(part):
        here = x_all[part, :].astype(F32) + (total[part, :] + out_bias[...].reshape(1, WIDTH))
        middle[part, :] = here
        normed, _ = normalize(here)
        xn2[part, :] = (normed * gain2 + shift2).astype(BF16)

    for part in quarters[0:2]:
        second_norm(part)
    xn2_copy = exchange(xn2.at[pl.ds(0, OWN), :], xn2.at[pl.ds(OWN, OWN), :], SIBLING)
    loaded(2)

    def feed(first, act_to, gh_to):
        for third in range(3):
            here = lanes(first + third * 256, 256)
            there = slice(third * 256, (third + 1) * 256)
            value = dot(xn2[0:OWN, :], w_up[:, here]) + up_bias[here].reshape(1, 256)
            grad = dot_cols(g_all[0:OWN, :], w_down[rows(first + third * 256, 256), :])
            below = 0.5 * (1.0 + lax.erf(value * math.sqrt(0.5)))
            slope = below + value * (jnp.exp(-0.5 * value * value) * (1.0 / math.sqrt(2.0 * math.pi)))
            act_to[:, there] = (value * below).astype(BF16)
            grad_hidden = (grad * slope).astype(BF16)
            gh_to[:, there] = grad_hidden
            small[pl.ds(8 + lax.div(first, WIDTH), 1), there] = jnp.sum(grad_hidden.astype(F32), axis=0, keepdims=True)

    def gather(number, first, act_from, gh_from):
        forward = dot(act_from[...], w_down[rows(first, WIDTH), :])
        backward = dot_cols(gh_from[...], w_up[:, lanes(first, WIDTH)])
        if number:
            total[...] += forward
            back[...] += backward
        else:
            total[...] = forward
            back[...] = backward

    def contract(index, first, left, right, width):
        def body(i, carry):
            here = lanes(i * 256, 256)
            mine[index, rows(i * 256, 256), first : first + width] = dot_rows(left[:, here], right[...]).astype(BF16)
            return carry

        lax.fori_loop(0, SIDE // 256, body, 0)

    tasks = {
        name: chunk_task(
            [STEPS[step] for step in ROUTES[k]], outer, mine.at[k // 2, :, pl.ds(k % 2 * HALF, HALF)], inbox.at[k],
            sems.at[k], landing(k, side, o_up, o_down, o_qkv, o_out),
        )
        for k, name in enumerate(NAMES)
    }
    tasks["s"] = small_task(inner + outer, small, small_in, small_sems)
    plan = iter(PLAN)

    def pump():
        for names in next(plan):
            for name in names:
                next(tasks[name], None)

    def feed_half(half):
        given = (1 - side) * (2 * WIDTH) + half * WIDTH
        kept = side * (2 * WIDTH) + half * WIDTH
        own_act, own_gh = act.at[half, pl.ds(0, OWN), :], gh.at[half, pl.ds(0, OWN), :]
        feed(given, act_give.at[half], gh_give.at[half])
        act_copy = exchange(act_give.at[half], act.at[half, pl.ds(OWN, OWN), :], SIBLING)
        gh_copy = exchange(gh_give.at[half], gh.at[half, pl.ds(OWN, OWN), :], SIBLING)
        if half:
            pump()
        feed(kept, own_act, own_gh)
        if half:
            pump()
        else:
            gs_copy.wait()
            xn2_copy.wait()
        act_copy.wait()
        contract(2 * half, 0, act.at[half], g_all, WIDTH)
        pump()
        gh_copy.wait()
        contract(2 * half + 1, 0, xn2, gh.at[half], WIDTH)
        pump()
        gather(2 * half, given, act_give.at[half], gh_give.at[half])
        gather(2 * half + 1, kept, own_act, own_gh)

    feed_half(0)
    feed_half(1)

    def second_back(part):
        normed, inv_std = normalize(middle[part, :])
        total[part, :] = middle[part, :] + (total[part, :] + down_bias[...].reshape(1, WIDTH))
        grad = back[part, :]
        grad_out = g_all[part, :].astype(F32)
        grad_middle = grad_out + norm_back(grad, normed, inv_std, gain2)
        middle[part, :] = grad_middle
        low = grad_middle.astype(BF16)
        gb[part, :] = low
        return grad * normed, grad, grad_out, low.astype(F32)

    def sum_up(slots, work):
        for number, part in enumerate(quarters[0:2]):
            for slot, value in zip(slots, work(part)):
                value = jnp.sum(value, axis=0, keepdims=True)
                small[slot : slot + 1, :] = small[slot : slot + 1, :] + value if number else value

    sum_up((5, 6, 7, 4), second_back)
    out_give[...] = total[BLOCK:OWN, :].astype(BF16)
    out_copy = exchange(out_give, out_far, ALONG_Y)
    own_out = pltpu.make_async_copy(total.at[pl.ds(0, BLOCK), :], o_output.at[row], load_sems.at[19])
    own_out.start()
    gb_all[0:OWN, :] = gb[:, lanes(side * 384, 384)]
    gb_copy = exchange(gb.at[:, lanes((1 - side) * 384, 384)], gb_all.at[pl.ds(OWN, OWN), :], SIBLING)
    gatt[...] = dot_cols(gb[...], w_out[...]).astype(BF16)
    pump()

    def attend_back(pair):
        here = slice(pair * 128, pair * 128 + 128)
        q_two, grad_two = split_heads(query[:, here]), split_heads(gatt[:, here])
        for number, part in enumerate(quarters):
            weights = probs[pair, part, :]
            grad_probs = dot_cols(grad_two[part], values[:, here])
            inner_sum = jnp.sum(weights * grad_probs, axis=-1, keepdims=True)
            grad_scores = weights * (grad_probs - inner_sum)
            low_a[part, :] = weights.astype(BF16)
            low_b[part, :] = grad_scores.astype(BF16)
            for kind, key_rest, low in ((0, rest_x, low_c), (1, rest_y, low_d)):
                less = key_rest < own_lanes(kind, quarters[number % 2], BIN_PX - 1)
                low[part, :] = jnp.where(less, grad_scores, 0.0).astype(BF16)
        grad_scores = low_b[...]
        grad_query = join_heads(dot(grad_scores, keys[:, here])) * HEAD_DIM**-0.5
        gj[:, here] = grad_query.astype(BF16)
        grad_key = dot(q_two.T, grad_scores).T
        grad_value = dot(grad_two.T, low_a[...]).T
        total_k, total_v = key_f.at[0], key_f.at[1]
        give_k, give_v = wide_f.at[3], wide_f.at[4]
        total_k[:, here], give_k[:, here] = grad_key[0:OWN], grad_key[OWN:]
        total_v[:, here], give_v[:, here] = grad_value[0:OWN], grad_value[OWN:]
        shared.append(exchange(give_k.at[:, here], key_f.at[2, :, here], SIBLING))
        shared.append(exchange(give_v.at[:, here], key_f.at[3, :, here], SIBLING))

        every = dot(grad_scores, one_key[...])
        both = lax.broadcasted_iota(jnp.int32, (FULL, 128), 1) < BUCKETS
        less = jnp.where(both, dot(low_c[...], one_key[...]), dot(low_d[...], one_key[...]))
        by_key = every - less + pltpu.roll(less, 127, 1)
        upper = by_key.astype(BF16)
        lower = (by_key - upper.astype(F32)).astype(BF16)
        left_half = lax.broadcasted_iota(jnp.int32, (BUCKETS, 128), 1) < BUCKETS
        spot = lax.broadcasted_iota(jnp.int32, (1, 128), 1)
        for odd in range(2):
            mine_part = slice(odd * OWN, (odd + 1) * OWN)
            table = dot(one_query[...], upper[mine_part]) + dot(one_query[...], lower[mine_part])
            found = []
            for part in (table[0:BUCKETS], pltpu.roll(table[BUCKETS:], BUCKETS, 1)):
                skewed = pltpu.roll(jnp.where(left_half, part, 0.0), 0, 1, stride=1, stride_axis=0)
                line_sum = jnp.sum(skewed, axis=0, keepdims=True)
                below = jnp.sum(jnp.where(spot <= 32, line_sum, 0.0), axis=-1, keepdims=True)
                above = jnp.sum(jnp.where(spot >= 95, line_sum, 0.0), axis=-1, keepdims=True)
                inside = pltpu.roll(line_sum, 96, 1)
                found.append(jnp.where(spot == 0, below, jnp.where(spot == BUCKETS - 1, above, inside)))
            merged = jnp.where(spot < BUCKETS, found[0], pltpu.roll(found[1], BUCKETS, 1))
            line, spot_in = table_spot(2 * pair + odd)
            small[line : line + 1, spot_in : spot_in + 128] = merged

    shared = []
    for pair in range(PAIRS):
        attend_back(pair)
        if pair == 0:
            att_copy.wait()
            gb_copy.wait()
            contract(5, HALF, att, gb_all, HALF)
        pump()
    xn1_copy.wait()
    for copy in shared:
        copy.wait()

    def join_kv(part):
        low_k = (key_f[0, part, :] + key_f[2, part, :]).astype(BF16)
        low_v = (key_f[1, part, :] + key_f[3, part, :]).astype(BF16)
        gj[part, WIDTH : 2 * WIDTH] = low_k
        gj[part, 2 * WIDTH :] = low_v
        return gj[part, 0:WIDTH].astype(F32), low_v.astype(F32)

    sum_up((2, 3), join_kv)
    gj_copy = exchange(gj.at[:, lanes((1 - side) * 1152, 1152)], gj_all.at[pl.ds(OWN, OWN), :], SIBLING)
    gj_all[0:OWN, :] = gj[:, lanes(side * 1152, 1152)]
    back[...] = (
        dot_cols(gj[:, 0:WIDTH], w_qkv[:, 0:WIDTH])
        + dot_cols(gj[:, WIDTH : 2 * WIDTH], w_qkv[:, WIDTH : 2 * WIDTH])
        + dot_cols(gj[:, 2 * WIDTH :], w_qkv[:, 2 * WIDTH :])
    )
    gj_copy.wait()
    pump()
    contract(4, 0, xn1, gj_all.at[:, pl.ds(0, WIDTH)], WIDTH)
    pump()
    contract(5, 0, xn1, gj_all.at[:, pl.ds(WIDTH, HALF)], HALF)
    pump()

    def first_back(part):
        normed, inv_std = normalize(x_all[part, :].astype(F32))
        grad = back[part, :]
        middle[part, :] = middle[part, :] + norm_back(grad, normed, inv_std, gain1)
        return grad * normed, grad

    sum_up((0, 1), first_back)
    in_give[...] = middle[BLOCK:OWN, :].astype(BF16)
    in_copy = exchange(in_give, in_far, ALONG_Y)
    own_in = pltpu.make_async_copy(middle.at[pl.ds(0, BLOCK), :], o_inputs.at[row], load_sems.at[20])
    own_in.start()

    pump()
    for copy in (out_copy, own_out, in_copy, own_in):
        copy.wait()
    total[0:BLOCK, :] = out_far[...].astype(F32)
    middle[0:BLOCK, :] = in_far[...].astype(F32)
    last = (
        pltpu.make_async_copy(total.at[pl.ds(0, BLOCK), :], o_output.at[other], load_sems.at[19]),
        pltpu.make_async_copy(middle.at[pl.ds(0, BLOCK), :], o_inputs.at[other], load_sems.at[20]),
        pltpu.make_async_copy(small, o_small, load_sems.at[21]),
    )
    for copy in last:
        copy.start()
    pump()
    for copy in last:
        copy.wait()


def per_device(
    inputs, ln1_gain, ln1_shift, w_qkv, q_bias, v_bias, w_out, out_bias, table_x, table_y, ln2_gain, ln2_shift,
    w_up, up_bias, w_down, down_bias, cotangent, page_ids, corners,
):
    outer = outer_steps(lax.axis_size("wide"))
    slots = 11 + len(outer)
    assert inputs.shape == (2, BLOCK, WIDTH) and lax.axis_size("blk") == 4 and lax.axis_size("wide") >= 8
    hbm = pl.BlockSpec(memory_space=pl.ANY)
    shape = jax.ShapeDtypeStruct
    args = (
        inputs, ln1_gain, ln1_shift, w_qkv, q_bias, v_bias, w_out, out_bias, table_x.T, table_y.T, ln2_gain, ln2_shift,
        w_up, up_bias, w_down, down_bias, cotangent, page_ids, corners,
    )
    output, grad_inputs, full_up, full_down, full_qkv, full_out, small = pl.pallas_call(
        functools.partial(layer_kernel, outer),
        out_shape=(
            shape(inputs.shape, F32), shape(inputs.shape, F32),
            shape(w_up.shape, BF16), shape(w_down.shape, BF16), shape(w_qkv.shape, BF16), shape(w_out.shape, BF16),
            shape((SMALL_ROWS, WIDTH), F32),
        ),
        in_specs=[hbm] * len(args),
        out_specs=(hbm,) * 7,
        scratch_shapes=[pltpu.VMEM((WIDTH,), F32)] * 8
        + [
            pltpu.VMEM((FF,), F32), pltpu.VMEM((HEADS, BUCKETS), F32), pltpu.VMEM((HEADS, BUCKETS), F32),
            pltpu.VMEM(page_ids.shape, jnp.int32), pltpu.VMEM(corners.shape, jnp.int32), pltpu.VMEM((SMALL_ROWS, WIDTH), F32),
            pltpu.VMEM(w_qkv.shape, BF16), pltpu.VMEM(w_out.shape, BF16),
            pltpu.VMEM(w_up.shape, BF16), pltpu.VMEM(w_down.shape, BF16),
            pltpu.VMEM((SQUARES, SIDE, SIDE), BF16),
            pltpu.VMEM((CHUNKS, SIDE - PIECE + PIECE * len(outer), HALF), BF16),
            pltpu.VMEM((5 + len(outer), SMALL_ROWS, WIDTH), F32),
            pltpu.VMEM((PAIRS, FULL, FULL), F32),
            pltpu.VMEM((FULL, FULL), BF16), pltpu.VMEM((FULL, FULL), BF16),
            pltpu.VMEM((FULL, FULL), BF16), pltpu.VMEM((FULL, FULL), BF16),
            pltpu.VMEM((5, OWN, WIDTH), F32), pltpu.VMEM((4, OWN, WIDTH), F32),
            pltpu.VMEM((OWN, WIDTH), BF16), pltpu.VMEM((FULL, WIDTH), BF16),
            pltpu.VMEM((FULL, WIDTH), BF16), pltpu.VMEM((FULL, WIDTH), BF16), pltpu.VMEM((FULL, WIDTH), BF16),
            pltpu.VMEM((OWN, WIDTH), BF16), pltpu.VMEM((FULL, WIDTH), BF16), pltpu.VMEM((FULL, WIDTH), BF16),
            pltpu.VMEM((2, FULL, WIDTH), BF16), pltpu.VMEM((2, FULL, WIDTH), BF16),
            pltpu.VMEM((2, OWN, WIDTH), BF16), pltpu.VMEM((2, OWN, WIDTH), BF16),
            pltpu.VMEM((OWN, WIDTH), BF16), pltpu.VMEM((FULL, 384), BF16), pltpu.VMEM((OWN, WIDTH), BF16),
            pltpu.VMEM((OWN, 3 * WIDTH), BF16), pltpu.VMEM((FULL, 1152), BF16),
            pltpu.VMEM((3, FULL, 128), jnp.int32), pltpu.VMEM((FULL, 256), BF16),
            pltpu.VMEM((FULL, 128), BF16), pltpu.VMEM((128, OWN), BF16), pltpu.VMEM((9, 16, 128), F32),
            pltpu.VMEM((BLOCK, WIDTH), BF16), pltpu.VMEM((BLOCK, WIDTH), BF16),
            pltpu.VMEM((BLOCK, WIDTH), BF16), pltpu.VMEM((BLOCK, WIDTH), BF16),
            pltpu.SemaphoreType.DMA((22,)),
            pltpu.SemaphoreType.DMA((32, 2)),
            pltpu.SemaphoreType.DMA((CHUNKS, slots, 2)),
            pltpu.SemaphoreType.DMA((5 + len(outer), 2)),
        ],
        compiler_params=pltpu.CompilerParams(
            collective_id=0, has_side_effects=True, vmem_limit_bytes=63 * MIB
        ),
        cost_estimate=pl.CostEstimate(flops=13 * 10**9, bytes_accessed=3 * 10**7, transcendentals=10**7),
    )(*args)
    ended = finish(full_up, full_down, full_qkv, full_out, output, grad_inputs, small)
    f_up, f_down, f_qkv, f_out, output, grad_inputs, grad_x, grad_y, f_upb = ended[:9]
    f_ln1g, f_ln1s, f_qb, f_vb, f_outb, f_ln2g, f_ln2s, f_downb = ended[9:]
    return (
        output, grad_inputs, f_ln1g, f_ln1s, f_qkv, f_qb, f_vb, f_out, f_outb, grad_x.T, grad_y.T, f_ln2g, f_ln2s,
        f_up, f_upb, f_down, f_downb,
    )


def table_spot(head):
    return 12 + head * 128 // WIDTH, head * 128 % WIDTH


def finish_kernel(*refs):
    sources, passed, small_from = refs[:4], refs[4:6], refs[6]
    targets, kept, little = refs[7:11], refs[11:13], refs[13:24]
    rings_in, rings_out, outs = refs[24:27], refs[27:30], refs[30:41]
    held, small, sems_in, sems_out, sems_kept = refs[41:]
    small_copy = pltpu.make_async_copy(small_from, small, sems_kept.at[4])
    arrive = [pltpu.make_async_copy(passed[k], held.at[k], sems_kept.at[k]) for k in range(2)]
    leave = [pltpu.make_async_copy(held.at[k], kept[k], sems_kept.at[2 + k]) for k in range(2)]
    leave += [pltpu.make_async_copy(outs[k], little[k], sems_kept.at[5 + k]) for k in range(len(outs))]
    ring_of = (0, 1, 2, 1)
    pieces = []
    for k, source in enumerate(sources):
        tall = SLAB // source.shape[1]
        pieces += [(k, ring_of[k], pl.ds(first, tall)) for first in range(0, source.shape[0], tall)]

    def fetch(n):
        k, ring, part = pieces[n]
        return pltpu.make_async_copy(sources[k].at[part, :], rings_in[ring].at[n % SLOTS], sems_in.at[n])

    def store(n):
        k, ring, part = pieces[n]
        return pltpu.make_async_copy(rings_out[ring].at[n % SLOTS], targets[k].at[part, :], sems_out.at[n])

    small_copy.start()
    for n in range(SLOTS):
        fetch(n).start()
    for copy in arrive:
        copy.start()
    small_copy.wait()
    for head in range(HEADS):
        line, first = table_spot(head)
        for kind in range(2):
            start = first + kind * BUCKETS
            outs[kind][head : head + 1, :] = small[line : line + 1, start : start + BUCKETS]
    for part in range(FF // WIDTH):
        outs[2][part * WIDTH : (part + 1) * WIDTH] = small[8 + part, :]
    for slot in range(8):
        outs[3 + slot][...] = small[slot, :]
    for copy in leave[2:]:
        copy.start()
    for n in range(len(pieces)):
        if n == SLOTS:
            for k in range(2):
                arrive[k].wait()
                leave[k].start()
        fetch(n).wait()
        if n >= SLOTS:
            store(n - SLOTS).wait()
        ring = pieces[n][1]
        rings_out[ring][n % SLOTS] = rings_in[ring][n % SLOTS].astype(F32)
        store(n).start()
        if n + SLOTS < len(pieces):
            fetch(n + SLOTS).start()
    for n in range(len(pieces) - SLOTS, len(pieces)):
        store(n).wait()
    for copy in leave:
        copy.wait()


def finish(*arrays):
    hbm = pl.BlockSpec(memory_space=pl.ANY)
    little = [(HEADS, BUCKETS)] * 2 + [(FF,)] + [(WIDTH,)] * 8
    widths = [array.shape[1] for array in arrays[:3]]
    count = sum(array.size for array in arrays[:4]) // SLAB
    return pl.pallas_call(
        finish_kernel,
        out_shape=[jax.ShapeDtypeStruct(array.shape, F32) for array in arrays[:6]]
        + [jax.ShapeDtypeStruct(shape, F32) for shape in little],
        in_specs=[hbm] * 7,
        out_specs=[hbm] * (6 + len(little)),
        scratch_shapes=[pltpu.VMEM((SLOTS, SLAB // width, width), kind) for kind in (BF16, F32) for width in widths]
        + [pltpu.VMEM(shape, F32) for shape in little]
        + [pltpu.VMEM((2,) + arrays[4].shape, F32), pltpu.VMEM((SMALL_ROWS, WIDTH), F32)]
        + [pltpu.SemaphoreType.DMA((size,)) for size in (count, count, 5 + len(little))],
        compiler_params=pltpu.CompilerParams(vmem_limit_bytes=60 * MIB),
        cost_estimate=pl.CostEstimate(flops=10**7, bytes_accessed=45 * 10**6, transcendentals=0),
    )(*arrays)


def solution(mesh):
    tokens, row_of_blk = P("wide", "blk", None), P("wide", None)
    return jax.shard_map(
        per_device,
        mesh=mesh,
        in_specs=(tokens,) + (P(),) * 15 + (tokens, row_of_blk, P(None, "wide", None)),
        out_specs=(tokens, tokens) + (P(),) * 15,
        check_vma=False,
    )
```

```python
import functools
import math

import jax
import jax.numpy as jnp
from jax import lax
from jax.experimental import pallas as pl
from jax.experimental.pallas import tpu as pltpu
from jax.sharding import PartitionSpec as P

HEADS = 12
HEAD_DIM = 64
BUCKETS = 64
BIN_PX = 16
MASKED = -1e30
EPS = 1e-05
MESH = pl.DeviceIdType.MESH
MIB = 1024 * 1024
F32, BF16 = jnp.float32, jnp.bfloat16

BLOCK = 128
OWN = 2 * BLOCK
FULL = 2 * OWN
WIDTH = HEADS * HEAD_DIM
FF = 4 * WIDTH
PAIRS = HEADS // 2

SQUARES = 6
CHUNKS = 2 * SQUARES
SIDE = WIDTH
HALF = SIDE // 2
PIECE = SIDE // 16
SIBLING = ("blk", 1)
ALONG_Y, ALONG_X, NEAR_Z, FAR_Z = ("blk", 2), ("wide", 1), ("wide", 2), ("wide", 4)
STEPS = {"Y": ALONG_Y, "X": ALONG_X, "1": NEAR_Z, "2": FAR_Z}
NAMES = "abcdefghijkl"
ROUTES = ("XY12", "Y1X2", "XY12", "YX12", "1XY2", "XY12", "X1Y2", "21YX", "Y1X2", "XY21", "XY12", "YX12")
PLAN = (
    ("ba",), ("",), ("",), ("",), ("ecd",), ("agfh",), ("b",), ("",), ("",), ("cdlag",),
    ("",), ("ca",), ("hfbecd",), ("blgaf",), ("ejhcblif",), ("cklbechjdfalicgklaj",),
    ("figkhdlfjasebihjkgsldcfgdekshgbikjslkhi",),
    ("ejafdkgbifcesijklehadghs",),
    ("ijdebkij",),
)
SMALL_ROWS = 16

SLAB = 384 * WIDTH
SLOTS = 8


def outer_steps(wide):
    return tuple(("wide", 1 << level) for level in range(3, wide.bit_length() - 1))


def step_bit(step):
    axis, mask = step
    return lax.rem(lax.div(lax.axis_index(axis), mask), 2)


def step_target(step):
    axis, mask = step
    return {axis: lax.axis_index(axis) + mask * (1 - 2 * step_bit(step))}


def remote(source, target, sems, step):
    return pltpu.make_async_remote_copy(
        source, target, sems.at[0], sems.at[1], device_id=step_target(step), device_id_type=MESH
    )


def greet(steps):
    for step in steps:
        pl.semaphore_signal(
            pltpu.get_barrier_semaphore(), inc=1, device_id=step_target(step), device_id_type=MESH
        )


def lanes(first, size):
    return pl.ds(pl.multiple_of(first, 128), size)


def rows(first, size):
    return pl.ds(pl.multiple_of(first, 16), size)


def dot(left, right):
    return jnp.dot(left, right, preferred_element_type=F32)


def dot_cols(left, right):
    return lax.dot_general(left, right, (((1,), (1,)), ((), ())), preferred_element_type=F32)


def dot_rows(left, right):
    return lax.dot_general(left, right, (((0,), (0,)), ((), ())), preferred_element_type=F32)


def normalize(values):
    mean_val = jnp.mean(values, axis=-1, keepdims=True)
    centered = values - mean_val
    inv_std = lax.rsqrt(jnp.mean(centered * centered, axis=-1, keepdims=True) + EPS)
    return centered * inv_std, inv_std


def norm_back(grad, normed, inv_std, gain):
    scaled = grad * gain
    first_mean = jnp.mean(scaled, axis=-1, keepdims=True)
    second_mean = jnp.mean(scaled * normed, axis=-1, keepdims=True)
    return inv_std * (scaled - first_mean - normed * second_mean)


def add_rows(total, first, inbox, box, count):
    block = min(count, 4 * PIECE)

    def body(i, carry):
        here = rows(first + i * block, block)
        both = total[here, :].astype(F32) + inbox[rows(box + i * block, block), :].astype(F32)
        total[here, :] = both.astype(total.dtype)
        return carry

    lax.fori_loop(0, count // block, body, 0)


def chunk_task(route, outer, mine, inbox, sems, place):
    first, size, box = 0, SIDE, 0
    firsts = []
    free = iter(range(sems.shape[0]))
    for step in route:
        half = size // 2
        bit = step_bit(step)
        keep, give = first + bit * half, first + (1 - bit) * half
        copy = remote(mine.at[rows(give, half), :], inbox.at[pl.ds(box, half), :], sems.at[next(free)], step)
        copy.start()
        yield
        copy.wait()
        add_rows(mine, keep, inbox, box, half)
        firsts.append(first)
        first, size, box = keep, half, box + half
    for step in outer:
        copy = remote(mine.at[rows(first, size), :], inbox.at[pl.ds(box, size), :], sems.at[next(free)], step)
        copy.start()
        copy.wait()
        add_rows(mine, first, inbox, box, size)
        box += size
    kept = pltpu.make_async_copy(mine.at[rows(first, size), :], place(first, size), sems.at[next(free), 0])
    kept.start()
    copies = []
    for step, before in zip(reversed(route), reversed(firsts)):
        source = mine.at[rows(first, size), :] if size == PIECE else place(first, size)
        copies.append(remote(source, place(first, size), sems.at[next(free)], step))
        if size == SIDE // 2:
            copies.append(remote(source, source, sems.at[next(free)], SIBLING))
        for copy in copies:
            copy.start()
        yield
        copies.pop(0).wait()
        if size == PIECE:
            kept.wait()
        first, size, arrived = before, size * 2, before + size - (first - before)
    late = place(arrived, SIDE // 2)
    copies.append(remote(late, late, sems.at[next(free)], SIBLING))
    copies[1].start()
    yield
    for copy in copies:
        copy.wait()


def small_task(steps, total, inbox, sems):
    for slot, step in enumerate(steps):
        copy = remote(total, inbox.at[slot], sems.at[slot], step)
        copy.start()
        yield
        copy.wait()
        total[...] += inbox[slot]


def landing(index, side, o_up, o_down, o_qkv, o_out):
    square, right = divmod(index, 2)
    if square in (0, 2):
        start = side * (2 * SIDE) + square // 2 * SIDE
        return lambda first, size: o_down.at[rows(start + first, size), pl.ds(right * HALF, HALF)]
    if square in (1, 3):
        array, start = o_up, side * (2 * SIDE) + square // 2 * SIDE + right * HALF
    elif index < CHUNKS - 1:
        array, start = o_qkv, side * (3 * HALF) + (index - 8) * HALF
    else:
        array, start = o_out, side * HALF
    return lambda first, size: array.at[rows(first, size), lanes(start, HALF)]


def layer_kernel(
    outer,
    x_in, ln1_gain_in, ln1_shift_in, w_qkv_in, q_bias_in, v_bias_in, w_out_in, out_bias_in, table_x_in, table_y_in,
    ln2_gain_in, ln2_shift_in, w_up_in, up_bias_in, w_down_in, down_bias_in, cot_in, page_ids_in, corners_in,
    o_output, o_inputs, o_up, o_down, o_qkv, o_out, o_small,
    ln1_gain, ln1_shift, q_bias, v_bias, out_bias, ln2_gain, ln2_shift, down_bias, up_bias, table_x, table_y,
    page_ids, corners, small,
    w_qkv, w_out, w_up, w_down, mine, inbox, small_in,
    probs, low_a, low_b, low_c, low_d,
    wide_f, key_f, x_all, g_all, xn1, xn2, att, query, keys, values, act, gh, act_give, gh_give,
    gb, gb_all, gatt, gj, gj_all, col, key_twice, one_key, one_query, tables, out_give, out_far, in_give, in_far,
    load_sems, ex_sems, sems, small_sems,
):
    inner = (SIBLING, ALONG_Y, ALONG_X, NEAR_Z, FAR_Z)
    place = lax.axis_index("blk")
    side = step_bit(SIBLING)
    row = step_bit(ALONG_Y)
    other = 1 - row
    blocks = (place, place + 2 - 4 * row, place + 1 - 2 * side, place + 2 - 4 * row + 1 - 2 * side)
    low_lane = lax.broadcasted_iota(jnp.int32, (OWN, 128), 1) < HEAD_DIM
    exchanges = []

    def exchange(source, target, step):
        copy = remote(source, target, ex_sems.at[len(exchanges)], step)
        copy.start()
        exchanges.append(copy)
        return copy

    greet(inner + outer)
    pairs = (
        (corners_in, corners), (page_ids_in, page_ids), (table_x_in, table_x), (table_y_in, table_y),
        (x_in.at[row], x_all.at[pl.ds(0, BLOCK), :]),
        (ln1_gain_in, ln1_gain), (ln1_shift_in, ln1_shift), (v_bias_in, v_bias),
        (w_qkv_in, w_qkv),
        (q_bias_in, q_bias), (cot_in.at[row], g_all.at[pl.ds(0, BLOCK), :]), (out_bias_in, out_bias),
        (ln2_gain_in, ln2_gain), (ln2_shift_in, ln2_shift), (down_bias_in, down_bias), (up_bias_in, up_bias),
        (w_out_in, w_out), (w_up_in, w_up), (w_down_in, w_down),
    )
    loads = [pltpu.make_async_copy(source, held, load_sems.at[k]) for k, (source, held) in enumerate(pairs)]
    waited = iter(loads)

    def loaded(count):
        for _ in range(count):
            next(waited).wait()

    for copy in loads:
        copy.start()
    small[...] = jnp.zeros_like(small)
    loaded(4)

    def along(kind, block):
        here = lanes(block * BLOCK, BLOCK)
        source = page_ids[:, here] if kind == 2 else corners[kind, :, here]
        return jnp.broadcast_to(jnp.where(row == 0, source[0:1], source[1:2]), (BLOCK, BLOCK))

    for kind in range(3):
        for slot, block in enumerate(blocks):
            down = along(kind, block).astype(F32).T.astype(jnp.int32)
            col[kind, slot * BLOCK : (slot + 1) * BLOCK, :] = down
    lane = lax.broadcasted_iota(jnp.int32, (BLOCK, BLOCK), 1)
    line = lax.broadcasted_iota(jnp.int32, (BLOCK, BLOCK), 0)
    for slot, block in enumerate(blocks):
        part = slice(slot * BLOCK, (slot + 1) * BLOCK)
        bins_x = lax.shift_right_arithmetic(col[0, part, :], 4) + 1
        bins_y = lax.shift_right_arithmetic(col[1, part, :], 4) + 1 + BUCKETS
        one_key[part, :] = jnp.where(lane == jnp.where(lane < BUCKETS, bins_x, bins_y), 1.0, 0.0).astype(BF16)
        if slot < 2:
            turned_x = BUCKETS - 1 - lax.shift_right_arithmetic(along(0, block), 4)
            turned_y = 2 * BUCKETS - 1 - lax.shift_right_arithmetic(along(1, block), 4)
            one_query[:, part] = jnp.where(line == jnp.where(line < BUCKETS, turned_x, turned_y), 1.0, 0.0).astype(BF16)
    key_rows = [jnp.concatenate([along(kind, block)[0:1] for block in blocks], axis=1) for kind in range(3)]
    rest_x, rest_y = (jnp.bitwise_and(key_rows[kind], BIN_PX - 1) for kind in range(2))

    def own_lanes(kind, part, mask):
        return jnp.concatenate([jnp.bitwise_and(col[kind, part, :], mask)] * 4, axis=1)

    pl.semaphore_wait(pltpu.get_barrier_semaphore(), len(inner + outer))
    x_copy = exchange(x_in.at[other], x_all.at[pl.ds(BLOCK, BLOCK), :], ALONG_Y)

    at = lax.broadcasted_iota(jnp.int32, (16, 128), 1)
    at = jnp.where(at < BUCKETS, jnp.minimum(at, BUCKETS // 2 - 1), jnp.maximum(at - 128, -(BUCKETS // 2))) + BUCKETS // 2
    for kind, table in enumerate((table_x, table_y)):
        tables[0, 0:HEADS, kind * BUCKETS : (kind + 1) * BUCKETS] = table[...]
    for kind in range(2):
        distance = jnp.take_along_axis(tables[0], at + kind * BUCKETS, axis=1, mode="promise_in_bounds")
        for slot, value in ((1, distance), (3, pltpu.roll(distance, 1, 1) - distance)):
            upper = value.astype(BF16).astype(F32)
            tables[kind * 4 + slot] = upper
            tables[kind * 4 + slot + 1] = value - upper

    square_lane = lax.broadcasted_iota(jnp.int32, (128, 128), 1) < BUCKETS
    square_line = lax.broadcasted_iota(jnp.int32, (128, 128), 0) < BUCKETS
    diagonal = square_lane == square_line
    lane_x = jnp.bitwise_and(lax.broadcasted_iota(jnp.int32, (OWN, 256), 1), 127) < BUCKETS
    key_twice[...] = jnp.concatenate((one_key[...], one_key[...]), axis=1)

    def bias_pair(pair, carry):
        for odd in range(2):
            squares = []
            for slot in range(1, 5):
                both = [jnp.broadcast_to(tables[kind * 4 + slot, pl.ds(2 * pair + odd, 1), :], (BUCKETS, 128)) for kind in range(2)]
                moved = pltpu.roll(jnp.concatenate(both, axis=0), 0, 1, stride=1, stride_axis=0)
                squares.append(jnp.where(diagonal, moved, 0.0).astype(BF16))
            picked = dot(one_key[0:OWN, :], jnp.concatenate(squares, axis=1))
            plain, change = picked[:, 0:256].astype(BF16), picked[:, 256:512]
            change_x = jnp.where(lane_x, change, 0.0).astype(BF16)
            change_y = jnp.where(lane_x, 0.0, change).astype(BF16)
            terms = dot_cols(jnp.concatenate((plain, change_x, change_y), axis=0), key_twice[...])
            for number in range(2):
                part = quarters[number]
                bias = terms[part]
                bias += jnp.where(rest_x < own_lanes(0, part, BIN_PX - 1), terms[OWN : 2 * OWN][part], 0.0)
                bias += jnp.where(rest_y < own_lanes(1, part, BIN_PX - 1), terms[2 * OWN :][part], 0.0)
                same = key_rows[2] == own_lanes(2, part, 7)
                probs[pair, odd * OWN + number * BLOCK : odd * OWN + (number + 1) * BLOCK, :] = jnp.where(same, bias, MASKED)
        return carry

    quarters = [slice(k * BLOCK, (k + 1) * BLOCK) for k in range(4)]
    loaded(5)
    gain1, shift1 = ln1_gain[...].reshape(1, WIDTH), ln1_shift[...].reshape(1, WIDTH)
    shared = []

    def first_norm(part):
        normed, _ = normalize(x_all[part, :].astype(F32))
        xn1[part, :] = (normed * gain1 + shift1).astype(BF16)
        keys[part, :] = dot(xn1[part, :], w_qkv[:, WIDTH : 2 * WIDTH]).astype(BF16)
        values[part, :] = (dot(xn1[part, :], w_qkv[:, 2 * WIDTH :]) + v_bias[...].reshape(1, WIDTH)).astype(BF16)
        for held in (keys, values):
            shared.append(exchange(held.at[part, :], held.at[pl.ds(OWN + part.start, BLOCK), :], SIBLING))

    first_norm(quarters[0])
    lax.fori_loop(0, PAIRS - 1, bias_pair, 0)

    loaded(8)
    gain2, shift2 = ln2_gain[...].reshape(1, WIDTH), ln2_shift[...].reshape(1, WIDTH)
    x_copy.wait()
    g_copy = exchange(cot_in.at[other], g_all.at[pl.ds(BLOCK, BLOCK), :], ALONG_Y)
    first_norm(quarters[1])
    xn1_copy = exchange(xn1.at[pl.ds(0, OWN), :], xn1.at[pl.ds(OWN, OWN), :], SIBLING)
    joined = (dot(xn1[0:OWN, :], w_qkv[:, 0:WIDTH]) + q_bias[...].reshape(1, WIDTH)).astype(BF16)
    query[...] = joined * jnp.asarray(HEAD_DIM**-0.5, BF16)
    bias_pair(PAIRS - 1, 0)
    for copy in shared:
        copy.wait()

    def split_heads(two):
        none = jnp.zeros_like(two)
        return jnp.concatenate((jnp.where(low_lane, two, none), jnp.where(low_lane, none, two)), axis=0)

    def join_heads(stacked):
        return jnp.where(low_lane, stacked[0:OWN], stacked[OWN:])

    for pair in range(PAIRS):
        here = slice(pair * 128, pair * 128 + 128)
        q_two, low = split_heads(query[:, here]), (low_a, low_b)[pair % 2]
        for part in quarters:
            masked = dot_cols(q_two[part], keys[:, here]) + probs[pair, part, :]
            terms = jnp.exp(masked - jnp.max(masked, axis=-1, keepdims=True))
            weights = terms * (1.0 / jnp.sum(terms, axis=-1, keepdims=True))
            probs[pair, part, :] = weights
            low[part, :] = weights.astype(BF16)
        att[0:OWN, here] = join_heads(dot(low[...], values[:, here])).astype(BF16)

    att_copy = exchange(att.at[pl.ds(0, OWN), :], att.at[pl.ds(OWN, OWN), :], SIBLING)
    g_copy.wait()
    gs_copy = exchange(g_all.at[pl.ds(0, OWN), :], g_all.at[pl.ds(OWN, OWN), :], SIBLING)
    middle, total, back = wide_f.at[0], wide_f.at[1], wide_f.at[2]
    total[...] = dot(att[0:OWN, :], w_out[...])

    def second_norm(part):
        here = x_all[part, :].astype(F32) + (total[part, :] + out_bias[...].reshape(1, WIDTH))
        middle[part, :] = here
        normed, _ = normalize(here)
        xn2[part, :] = (normed * gain2 + shift2).astype(BF16)

    for part in quarters[0:2]:
        second_norm(part)
    xn2_copy = exchange(xn2.at[pl.ds(0, OWN), :], xn2.at[pl.ds(OWN, OWN), :], SIBLING)
    loaded(2)

    def feed(first, act_to, gh_to):
        for third in range(3):
            here = lanes(first + third * 256, 256)
            there = slice(third * 256, (third + 1) * 256)
            value = dot(xn2[0:OWN, :], w_up[:, here]) + up_bias[here].reshape(1, 256)
            grad = dot_cols(g_all[0:OWN, :], w_down[rows(first + third * 256, 256), :])
            below = 0.5 * (1.0 + lax.erf(value * math.sqrt(0.5)))
            slope = below + value * (jnp.exp(-0.5 * value * value) * (1.0 / math.sqrt(2.0 * math.pi)))
            act_to[:, there] = (value * below).astype(BF16)
            grad_hidden = (grad * slope).astype(BF16)
            gh_to[:, there] = grad_hidden
            small[pl.ds(8 + lax.div(first, WIDTH), 1), there] = jnp.sum(grad_hidden.astype(F32), axis=0, keepdims=True)

    def gather(number, first, act_from, gh_from):
        forward = dot(act_from[...], w_down[rows(first, WIDTH), :])
        backward = dot_cols(gh_from[...], w_up[:, lanes(first, WIDTH)])
        if number:
            total[...] += forward
            back[...] += backward
        else:
            total[...] = forward
            back[...] = backward

    def contract(index, first, left, right, width):
        def body(i, carry):
            here = lanes(i * 256, 256)
            mine[index, rows(i * 256, 256), first : first + width] = dot_rows(left[:, here], right[...]).astype(BF16)
            return carry

        lax.fori_loop(0, SIDE // 256, body, 0)

    tasks = {
        name: chunk_task(
            [STEPS[step] for step in ROUTES[k]], outer, mine.at[k // 2, :, pl.ds(k % 2 * HALF, HALF)], inbox.at[k],
            sems.at[k], landing(k, side, o_up, o_down, o_qkv, o_out),
        )
        for k, name in enumerate(NAMES)
    }
    tasks["s"] = small_task(inner + outer, small, small_in, small_sems)
    plan = iter(PLAN)

    def pump():
        for names in next(plan):
            for name in names:
                next(tasks[name], None)

    def feed_half(half):
        given = (1 - side) * (2 * WIDTH) + half * WIDTH
        kept = side * (2 * WIDTH) + half * WIDTH
        own_act, own_gh = act.at[half, pl.ds(0, OWN), :], gh.at[half, pl.ds(0, OWN), :]
        feed(given, act_give.at[half], gh_give.at[half])
        act_copy = exchange(act_give.at[half], act.at[half, pl.ds(OWN, OWN), :], SIBLING)
        gh_copy = exchange(gh_give.at[half], gh.at[half, pl.ds(OWN, OWN), :], SIBLING)
        if half:
            pump()
        feed(kept, own_act, own_gh)
        if half:
            pump()
        else:
            gs_copy.wait()
            xn2_copy.wait()
        act_copy.wait()
        contract(2 * half, 0, act.at[half], g_all, WIDTH)
        pump()
        gh_copy.wait()
        contract(2 * half + 1, 0, xn2, gh.at[half], WIDTH)
        pump()
        gather(2 * half, given, act_give.at[half], gh_give.at[half])
        gather(2 * half + 1, kept, own_act, own_gh)

    feed_half(0)
    feed_half(1)

    def second_back(part):
        normed, inv_std = normalize(middle[part, :])
        total[part, :] = middle[part, :] + (total[part, :] + down_bias[...].reshape(1, WIDTH))
        grad = back[part, :]
        grad_out = g_all[part, :].astype(F32)
        grad_middle = grad_out + norm_back(grad, normed, inv_std, gain2)
        middle[part, :] = grad_middle
        low = grad_middle.astype(BF16)
        gb[part, :] = low
        return grad * normed, grad, grad_out, low.astype(F32)

    def sum_up(slots, work):
        for number, part in enumerate(quarters[0:2]):
            for slot, value in zip(slots, work(part)):
                value = jnp.sum(value, axis=0, keepdims=True)
                small[slot : slot + 1, :] = small[slot : slot + 1, :] + value if number else value

    sum_up((5, 6, 7, 4), second_back)
    out_give[...] = total[BLOCK:OWN, :].astype(BF16)
    out_copy = exchange(out_give, out_far, ALONG_Y)
    own_out = pltpu.make_async_copy(total.at[pl.ds(0, BLOCK), :], o_output.at[row], load_sems.at[19])
    own_out.start()
    gb_all[0:OWN, :] = gb[:, lanes(side * 384, 384)]
    gb_copy = exchange(gb.at[:, lanes((1 - side) * 384, 384)], gb_all.at[pl.ds(OWN, OWN), :], SIBLING)
    gatt[...] = dot_cols(gb[...], w_out[...]).astype(BF16)
    pump()

    def attend_back(pair):
        here = slice(pair * 128, pair * 128 + 128)
        q_two, grad_two = split_heads(query[:, here]), split_heads(gatt[:, here])
        for number, part in enumerate(quarters):
            weights = probs[pair, part, :]
            grad_probs = dot_cols(grad_two[part], values[:, here])
            inner_sum = jnp.sum(weights * grad_probs, axis=-1, keepdims=True)
            grad_scores = weights * (grad_probs - inner_sum)
            low_a[part, :] = weights.astype(BF16)
            low_b[part, :] = grad_scores.astype(BF16)
            for kind, key_rest, low in ((0, rest_x, low_c), (1, rest_y, low_d)):
                less = key_rest < own_lanes(kind, quarters[number % 2], BIN_PX - 1)
                low[part, :] = jnp.where(less, grad_scores, 0.0).astype(BF16)
        grad_scores = low_b[...]
        grad_query = join_heads(dot(grad_scores, keys[:, here])) * HEAD_DIM**-0.5
        gj[:, here] = grad_query.astype(BF16)
        grad_key = dot(q_two.T, grad_scores).T
        grad_value = dot(grad_two.T, low_a[...]).T
        total_k, total_v = key_f.at[0], key_f.at[1]
        give_k, give_v = wide_f.at[3], wide_f.at[4]
        total_k[:, here], give_k[:, here] = grad_key[0:OWN], grad_key[OWN:]
        total_v[:, here], give_v[:, here] = grad_value[0:OWN], grad_value[OWN:]
        shared.append(exchange(give_k.at[:, here], key_f.at[2, :, here], SIBLING))
        shared.append(exchange(give_v.at[:, here], key_f.at[3, :, here], SIBLING))

        every = dot(grad_scores, one_key[...])
        both = lax.broadcasted_iota(jnp.int32, (FULL, 128), 1) < BUCKETS
        less = jnp.where(both, dot(low_c[...], one_key[...]), dot(low_d[...], one_key[...]))
        by_key = every - less + pltpu.roll(less, 127, 1)
        upper = by_key.astype(BF16)
        lower = (by_key - upper.astype(F32)).astype(BF16)
        left_half = lax.broadcasted_iota(jnp.int32, (BUCKETS, 128), 1) < BUCKETS
        spot = lax.broadcasted_iota(jnp.int32, (1, 128), 1)
        for odd in range(2):
            mine_part = slice(odd * OWN, (odd + 1) * OWN)
            table = dot(one_query[...], upper[mine_part]) + dot(one_query[...], lower[mine_part])
            found = []
            for part in (table[0:BUCKETS], pltpu.roll(table[BUCKETS:], BUCKETS, 1)):
                skewed = pltpu.roll(jnp.where(left_half, part, 0.0), 0, 1, stride=1, stride_axis=0)
                line_sum = jnp.sum(skewed, axis=0, keepdims=True)
                below = jnp.sum(jnp.where(spot <= 32, line_sum, 0.0), axis=-1, keepdims=True)
                above = jnp.sum(jnp.where(spot >= 95, line_sum, 0.0), axis=-1, keepdims=True)
                inside = pltpu.roll(line_sum, 96, 1)
                found.append(jnp.where(spot == 0, below, jnp.where(spot == BUCKETS - 1, above, inside)))
            merged = jnp.where(spot < BUCKETS, found[0], pltpu.roll(found[1], BUCKETS, 1))
            line, spot_in = table_spot(2 * pair + odd)
            small[line : line + 1, spot_in : spot_in + 128] = merged

    shared = []
    for pair in range(PAIRS):
        attend_back(pair)
        if pair == 0:
            att_copy.wait()
            gb_copy.wait()
            contract(5, HALF, att, gb_all, HALF)
        pump()
    xn1_copy.wait()
    for copy in shared:
        copy.wait()

    def join_kv(part):
        low_k = (key_f[0, part, :] + key_f[2, part, :]).astype(BF16)
        low_v = (key_f[1, part, :] + key_f[3, part, :]).astype(BF16)
        gj[part, WIDTH : 2 * WIDTH] = low_k
        gj[part, 2 * WIDTH :] = low_v
        return gj[part, 0:WIDTH].astype(F32), low_v.astype(F32)

    sum_up((2, 3), join_kv)
    gj_copy = exchange(gj.at[:, lanes((1 - side) * 1152, 1152)], gj_all.at[pl.ds(OWN, OWN), :], SIBLING)
    gj_all[0:OWN, :] = gj[:, lanes(side * 1152, 1152)]
    back[...] = (
        dot_cols(gj[:, 0:WIDTH], w_qkv[:, 0:WIDTH])
        + dot_cols(gj[:, WIDTH : 2 * WIDTH], w_qkv[:, WIDTH : 2 * WIDTH])
        + dot_cols(gj[:, 2 * WIDTH :], w_qkv[:, 2 * WIDTH :])
    )
    gj_copy.wait()
    pump()
    contract(4, 0, xn1, gj_all.at[:, pl.ds(0, WIDTH)], WIDTH)
    pump()
    contract(5, 0, xn1, gj_all.at[:, pl.ds(WIDTH, HALF)], HALF)
    pump()

    def first_back(part):
        normed, inv_std = normalize(x_all[part, :].astype(F32))
        grad = back[part, :]
        middle[part, :] = middle[part, :] + norm_back(grad, normed, inv_std, gain1)
        return grad * normed, grad

    sum_up((0, 1), first_back)
    in_give[...] = middle[BLOCK:OWN, :].astype(BF16)
    in_copy = exchange(in_give, in_far, ALONG_Y)
    own_in = pltpu.make_async_copy(middle.at[pl.ds(0, BLOCK), :], o_inputs.at[row], load_sems.at[20])
    own_in.start()

    pump()
    for copy in (out_copy, own_out, in_copy, own_in):
        copy.wait()
    total[0:BLOCK, :] = out_far[...].astype(F32)
    middle[0:BLOCK, :] = in_far[...].astype(F32)
    last = (
        pltpu.make_async_copy(total.at[pl.ds(0, BLOCK), :], o_output.at[other], load_sems.at[19]),
        pltpu.make_async_copy(middle.at[pl.ds(0, BLOCK), :], o_inputs.at[other], load_sems.at[20]),
        pltpu.make_async_copy(small, o_small, load_sems.at[21]),
    )
    for copy in last[:2]:
        copy.start()
    pump()
    last[2].start()
    pump()
    for copy in last:
        copy.wait()


def per_device(
    inputs, ln1_gain, ln1_shift, w_qkv, q_bias, v_bias, w_out, out_bias, table_x, table_y, ln2_gain, ln2_shift,
    w_up, up_bias, w_down, down_bias, cotangent, page_ids, corners,
):
    outer = outer_steps(lax.axis_size("wide"))
    slots = 11 + len(outer)
    assert inputs.shape == (2, BLOCK, WIDTH) and lax.axis_size("blk") == 4 and lax.axis_size("wide") >= 8
    hbm = pl.BlockSpec(memory_space=pl.ANY)
    shape = jax.ShapeDtypeStruct
    args = (
        inputs, ln1_gain, ln1_shift, w_qkv, q_bias, v_bias, w_out, out_bias, table_x.T, table_y.T, ln2_gain, ln2_shift,
        w_up, up_bias, w_down, down_bias, cotangent, page_ids, corners,
    )
    output, grad_inputs, full_up, full_down, full_qkv, full_out, small = pl.pallas_call(
        functools.partial(layer_kernel, outer),
        out_shape=(
            shape(inputs.shape, F32), shape(inputs.shape, F32),
            shape(w_up.shape, BF16), shape(w_down.shape, BF16), shape(w_qkv.shape, BF16), shape(w_out.shape, BF16),
            shape((SMALL_ROWS, WIDTH), F32),
        ),
        in_specs=[hbm] * len(args),
        out_specs=(hbm,) * 7,
        scratch_shapes=[pltpu.VMEM((WIDTH,), F32)] * 8
        + [
            pltpu.VMEM((FF,), F32), pltpu.VMEM((HEADS, BUCKETS), F32), pltpu.VMEM((HEADS, BUCKETS), F32),
            pltpu.VMEM(page_ids.shape, jnp.int32), pltpu.VMEM(corners.shape, jnp.int32), pltpu.VMEM((SMALL_ROWS, WIDTH), F32),
            pltpu.VMEM(w_qkv.shape, BF16), pltpu.VMEM(w_out.shape, BF16),
            pltpu.VMEM(w_up.shape, BF16), pltpu.VMEM(w_down.shape, BF16),
            pltpu.VMEM((SQUARES, SIDE, SIDE), BF16),
            pltpu.VMEM((CHUNKS, SIDE - PIECE + PIECE * len(outer), HALF), BF16),
            pltpu.VMEM((5 + len(outer), SMALL_ROWS, WIDTH), F32),
            pltpu.VMEM((PAIRS, FULL, FULL), F32),
            pltpu.VMEM((FULL, FULL), BF16), pltpu.VMEM((FULL, FULL), BF16),
            pltpu.VMEM((FULL, FULL), BF16), pltpu.VMEM((FULL, FULL), BF16),
            pltpu.VMEM((5, OWN, WIDTH), F32), pltpu.VMEM((4, OWN, WIDTH), F32),
            pltpu.VMEM((OWN, WIDTH), BF16), pltpu.VMEM((FULL, WIDTH), BF16),
            pltpu.VMEM((FULL, WIDTH), BF16), pltpu.VMEM((FULL, WIDTH), BF16), pltpu.VMEM((FULL, WIDTH), BF16),
            pltpu.VMEM((OWN, WIDTH), BF16), pltpu.VMEM((FULL, WIDTH), BF16), pltpu.VMEM((FULL, WIDTH), BF16),
            pltpu.VMEM((2, FULL, WIDTH), BF16), pltpu.VMEM((2, FULL, WIDTH), BF16),
            pltpu.VMEM((2, OWN, WIDTH), BF16), pltpu.VMEM((2, OWN, WIDTH), BF16),
            pltpu.VMEM((OWN, WIDTH), BF16), pltpu.VMEM((FULL, 384), BF16), pltpu.VMEM((OWN, WIDTH), BF16),
            pltpu.VMEM((OWN, 3 * WIDTH), BF16), pltpu.VMEM((FULL, 1152), BF16),
            pltpu.VMEM((3, FULL, 128), jnp.int32), pltpu.VMEM((FULL, 256), BF16),
            pltpu.VMEM((FULL, 128), BF16), pltpu.VMEM((128, OWN), BF16), pltpu.VMEM((9, 16, 128), F32),
            pltpu.VMEM((BLOCK, WIDTH), BF16), pltpu.VMEM((BLOCK, WIDTH), BF16),
            pltpu.VMEM((BLOCK, WIDTH), BF16), pltpu.VMEM((BLOCK, WIDTH), BF16),
            pltpu.SemaphoreType.DMA((22,)),
            pltpu.SemaphoreType.DMA((32, 2)),
            pltpu.SemaphoreType.DMA((CHUNKS, slots, 2)),
            pltpu.SemaphoreType.DMA((5 + len(outer), 2)),
        ],
        compiler_params=pltpu.CompilerParams(
            collective_id=0, has_side_effects=True, vmem_limit_bytes=63 * MIB
        ),
        cost_estimate=pl.CostEstimate(flops=13 * 10**9, bytes_accessed=3 * 10**7, transcendentals=10**7),
    )(*args)
    ended = finish(full_up, full_down, full_qkv, full_out, output, grad_inputs, small)
    f_up, f_down, f_qkv, f_out, output, grad_inputs, grad_x, grad_y, f_upb = ended[:9]
    f_ln1g, f_ln1s, f_qb, f_vb, f_outb, f_ln2g, f_ln2s, f_downb = ended[9:]
    return (
        output, grad_inputs, f_ln1g, f_ln1s, f_qkv, f_qb, f_vb, f_out, f_outb, grad_x.T, grad_y.T, f_ln2g, f_ln2s,
        f_up, f_upb, f_down, f_downb,
    )


def table_spot(head):
    return 12 + head * 128 // WIDTH, head * 128 % WIDTH


def finish_kernel(*refs):
    sources, passed, small_from = refs[:4], refs[4:6], refs[6]
    targets, kept, little = refs[7:11], refs[11:13], refs[13:24]
    rings_in, rings_out, outs = refs[24:27], refs[27:30], refs[30:41]
    held, small, sems_in, sems_out, sems_kept = refs[41:]
    small_copy = pltpu.make_async_copy(small_from, small, sems_kept.at[4])
    arrive = [pltpu.make_async_copy(passed[k], held.at[k], sems_kept.at[k]) for k in range(2)]
    leave = [pltpu.make_async_copy(held.at[k], kept[k], sems_kept.at[2 + k]) for k in range(2)]
    leave += [pltpu.make_async_copy(outs[k], little[k], sems_kept.at[5 + k]) for k in range(len(outs))]
    ring_of = (0, 1, 2, 1)
    pieces = []
    for k, source in enumerate(sources):
        tall = SLAB // source.shape[1]
        pieces += [(k, ring_of[k], pl.ds(first, tall)) for first in range(0, source.shape[0], tall)]

    def fetch(n):
        k, ring, part = pieces[n]
        return pltpu.make_async_copy(sources[k].at[part, :], rings_in[ring].at[n % SLOTS], sems_in.at[n])

    def store(n):
        k, ring, part = pieces[n]
        return pltpu.make_async_copy(rings_out[ring].at[n % SLOTS], targets[k].at[part, :], sems_out.at[n])

    small_copy.start()
    for n in range(SLOTS):
        fetch(n).start()
    for copy in arrive:
        copy.start()
    small_copy.wait()
    for head in range(HEADS):
        line, first = table_spot(head)
        for kind in range(2):
            start = first + kind * BUCKETS
            outs[kind][head : head + 1, :] = small[line : line + 1, start : start + BUCKETS]
    for part in range(FF // WIDTH):
        outs[2][part * WIDTH : (part + 1) * WIDTH] = small[8 + part, :]
    for slot in range(8):
        outs[3 + slot][...] = small[slot, :]
    for copy in leave[2:]:
        copy.start()
    for n in range(len(pieces)):
        if n == SLOTS:
            for k in range(2):
                arrive[k].wait()
                leave[k].start()
        fetch(n).wait()
        if n >= SLOTS:
            store(n - SLOTS).wait()
        ring = pieces[n][1]
        rings_out[ring][n % SLOTS] = rings_in[ring][n % SLOTS].astype(F32)
        store(n).start()
        if n + SLOTS < len(pieces):
            fetch(n + SLOTS).start()
    for n in range(len(pieces) - SLOTS, len(pieces)):
        store(n).wait()
    for copy in leave:
        copy.wait()


def finish(*arrays):
    hbm = pl.BlockSpec(memory_space=pl.ANY)
    little = [(HEADS, BUCKETS)] * 2 + [(FF,)] + [(WIDTH,)] * 8
    widths = [array.shape[1] for array in arrays[:3]]
    count = sum(array.size for array in arrays[:4]) // SLAB
    return pl.pallas_call(
        finish_kernel,
        out_shape=[jax.ShapeDtypeStruct(array.shape, F32) for array in arrays[:6]]
        + [jax.ShapeDtypeStruct(shape, F32) for shape in little],
        in_specs=[hbm] * 7,
        out_specs=[hbm] * (6 + len(little)),
        scratch_shapes=[pltpu.VMEM((SLOTS, SLAB // width, width), kind) for kind in (BF16, F32) for width in widths]
        + [pltpu.VMEM(shape, F32) for shape in little]
        + [pltpu.VMEM((2,) + arrays[4].shape, F32), pltpu.VMEM((SMALL_ROWS, WIDTH), F32)]
        + [pltpu.SemaphoreType.DMA((size,)) for size in (count, count, 5 + len(little))],
        compiler_params=pltpu.CompilerParams(vmem_limit_bytes=60 * MIB),
        cost_estimate=pl.CostEstimate(flops=10**7, bytes_accessed=45 * 10**6, transcendentals=0),
    )(*arrays)


def solution(mesh):
    tokens, row_of_blk = P("wide", "blk", None), P("wide", None)
    return jax.shard_map(
        per_device,
        mesh=mesh,
        in_specs=(tokens,) + (P(),) * 15 + (tokens, row_of_blk, P(None, "wide", None)),
        out_specs=(tokens, tokens) + (P(),) * 15,
        check_vma=False,
    )
```

```python
import functools
import math

import jax
import jax.numpy as jnp
from jax import lax
from jax.experimental import pallas as pl
from jax.experimental.pallas import tpu as pltpu
from jax.sharding import PartitionSpec as P

HEADS = 12
HEAD_DIM = 64
BUCKETS = 64
BIN_PX = 16
MASKED = -1e30
EPS = 1e-05
MESH = pl.DeviceIdType.MESH
MIB = 1024 * 1024
F32, BF16 = jnp.float32, jnp.bfloat16

BLOCK = 128
OWN = 2 * BLOCK
FULL = 2 * OWN
WIDTH = HEADS * HEAD_DIM
FF = 4 * WIDTH
PAIRS = HEADS // 2

SQUARES = 6
CHUNKS = 2 * SQUARES
SIDE = WIDTH
HALF = SIDE // 2
PIECE = SIDE // 16
SIBLING = ("blk", 1)
ALONG_Y, ALONG_X, NEAR_Z, FAR_Z = ("blk", 2), ("wide", 1), ("wide", 2), ("wide", 4)
STEPS = {"Y": ALONG_Y, "X": ALONG_X, "1": NEAR_Z, "2": FAR_Z}
NAMES = "abcdefghijkl"
ROUTES = ("YX21", "XY12", "XY12", "Y1X2", "2YX1", "XY12", "XY12", "12XY", "Y1X2", "XY12", "XY12", "YX12")
PLAN = (
    ("ab",), ("",), ("",), ("d",), ("ce",), ("ahb",), ("",), ("lgf",), ("acb",), ("hd",),
    ("bega",), ("",), ("dfcl",), ("ecabh",), ("jil",), ("ceaf",),
    ("cklgadcbfhjdelchbigksejafldsgibjkilgkfeghijfdksa", "c"),
    ("igjhlckafjibksdehjlkisbjfgdjghelkidefs",),
    ("khi",),
)
SMALL_ROWS = 16

SLAB = 384 * WIDTH
SLOTS = 10


def outer_steps(wide):
    return tuple(("wide", 1 << level) for level in range(3, wide.bit_length() - 1))


def step_bit(step):
    axis, mask = step
    return lax.rem(lax.div(lax.axis_index(axis), mask), 2)


def step_target(step):
    axis, mask = step
    return {axis: lax.axis_index(axis) + mask * (1 - 2 * step_bit(step))}


def remote(source, target, sems, step):
    return pltpu.make_async_remote_copy(
        source, target, sems.at[0], sems.at[1], device_id=step_target(step), device_id_type=MESH
    )


def greet(steps):
    for step in steps:
        pl.semaphore_signal(
            pltpu.get_barrier_semaphore(), inc=1, device_id=step_target(step), device_id_type=MESH
        )


def lanes(first, size):
    return pl.ds(pl.multiple_of(first, 128), size)


def rows(first, size):
    return pl.ds(pl.multiple_of(first, 16), size)


def dot(left, right):
    return jnp.dot(left, right, preferred_element_type=F32)


def dot_cols(left, right):
    return lax.dot_general(left, right, (((1,), (1,)), ((), ())), preferred_element_type=F32)


def dot_rows(left, right):
    return lax.dot_general(left, right, (((0,), (0,)), ((), ())), preferred_element_type=F32)


def normalize(values):
    mean_val = jnp.mean(values, axis=-1, keepdims=True)
    centered = values - mean_val
    inv_std = lax.rsqrt(jnp.mean(centered * centered, axis=-1, keepdims=True) + EPS)
    return centered * inv_std, inv_std


def norm_back(grad, normed, inv_std, gain):
    scaled = grad * gain
    first_mean = jnp.mean(scaled, axis=-1, keepdims=True)
    second_mean = jnp.mean(scaled * normed, axis=-1, keepdims=True)
    return inv_std * (scaled - first_mean - normed * second_mean)


def add_rows(total, first, inbox, box, count):
    block = min(count, 4 * PIECE)

    def body(i, carry):
        here = rows(first + i * block, block)
        both = total[here, :].astype(F32) + inbox[rows(box + i * block, block), :].astype(F32)
        total[here, :] = both.astype(total.dtype)
        return carry

    lax.fori_loop(0, count // block, body, 0)


def chunk_task(route, outer, mine, inbox, sems, place):
    first, size, box = 0, SIDE, 0
    firsts = []
    free = iter(range(sems.shape[0]))
    for step in route:
        half = size // 2
        bit = step_bit(step)
        keep, give = first + bit * half, first + (1 - bit) * half
        copy = remote(mine.at[rows(give, half), :], inbox.at[pl.ds(box, half), :], sems.at[next(free)], step)
        copy.start()
        yield
        copy.wait()
        add_rows(mine, keep, inbox, box, half)
        firsts.append(first)
        first, size, box = keep, half, box + half
    for step in outer:
        copy = remote(mine.at[rows(first, size), :], inbox.at[pl.ds(box, size), :], sems.at[next(free)], step)
        copy.start()
        copy.wait()
        add_rows(mine, first, inbox, box, size)
        box += size
    kept = pltpu.make_async_copy(mine.at[rows(first, size), :], place(first, size), sems.at[next(free), 0])
    kept.start()
    copies = []
    for step, before in zip(reversed(route), reversed(firsts)):
        source = mine.at[rows(first, size), :] if size == PIECE else place(first, size)
        copies.append(remote(source, place(first, size), sems.at[next(free)], step))
        if size == SIDE // 2:
            copies.append(remote(source, source, sems.at[next(free)], SIBLING))
        for copy in copies:
            copy.start()
        yield
        copies.pop(0).wait()
        if size == PIECE:
            kept.wait()
        first, size, arrived = before, size * 2, before + size - (first - before)
    late = place(arrived, SIDE // 2)
    copies.append(remote(late, late, sems.at[next(free)], SIBLING))
    copies[1].start()
    yield
    for copy in copies:
        copy.wait()


def small_task(steps, total, inbox, sems):
    for slot, step in enumerate(steps):
        copy = remote(total, inbox.at[slot], sems.at[slot], step)
        copy.start()
        yield
        copy.wait()
        total[...] += inbox[slot]


def landing(index, side, o_up, o_down, o_qkv, o_out):
    square, right = divmod(index, 2)
    if square in (0, 2):
        start = side * (2 * SIDE) + square // 2 * SIDE
        return lambda first, size: o_down.at[rows(start + first, size), pl.ds(right * HALF, HALF)]
    if square in (1, 3):
        array, start = o_up, side * (2 * SIDE) + square // 2 * SIDE + right * HALF
    elif index < CHUNKS - 1:
        array, start = o_qkv, side * (3 * HALF) + (index - 8) * HALF
    else:
        array, start = o_out, side * HALF
    return lambda first, size: array.at[rows(first, size), lanes(start, HALF)]


def layer_kernel(
    outer,
    x_in, ln1_gain_in, ln1_shift_in, w_qkv_in, q_bias_in, v_bias_in, w_out_in, out_bias_in, table_x_in, table_y_in,
    ln2_gain_in, ln2_shift_in, w_up_in, up_bias_in, w_down_in, down_bias_in, cot_in, page_ids_in, corners_in,
    o_output, o_inputs, o_up, o_down, o_qkv, o_out, o_small,
    ln1_gain, ln1_shift, q_bias, v_bias, out_bias, ln2_gain, ln2_shift, down_bias, up_bias, table_x, table_y,
    page_ids, corners, small,
    w_qkv, w_out, w_up, w_down, mine, inbox, small_in,
    probs, low_a, low_b, low_c, low_d,
    wide_f, key_f, x_all, g_all, xn1, xn2, att, query, keys, values, act, gh, act_give, gh_give,
    gb, gb_all, gatt, gj, gj_all, col, key_twice, one_key, one_query, tables, out_give, out_far, in_give, in_far,
    load_sems, ex_sems, sems, small_sems,
):
    inner = (SIBLING, ALONG_Y, ALONG_X, NEAR_Z, FAR_Z)
    place = lax.axis_index("blk")
    side = step_bit(SIBLING)
    row = step_bit(ALONG_Y)
    other = 1 - row
    blocks = (place, place + 2 - 4 * row, place + 1 - 2 * side, place + 2 - 4 * row + 1 - 2 * side)
    low_lane = lax.broadcasted_iota(jnp.int32, (OWN, 128), 1) < HEAD_DIM
    exchanges = []

    def exchange(source, target, step):
        copy = remote(source, target, ex_sems.at[len(exchanges)], step)
        copy.start()
        exchanges.append(copy)
        return copy

    greet(inner + outer)
    pairs = (
        (corners_in, corners), (page_ids_in, page_ids), (table_x_in, table_x), (table_y_in, table_y),
        (x_in.at[row], x_all.at[pl.ds(0, BLOCK), :]),
        (ln1_gain_in, ln1_gain), (ln1_shift_in, ln1_shift), (v_bias_in, v_bias),
        (w_qkv_in, w_qkv),
        (q_bias_in, q_bias), (cot_in.at[row], g_all.at[pl.ds(0, BLOCK), :]), (out_bias_in, out_bias),
        (ln2_gain_in, ln2_gain), (ln2_shift_in, ln2_shift), (down_bias_in, down_bias), (up_bias_in, up_bias),
        (w_out_in, w_out), (w_up_in, w_up), (w_down_in, w_down),
    )
    loads = [pltpu.make_async_copy(source, held, load_sems.at[k]) for k, (source, held) in enumerate(pairs)]
    waited = iter(loads)

    def loaded(count):
        for _ in range(count):
            next(waited).wait()

    for copy in loads:
        copy.start()
    small[...] = jnp.zeros_like(small)
    loaded(4)

    def along(kind, block):
        here = lanes(block * BLOCK, BLOCK)
        source = page_ids[:, here] if kind == 2 else corners[kind, :, here]
        return jnp.broadcast_to(jnp.where(row == 0, source[0:1], source[1:2]), (BLOCK, BLOCK))

    for kind in range(3):
        for slot, block in enumerate(blocks):
            down = along(kind, block).astype(F32).T.astype(jnp.int32)
            col[kind, slot * BLOCK : (slot + 1) * BLOCK, :] = down
    lane = lax.broadcasted_iota(jnp.int32, (BLOCK, BLOCK), 1)
    line = lax.broadcasted_iota(jnp.int32, (BLOCK, BLOCK), 0)
    for slot, block in enumerate(blocks):
        part = slice(slot * BLOCK, (slot + 1) * BLOCK)
        bins_x = lax.shift_right_arithmetic(col[0, part, :], 4) + 1
        bins_y = lax.shift_right_arithmetic(col[1, part, :], 4) + 1 + BUCKETS
        one_key[part, :] = jnp.where(lane == jnp.where(lane < BUCKETS, bins_x, bins_y), 1.0, 0.0).astype(BF16)
        if slot < 2:
            turned_x = BUCKETS - 1 - lax.shift_right_arithmetic(along(0, block), 4)
            turned_y = 2 * BUCKETS - 1 - lax.shift_right_arithmetic(along(1, block), 4)
            one_query[:, part] = jnp.where(line == jnp.where(line < BUCKETS, turned_x, turned_y), 1.0, 0.0).astype(BF16)
    key_rows = [jnp.concatenate([along(kind, block)[0:1] for block in blocks], axis=1) for kind in range(3)]
    rest_x, rest_y = (jnp.bitwise_and(key_rows[kind], BIN_PX - 1) for kind in range(2))

    def own_lanes(kind, part, mask):
        return jnp.concatenate([jnp.bitwise_and(col[kind, part, :], mask)] * 4, axis=1)

    pl.semaphore_wait(pltpu.get_barrier_semaphore(), len(inner + outer))
    x_copy = exchange(x_in.at[other], x_all.at[pl.ds(BLOCK, BLOCK), :], ALONG_Y)

    at = lax.broadcasted_iota(jnp.int32, (16, 128), 1)
    at = jnp.where(at < BUCKETS, jnp.minimum(at, BUCKETS // 2 - 1), jnp.maximum(at - 128, -(BUCKETS // 2))) + BUCKETS // 2
    for kind, table in enumerate((table_x, table_y)):
        tables[0, 0:HEADS, kind * BUCKETS : (kind + 1) * BUCKETS] = table[...]
    for kind in range(2):
        distance = jnp.take_along_axis(tables[0], at + kind * BUCKETS, axis=1, mode="promise_in_bounds")
        for slot, value in ((1, distance), (3, pltpu.roll(distance, 1, 1) - distance)):
            upper = value.astype(BF16).astype(F32)
            tables[kind * 4 + slot] = upper
            tables[kind * 4 + slot + 1] = value - upper

    square_lane = lax.broadcasted_iota(jnp.int32, (128, 128), 1) < BUCKETS
    square_line = lax.broadcasted_iota(jnp.int32, (128, 128), 0) < BUCKETS
    diagonal = square_lane == square_line
    lane_x = jnp.bitwise_and(lax.broadcasted_iota(jnp.int32, (OWN, 256), 1), 127) < BUCKETS
    key_twice[...] = jnp.concatenate((one_key[...], one_key[...]), axis=1)

    def bias_pair(pair, carry):
        for odd in range(2):
            squares = []
            for slot in range(1, 5):
                both = [jnp.broadcast_to(tables[kind * 4 + slot, pl.ds(2 * pair + odd, 1), :], (BUCKETS, 128)) for kind in range(2)]
                moved = pltpu.roll(jnp.concatenate(both, axis=0), 0, 1, stride=1, stride_axis=0)
                squares.append(jnp.where(diagonal, moved, 0.0).astype(BF16))
            picked = dot(one_key[0:OWN, :], jnp.concatenate(squares, axis=1))
            plain, change = picked[:, 0:256].astype(BF16), picked[:, 256:512]
            change_x = jnp.where(lane_x, change, 0.0).astype(BF16)
            change_y = jnp.where(lane_x, 0.0, change).astype(BF16)
            terms = dot_cols(jnp.concatenate((plain, change_x, change_y), axis=0), key_twice[...])
            for number in range(2):
                part = quarters[number]
                bias = terms[part]
                bias += jnp.where(rest_x < own_lanes(0, part, BIN_PX - 1), terms[OWN : 2 * OWN][part], 0.0)
                bias += jnp.where(rest_y < own_lanes(1, part, BIN_PX - 1), terms[2 * OWN :][part], 0.0)
                same = key_rows[2] == own_lanes(2, part, 7)
                probs[pair, odd * OWN + number * BLOCK : odd * OWN + (number + 1) * BLOCK, :] = jnp.where(same, bias, MASKED)
        return carry

    quarters = [slice(k * BLOCK, (k + 1) * BLOCK) for k in range(4)]
    loaded(5)
    gain1, shift1 = ln1_gain[...].reshape(1, WIDTH), ln1_shift[...].reshape(1, WIDTH)
    shared = []

    def first_norm(part):
        normed, _ = normalize(x_all[part, :].astype(F32))
        xn1[part, :] = (normed * gain1 + shift1).astype(BF16)
        keys[part, :] = dot(xn1[part, :], w_qkv[:, WIDTH : 2 * WIDTH]).astype(BF16)
        values[part, :] = (dot(xn1[part, :], w_qkv[:, 2 * WIDTH :]) + v_bias[...].reshape(1, WIDTH)).astype(BF16)
        for held in (keys, values):
            shared.append(exchange(held.at[part, :], held.at[pl.ds(OWN + part.start, BLOCK), :], SIBLING))

    first_norm(quarters[0])
    lax.fori_loop(0, PAIRS - 1, bias_pair, 0)

    loaded(8)
    gain2, shift2 = ln2_gain[...].reshape(1, WIDTH), ln2_shift[...].reshape(1, WIDTH)
    x_copy.wait()
    g_copy = exchange(cot_in.at[other], g_all.at[pl.ds(BLOCK, BLOCK), :], ALONG_Y)
    first_norm(quarters[1])
    xn1_copy = exchange(xn1.at[pl.ds(0, OWN), :], xn1.at[pl.ds(OWN, OWN), :], SIBLING)
    joined = (dot(xn1[0:OWN, :], w_qkv[:, 0:WIDTH]) + q_bias[...].reshape(1, WIDTH)).astype(BF16)
    query[...] = joined * jnp.asarray(HEAD_DIM**-0.5, BF16)
    bias_pair(PAIRS - 1, 0)
    for copy in shared:
        copy.wait()

    def split_heads(two):
        none = jnp.zeros_like(two)
        return jnp.concatenate((jnp.where(low_lane, two, none), jnp.where(low_lane, none, two)), axis=0)

    def join_heads(stacked):
        return jnp.where(low_lane, stacked[0:OWN], stacked[OWN:])

    for pair in range(PAIRS):
        here = slice(pair * 128, pair * 128 + 128)
        q_two, low = split_heads(query[:, here]), (low_a, low_b)[pair % 2]
        for part in quarters:
            masked = dot_cols(q_two[part], keys[:, here]) + probs[pair, part, :]
            terms = jnp.exp(masked - jnp.max(masked, axis=-1, keepdims=True))
            weights = terms * (1.0 / jnp.sum(terms, axis=-1, keepdims=True))
            probs[pair, part, :] = weights
            low[part, :] = weights.astype(BF16)
        att[0:OWN, here] = join_heads(dot(low[...], values[:, here])).astype(BF16)

    att_copy = exchange(att.at[pl.ds(0, OWN), :], att.at[pl.ds(OWN, OWN), :], SIBLING)
    g_copy.wait()
    gs_copy = exchange(g_all.at[pl.ds(0, OWN), :], g_all.at[pl.ds(OWN, OWN), :], SIBLING)
    middle, total, back = wide_f.at[0], wide_f.at[1], wide_f.at[2]
    total[...] = dot(att[0:OWN, :], w_out[...])

    def second_norm(part):
        here = x_all[part, :].astype(F32) + (total[part, :] + out_bias[...].reshape(1, WIDTH))
        middle[part, :] = here
        normed, _ = normalize(here)
        xn2[part, :] = (normed * gain2 + shift2).astype(BF16)

    for part in quarters[0:2]:
        second_norm(part)
    xn2_copy = exchange(xn2.at[pl.ds(0, OWN), :], xn2.at[pl.ds(OWN, OWN), :], SIBLING)
    loaded(2)

    def feed(first, act_to, gh_to):
        for third in range(3):
            here = lanes(first + third * 256, 256)
            there = slice(third * 256, (third + 1) * 256)
            value = dot(xn2[0:OWN, :], w_up[:, here]) + up_bias[here].reshape(1, 256)
            grad = dot_cols(g_all[0:OWN, :], w_down[rows(first + third * 256, 256), :])
            below = 0.5 * (1.0 + lax.erf(value * math.sqrt(0.5)))
            slope = below + value * (jnp.exp(-0.5 * value * value) * (1.0 / math.sqrt(2.0 * math.pi)))
            act_to[:, there] = (value * below).astype(BF16)
            grad_hidden = (grad * slope).astype(BF16)
            gh_to[:, there] = grad_hidden
            small[pl.ds(8 + lax.div(first, WIDTH), 1), there] = jnp.sum(grad_hidden.astype(F32), axis=0, keepdims=True)

    def gather(number, first, act_from, gh_from):
        forward = dot(act_from[...], w_down[rows(first, WIDTH), :])
        backward = dot_cols(gh_from[...], w_up[:, lanes(first, WIDTH)])
        if number:
            total[...] += forward
            back[...] += backward
        else:
            total[...] = forward
            back[...] = backward

    def contract(index, first, left, right, width):
        def body(i, carry):
            here = lanes(i * 256, 256)
            mine[index, rows(i * 256, 256), first : first + width] = dot_rows(left[:, here], right[...]).astype(BF16)
            return carry

        lax.fori_loop(0, SIDE // 256, body, 0)

    tasks = {
        name: chunk_task(
            [STEPS[step] for step in ROUTES[k]], outer, mine.at[k // 2, :, pl.ds(k % 2 * HALF, HALF)], inbox.at[k],
            sems.at[k], landing(k, side, o_up, o_down, o_qkv, o_out),
        )
        for k, name in enumerate(NAMES)
    }
    tasks["s"] = small_task(inner + outer, small, small_in, small_sems)
    plan = iter(PLAN)

    def pump():
        for names in next(plan):
            for name in names:
                next(tasks[name], None)

    def feed_half(half):
        given = (1 - side) * (2 * WIDTH) + half * WIDTH
        kept = side * (2 * WIDTH) + half * WIDTH
        own_act, own_gh = act.at[half, pl.ds(0, OWN), :], gh.at[half, pl.ds(0, OWN), :]
        feed(given, act_give.at[half], gh_give.at[half])
        act_copy = exchange(act_give.at[half], act.at[half, pl.ds(OWN, OWN), :], SIBLING)
        gh_copy = exchange(gh_give.at[half], gh.at[half, pl.ds(OWN, OWN), :], SIBLING)
        if half:
            pump()
        feed(kept, own_act, own_gh)
        if half:
            pump()
        else:
            gs_copy.wait()
            xn2_copy.wait()
        act_copy.wait()
        contract(2 * half, 0, act.at[half], g_all, WIDTH)
        pump()
        gh_copy.wait()
        contract(2 * half + 1, 0, xn2, gh.at[half], WIDTH)
        pump()
        gather(2 * half, given, act_give.at[half], gh_give.at[half])
        gather(2 * half + 1, kept, own_act, own_gh)

    feed_half(0)
    feed_half(1)

    def second_back(part):
        normed, inv_std = normalize(middle[part, :])
        total[part, :] = middle[part, :] + (total[part, :] + down_bias[...].reshape(1, WIDTH))
        grad = back[part, :]
        grad_out = g_all[part, :].astype(F32)
        grad_middle = grad_out + norm_back(grad, normed, inv_std, gain2)
        middle[part, :] = grad_middle
        low = grad_middle.astype(BF16)
        gb[part, :] = low
        return grad * normed, grad, grad_out, low.astype(F32)

    def sum_up(slots, work):
        for number, part in enumerate(quarters[0:2]):
            for slot, value in zip(slots, work(part)):
                value = jnp.sum(value, axis=0, keepdims=True)
                small[slot : slot + 1, :] = small[slot : slot + 1, :] + value if number else value

    sum_up((5, 6, 7, 4), second_back)
    out_give[...] = total[BLOCK:OWN, :].astype(BF16)
    out_copy = exchange(out_give, out_far, ALONG_Y)
    own_out = pltpu.make_async_copy(total.at[pl.ds(0, BLOCK), :], o_output.at[row], load_sems.at[19])
    own_out.start()
    gb_all[0:OWN, :] = gb[:, lanes(side * 384, 384)]
    gb_copy = exchange(gb.at[:, lanes((1 - side) * 384, 384)], gb_all.at[pl.ds(OWN, OWN), :], SIBLING)
    gatt[...] = dot_cols(gb[...], w_out[...]).astype(BF16)
    pump()

    def attend_back(pair):
        here = slice(pair * 128, pair * 128 + 128)
        q_two, grad_two = split_heads(query[:, here]), split_heads(gatt[:, here])
        for number, part in enumerate(quarters):
            weights = probs[pair, part, :]
            grad_probs = dot_cols(grad_two[part], values[:, here])
            inner_sum = jnp.sum(weights * grad_probs, axis=-1, keepdims=True)
            grad_scores = weights * (grad_probs - inner_sum)
            low_a[part, :] = weights.astype(BF16)
            low_b[part, :] = grad_scores.astype(BF16)
            for kind, key_rest, low in ((0, rest_x, low_c), (1, rest_y, low_d)):
                less = key_rest < own_lanes(kind, quarters[number % 2], BIN_PX - 1)
                low[part, :] = jnp.where(less, grad_scores, 0.0).astype(BF16)
        grad_scores = low_b[...]
        grad_query = join_heads(dot(grad_scores, keys[:, here])) * HEAD_DIM**-0.5
        gj[:, here] = grad_query.astype(BF16)
        grad_key = dot(q_two.T, grad_scores).T
        grad_value = dot(grad_two.T, low_a[...]).T
        total_k, total_v = key_f.at[0], key_f.at[1]
        give_k, give_v = wide_f.at[3], wide_f.at[4]
        total_k[:, here], give_k[:, here] = grad_key[0:OWN], grad_key[OWN:]
        total_v[:, here], give_v[:, here] = grad_value[0:OWN], grad_value[OWN:]
        shared.append(exchange(give_k.at[:, here], key_f.at[2, :, here], SIBLING))
        shared.append(exchange(give_v.at[:, here], key_f.at[3, :, here], SIBLING))

        every = dot(grad_scores, one_key[...])
        both = lax.broadcasted_iota(jnp.int32, (FULL, 128), 1) < BUCKETS
        less = jnp.where(both, dot(low_c[...], one_key[...]), dot(low_d[...], one_key[...]))
        by_key = every - less + pltpu.roll(less, 127, 1)
        upper = by_key.astype(BF16)
        lower = (by_key - upper.astype(F32)).astype(BF16)
        left_half = lax.broadcasted_iota(jnp.int32, (BUCKETS, 128), 1) < BUCKETS
        spot = lax.broadcasted_iota(jnp.int32, (1, 128), 1)
        for odd in range(2):
            mine_part = slice(odd * OWN, (odd + 1) * OWN)
            table = dot(one_query[...], upper[mine_part]) + dot(one_query[...], lower[mine_part])
            found = []
            for part in (table[0:BUCKETS], pltpu.roll(table[BUCKETS:], BUCKETS, 1)):
                skewed = pltpu.roll(jnp.where(left_half, part, 0.0), 0, 1, stride=1, stride_axis=0)
                line_sum = jnp.sum(skewed, axis=0, keepdims=True)
                below = jnp.sum(jnp.where(spot <= 32, line_sum, 0.0), axis=-1, keepdims=True)
                above = jnp.sum(jnp.where(spot >= 95, line_sum, 0.0), axis=-1, keepdims=True)
                inside = pltpu.roll(line_sum, 96, 1)
                found.append(jnp.where(spot == 0, below, jnp.where(spot == BUCKETS - 1, above, inside)))
            merged = jnp.where(spot < BUCKETS, found[0], pltpu.roll(found[1], BUCKETS, 1))
            line, spot_in = table_spot(2 * pair + odd)
            small[line : line + 1, spot_in : spot_in + 128] = merged

    shared = []
    for pair in range(PAIRS):
        attend_back(pair)
        if pair == 0:
            att_copy.wait()
            gb_copy.wait()
            contract(5, HALF, att, gb_all, HALF)
        pump()
    xn1_copy.wait()
    for copy in shared:
        copy.wait()

    def join_kv(part):
        low_k = (key_f[0, part, :] + key_f[2, part, :]).astype(BF16)
        low_v = (key_f[1, part, :] + key_f[3, part, :]).astype(BF16)
        gj[part, WIDTH : 2 * WIDTH] = low_k
        gj[part, 2 * WIDTH :] = low_v
        return gj[part, 0:WIDTH].astype(F32), low_v.astype(F32)

    sum_up((2, 3), join_kv)
    gj_copy = exchange(gj.at[:, lanes((1 - side) * 1152, 1152)], gj_all.at[pl.ds(OWN, OWN), :], SIBLING)
    gj_all[0:OWN, :] = gj[:, lanes(side * 1152, 1152)]
    back[...] = (
        dot_cols(gj[:, 0:WIDTH], w_qkv[:, 0:WIDTH])
        + dot_cols(gj[:, WIDTH : 2 * WIDTH], w_qkv[:, WIDTH : 2 * WIDTH])
        + dot_cols(gj[:, 2 * WIDTH :], w_qkv[:, 2 * WIDTH :])
    )
    gj_copy.wait()
    pump()
    contract(4, 0, xn1, gj_all.at[:, pl.ds(0, WIDTH)], WIDTH)
    pump()
    contract(5, 0, xn1, gj_all.at[:, pl.ds(WIDTH, HALF)], HALF)
    pump()

    def first_back(part):
        normed, inv_std = normalize(x_all[part, :].astype(F32))
        grad = back[part, :]
        middle[part, :] = middle[part, :] + norm_back(grad, normed, inv_std, gain1)
        return grad * normed, grad

    sum_up((0, 1), first_back)
    in_give[...] = middle[BLOCK:OWN, :].astype(BF16)
    in_copy = exchange(in_give, in_far, ALONG_Y)
    own_in = pltpu.make_async_copy(middle.at[pl.ds(0, BLOCK), :], o_inputs.at[row], load_sems.at[20])
    own_in.start()

    pump()
    for copy in (out_copy, own_out, in_copy, own_in):
        copy.wait()
    total[0:BLOCK, :] = out_far[...].astype(F32)
    middle[0:BLOCK, :] = in_far[...].astype(F32)
    last = (
        pltpu.make_async_copy(total.at[pl.ds(0, BLOCK), :], o_output.at[other], load_sems.at[19]),
        pltpu.make_async_copy(middle.at[pl.ds(0, BLOCK), :], o_inputs.at[other], load_sems.at[20]),
        pltpu.make_async_copy(small, o_small, load_sems.at[21]),
    )
    for copy in last[:2]:
        copy.start()
    pump()
    last[2].start()
    pump()
    for copy in last:
        copy.wait()


def per_device(
    inputs, ln1_gain, ln1_shift, w_qkv, q_bias, v_bias, w_out, out_bias, table_x, table_y, ln2_gain, ln2_shift,
    w_up, up_bias, w_down, down_bias, cotangent, page_ids, corners,
):
    outer = outer_steps(lax.axis_size("wide"))
    slots = 11 + len(outer)
    assert inputs.shape == (2, BLOCK, WIDTH) and lax.axis_size("blk") == 4 and lax.axis_size("wide") >= 8
    hbm = pl.BlockSpec(memory_space=pl.ANY)
    shape = jax.ShapeDtypeStruct
    args = (
        inputs, ln1_gain, ln1_shift, w_qkv, q_bias, v_bias, w_out, out_bias, table_x.T, table_y.T, ln2_gain, ln2_shift,
        w_up, up_bias, w_down, down_bias, cotangent, page_ids, corners,
    )
    output, grad_inputs, full_up, full_down, full_qkv, full_out, small = pl.pallas_call(
        functools.partial(layer_kernel, outer),
        out_shape=(
            shape(inputs.shape, F32), shape(inputs.shape, F32),
            shape(w_up.shape, BF16), shape(w_down.shape, BF16), shape(w_qkv.shape, BF16), shape(w_out.shape, BF16),
            shape((SMALL_ROWS, WIDTH), F32),
        ),
        in_specs=[hbm] * len(args),
        out_specs=(hbm,) * 7,
        scratch_shapes=[pltpu.VMEM((WIDTH,), F32)] * 8
        + [
            pltpu.VMEM((FF,), F32), pltpu.VMEM((HEADS, BUCKETS), F32), pltpu.VMEM((HEADS, BUCKETS), F32),
            pltpu.VMEM(page_ids.shape, jnp.int32), pltpu.VMEM(corners.shape, jnp.int32), pltpu.VMEM((SMALL_ROWS, WIDTH), F32),
            pltpu.VMEM(w_qkv.shape, BF16), pltpu.VMEM(w_out.shape, BF16),
            pltpu.VMEM(w_up.shape, BF16), pltpu.VMEM(w_down.shape, BF16),
            pltpu.VMEM((SQUARES, SIDE, SIDE), BF16),
            pltpu.VMEM((CHUNKS, SIDE - PIECE + PIECE * len(outer), HALF), BF16),
            pltpu.VMEM((5 + len(outer), SMALL_ROWS, WIDTH), F32),
            pltpu.VMEM((PAIRS, FULL, FULL), F32),
            pltpu.VMEM((FULL, FULL), BF16), pltpu.VMEM((FULL, FULL), BF16),
            pltpu.VMEM((FULL, FULL), BF16), pltpu.VMEM((FULL, FULL), BF16),
            pltpu.VMEM((5, OWN, WIDTH), F32), pltpu.VMEM((4, OWN, WIDTH), F32),
            pltpu.VMEM((OWN, WIDTH), BF16), pltpu.VMEM((FULL, WIDTH), BF16),
            pltpu.VMEM((FULL, WIDTH), BF16), pltpu.VMEM((FULL, WIDTH), BF16), pltpu.VMEM((FULL, WIDTH), BF16),
            pltpu.VMEM((OWN, WIDTH), BF16), pltpu.VMEM((FULL, WIDTH), BF16), pltpu.VMEM((FULL, WIDTH), BF16),
            pltpu.VMEM((2, FULL, WIDTH), BF16), pltpu.VMEM((2, FULL, WIDTH), BF16),
            pltpu.VMEM((2, OWN, WIDTH), BF16), pltpu.VMEM((2, OWN, WIDTH), BF16),
            pltpu.VMEM((OWN, WIDTH), BF16), pltpu.VMEM((FULL, 384), BF16), pltpu.VMEM((OWN, WIDTH), BF16),
            pltpu.VMEM((OWN, 3 * WIDTH), BF16), pltpu.VMEM((FULL, 1152), BF16),
            pltpu.VMEM((3, FULL, 128), jnp.int32), pltpu.VMEM((FULL, 256), BF16),
            pltpu.VMEM((FULL, 128), BF16), pltpu.VMEM((128, OWN), BF16), pltpu.VMEM((9, 16, 128), F32),
            pltpu.VMEM((BLOCK, WIDTH), BF16), pltpu.VMEM((BLOCK, WIDTH), BF16),
            pltpu.VMEM((BLOCK, WIDTH), BF16), pltpu.VMEM((BLOCK, WIDTH), BF16),
            pltpu.SemaphoreType.DMA((22,)),
            pltpu.SemaphoreType.DMA((32, 2)),
            pltpu.SemaphoreType.DMA((CHUNKS, slots, 2)),
            pltpu.SemaphoreType.DMA((5 + len(outer), 2)),
        ],
        compiler_params=pltpu.CompilerParams(
            collective_id=0, has_side_effects=True, vmem_limit_bytes=63 * MIB
        ),
        cost_estimate=pl.CostEstimate(flops=13 * 10**9, bytes_accessed=3 * 10**7, transcendentals=10**7),
    )(*args)
    ended = finish(full_up, full_down, full_qkv, full_out, output, grad_inputs, small)
    f_up, f_down, f_qkv, f_out, output, grad_inputs, grad_x, grad_y, f_upb = ended[:9]
    f_ln1g, f_ln1s, f_qb, f_vb, f_outb, f_ln2g, f_ln2s, f_downb = ended[9:]
    return (
        output, grad_inputs, f_ln1g, f_ln1s, f_qkv, f_qb, f_vb, f_out, f_outb, grad_x.T, grad_y.T, f_ln2g, f_ln2s,
        f_up, f_upb, f_down, f_downb,
    )


def table_spot(head):
    return 12 + head * 128 // WIDTH, head * 128 % WIDTH


def finish_kernel(*refs):
    sources, passed, small_from = refs[:4], refs[4:6], refs[6]
    targets, kept, little = refs[7:11], refs[11:13], refs[13:24]
    rings_in, rings_out, outs = refs[24:27], refs[27:30], refs[30:41]
    held, small, sems_in, sems_out, sems_kept = refs[41:]
    small_copy = pltpu.make_async_copy(small_from, small, sems_kept.at[4])
    arrive = [pltpu.make_async_copy(passed[k], held.at[k], sems_kept.at[k]) for k in range(2)]
    leave = [pltpu.make_async_copy(held.at[k], kept[k], sems_kept.at[2 + k]) for k in range(2)]
    leave += [pltpu.make_async_copy(outs[k], little[k], sems_kept.at[5 + k]) for k in range(len(outs))]
    ring_of = (0, 1, 2, 1)
    pieces = []
    for k, source in enumerate(sources):
        tall = SLAB // source.shape[1]
        pieces += [(k, ring_of[k], pl.ds(first, tall)) for first in range(0, source.shape[0], tall)]

    def fetch(n):
        k, ring, part = pieces[n]
        return pltpu.make_async_copy(sources[k].at[part, :], rings_in[ring].at[n % SLOTS], sems_in.at[n])

    def store(n):
        k, ring, part = pieces[n]
        return pltpu.make_async_copy(rings_out[ring].at[n % SLOTS], targets[k].at[part, :], sems_out.at[n])

    small_copy.start()
    for n in range(SLOTS):
        fetch(n).start()
    for copy in arrive:
        copy.start()
    small_copy.wait()
    for head in range(HEADS):
        line, first = table_spot(head)
        for kind in range(2):
            start = first + kind * BUCKETS
            outs[kind][head : head + 1, :] = small[line : line + 1, start : start + BUCKETS]
    for part in range(FF // WIDTH):
        outs[2][part * WIDTH : (part + 1) * WIDTH] = small[8 + part, :]
    for slot in range(8):
        outs[3 + slot][...] = small[slot, :]
    for copy in leave[2:]:
        copy.start()
    for n in range(len(pieces)):
        if n == SLOTS:
            for k in range(2):
                arrive[k].wait()
                leave[k].start()
        fetch(n).wait()
        if n >= SLOTS:
            store(n - SLOTS).wait()
        ring = pieces[n][1]
        rings_out[ring][n % SLOTS] = rings_in[ring][n % SLOTS].astype(F32)
        store(n).start()
        if n + SLOTS < len(pieces):
            fetch(n + SLOTS).start()
    for n in range(len(pieces) - SLOTS, len(pieces)):
        store(n).wait()
    for copy in leave:
        copy.wait()


def finish(*arrays):
    hbm = pl.BlockSpec(memory_space=pl.ANY)
    little = [(HEADS, BUCKETS)] * 2 + [(FF,)] + [(WIDTH,)] * 8
    widths = [array.shape[1] for array in arrays[:3]]
    count = sum(array.size for array in arrays[:4]) // SLAB
    return pl.pallas_call(
        finish_kernel,
        out_shape=[jax.ShapeDtypeStruct(array.shape, F32) for array in arrays[:6]]
        + [jax.ShapeDtypeStruct(shape, F32) for shape in little],
        in_specs=[hbm] * 7,
        out_specs=[hbm] * (6 + len(little)),
        scratch_shapes=[pltpu.VMEM((SLOTS, SLAB // width, width), kind) for kind in (BF16, F32) for width in widths]
        + [pltpu.VMEM(shape, F32) for shape in little]
        + [pltpu.VMEM((2,) + arrays[4].shape, F32), pltpu.VMEM((SMALL_ROWS, WIDTH), F32)]
        + [pltpu.SemaphoreType.DMA((size,)) for size in (count, count, 5 + len(little))],
        compiler_params=pltpu.CompilerParams(vmem_limit_bytes=60 * MIB),
        cost_estimate=pl.CostEstimate(flops=10**7, bytes_accessed=45 * 10**6, transcendentals=0),
    )(*arrays)


def solution(mesh):
    tokens, row_of_blk = P("wide", "blk", None), P("wide", None)
    return jax.shard_map(
        per_device,
        mesh=mesh,
        in_specs=(tokens,) + (P(),) * 15 + (tokens, row_of_blk, P(None, "wide", None)),
        out_specs=(tokens, tokens) + (P(),) * 15,
        check_vma=False,
    )
```
